32 devices in a mesh: dp: 32 (over z, y, x, core).
Axes of the slice: x: 2, y: 2, z: 4, core: 2. Of those that a mesh axis runs over, the one named last changes fastest.
Arguments:
- tokens: bfloat16 [16384, 1024], P('dp'), may hold values from -6 to 6
- query_weight: bfloat16 [1024, 1024], P('dp'), may hold values from -0.375 to 0.375
- key_projection_weight: bfloat16 [1024, 512], P('dp'), may hold values from -0.1875 to 0.1875
- value_projection_weight: bfloat16 [1024, 512], P('dp'), may hold values from -0.1875 to 0.1875
- output_weight: bfloat16 [1024, 1024], P(None, 'dp'), may hold values from -1.5 to 1.5
- first_gain: bfloat16 [1024], P('dp'), may hold values from 0.5 to 1.5
- second_gain: bfloat16 [1024], P('dp'), may hold values from 0.5 to 1.5
- router_weight: bfloat16 [1024, 16], P('dp'), may hold values from -0.09375 to 0.09375
- gate_weight: bfloat16 [16, 1024, 512], P(None, 'dp'), may hold values from -0.1875 to 0.1875
- up_weight: bfloat16 [16, 1024, 512], P(None, 'dp'), may hold values from -0.1875 to 0.1875
- down_weight: bfloat16 [16, 512, 1024], P(None, None, 'dp'), may hold values from -0.75 to 0.75
- routes: int32 [16384, 8], P('dp'), may hold values from 0 to 15, all different within a row; in each aligned block of 512 rows (0 to 511, 512 to 1023, ...) at most 288 rows name the same one
- segments: int32 [32, 512], P('dp'), may hold values from 0 to 7, never falling along the last dimension, each value on 1 to 256 neighbouring positions
- cotangent: bfloat16 [16384, 1024], P('dp'), may hold values from -6 to 6
Outputs:
- output: bfloat16 [16384, 1024], P('dp')
- input_grad: float32 [16384, 1024], P('dp')
- query_grad: float32 [1024, 1024], P('dp')
- key_grad: float32 [1024, 512], P('dp')
- value_grad: float32 [1024, 512], P('dp')
- output_weight_grad: float32 [1024, 1024], P(None, 'dp')
- first_gain_grad: float32 [1024], P('dp')
- second_gain_grad: float32 [1024], P('dp')
- router_grad: float32 [1024, 16], P('dp')
- gate_grad: float32 [16, 1024, 512], P(None, 'dp')
- up_grad: float32 [16, 1024, 512], P(None, 'dp')
- down_grad: float32 [16, 512, 1024], P(None, None, 'dp')
The draws below stay inside these ranges and needn't reach their ends.
Inputs may be any that keep to these rules, and one draw needn't show every extreme that they name: `routes`: each token names 8 different experts; the 512 tokens of one device name no expert more than 288 times, a bound that some block reaches. `segments`: along each sequence the document numbers never fall; each document has 1 to 256 tokens, one exactly 256.
All inputs are finite; a program needn't handle non-finite values.
Results may differ from the reference program's by a relative error of at most 0.013.
The reference program's roundings to bfloat16 on the way count: a program that leaves them out, or rounds other values in their place, can miss the bound.
Values may be sent and summed in bfloat16 or wider, within the bound.
No kernel may reach another device: no remote copies, remote signals or barrier semaphores. Data moves between devices by JAX's collectives and lax.ppermute only.
A program may use at most 320 MiB of HBM per device.

```python
import math
import jax
import jax.numpy as jnp
import numpy as np
from jax import lax

MODEL_WIDTH = 1024
QUERY_HEADS = 16
KEY_VALUE_HEADS = 8
HEAD_SIZE = 64
FF = 512
EXPERTS = 16
TOP = 8
SEQUENCE_TOKENS = 512
DEVICE_SEQUENCES = 1
DOCS = 8
MOST_DOC = 256
TOK_DEV = 512
CAP = 288
TOKENS = 16384
SEQS = 32
N_DP = 32


def strengthened(drawn, rng, source, target, blocks, factor):
    def block_of(position):
        return (jnp.arange(drawn.shape[position]) // (drawn.shape[position] // blocks)).reshape((-1,) + (1,) * (drawn.ndim - 1 - position))

    one_side = jax.random.permutation(rng, blocks)[block_of(target)]
    other_side = (block_of(target) + blocks // 2) % blocks
    return jnp.where((block_of(source) == one_side) | (block_of(source) == other_side), factor * drawn, drawn)


def block_scale(rng, shape, shards, low, high):
    factor_of, own = 1.0, jax.random.fold_in(rng, 6)
    for axis_at, blocks in shards:
        steps = jnp.exp(jax.random.uniform(jax.random.fold_in(own, axis_at), (blocks,), jnp.float32, low / len(shards), high / len(shards)))
        factor_of = factor_of * jnp.repeat(steps, shape[axis_at] // blocks).reshape([-1 if axis == axis_at else 1 for axis in range(len(shape))])
    return factor_of


def length_profile(number_of, total, limit, slope):
    weights = [(1 << 20) // math.isqrt(rank ** slope) + 1 for rank in range(2, number_of + 1)]
    rest, counts = total - limit - (number_of - 1), [1] * (number_of - 1)
    while rest > 0:
        free = [i for i in range(number_of - 1) if counts[i] < limit]
        mass, budget = sum([weights[i] for i in free]), rest
        for i in free:
            more = min(limit - counts[i], max(1, budget * weights[i] // mass), rest)
            counts[i] = counts[i] + more
            rest = rest - more
    return np.array([limit] + counts)


def ragged_sizes(stream_key, count, total, most, skew):
    if count == 2:
        one = jax.random.randint(stream_key, (), max(1, total - most), min(most, total - 1) + 1)
        return jnp.stack([one, total - one])
    lengths = jnp.asarray(length_profile(count, total, most, skew), jnp.int32)
    pairs = (count - 1) // 2
    donor, receiver = lengths[1:1 + 2 * pairs:2], lengths[2:2 + 2 * pairs:2]
    margin = jnp.minimum(donor - 1, most - receiver)
    passed = jax.random.randint(jax.random.fold_in(stream_key, 1), (pairs,), 0, 1 << 20) % (margin + 1)
    lengths = lengths.at[1:1 + 2 * pairs:2].set(donor - passed).at[2:2 + 2 * pairs:2].set(receiver + passed)
    return lengths[jax.random.permutation(jax.random.fold_in(stream_key, 2), count)]


def assign_block(key, own, number, rows, amount, top, bound, lean):
    order = jax.random.permutation(key, amount)
    crowded, common = load_shares(amount, rows * top, bound, lean, True), load_shares(amount, rows * top, bound, lean, False)
    places = jnp.arange(amount)

    def named(lengths, rotation):
        used = int((lengths > 0).sum())
        fixed = max(1, used // 4)
        moved = fixed + (places - fixed + rotation * (used - fixed)) % max(1, amount - fixed)
        return jnp.zeros((amount,), jnp.int32).at[order[jnp.where(places < fixed, places, moved)]].set(jnp.asarray(lengths, jnp.int32))

    lengths = jnp.where(number % 4 == 0, named(crowded, number // 4), named(common, number - number // 4 - 1))
    mixed = jax.random.permutation(jax.random.fold_in(own, 3), amount)
    giver, taker = mixed[0:amount // 2 * 2:2], mixed[1:amount // 2 * 2:2]
    margin = jnp.minimum(lengths[giver] - 1, bound - lengths[taker]) // 2
    margin = jnp.where((giver == order[0]) | (taker == order[0]) | (lengths[taker] == 0), 0, jnp.maximum(margin, 0))
    moved = jax.random.randint(jax.random.fold_in(own, 4), (amount // 2,), 0, 1 << 20) % (margin + 1)
    lengths = lengths.at[giver].add(-moved).at[taker].add(moved)
    labels = jnp.searchsorted(jnp.cumsum(lengths), jnp.arange(rows * top), side="right").astype(jnp.int32)
    table = labels.reshape(top, rows).T
    table = table[jax.random.permutation(jax.random.fold_in(own, 1), rows)]
    rotation = jax.random.randint(jax.random.fold_in(own, 2), (rows, 1), 0, top)
    return jnp.take_along_axis(table, (jnp.arange(top)[None, :] + rotation) % top, axis=1)


def load_shares(number_of, total, bound, skew, full):
    portions = [(1 << 20) // math.isqrt(rank ** skew) + 1 for rank in range(1, number_of + 1)]
    largest = bound if full else min(bound, max(-(-total // number_of), total * portions[0] // sum(portions)))
    least = 1 if total - largest >= number_of - 1 else 0
    given, rest = [largest] + [least] * (number_of - 1), total - largest - least * (number_of - 1)
    while rest > 0:
        movable = [i for i in range(1, number_of) if given[i] < largest] or [i for i in range(1, number_of) if given[i] < bound]
        pool, remaining = sum([portions[i] for i in movable]), rest
        for i in movable:
            extra = min(bound - given[i], max(1, remaining * portions[i] // pool), rest)
            given[i] = given[i] + extra
            rest = rest - extra
    return np.array(given)


def gaussian(own_key, extent, width, reach, shards=(), kind=jnp.bfloat16):
    drawn = width * jax.random.normal(own_key, extent, jnp.float32)
    if shards:
        drawn = drawn * block_scale(own_key, extent, shards, -0.22, 0.18)
    return jnp.clip(drawn, -reach, reach).astype(kind)


def bell_draw_with(rng, extent, spread, most, pieces, heavy, held_as=jnp.bfloat16):
    values = spread * jax.random.normal(rng, extent, jnp.float32)
    if pieces:
        values = values * block_scale(rng, extent, pieces, -0.22, 0.18)
    return jnp.clip(strengthened(values, jax.random.fold_in(rng, 3), *heavy), -most, most).astype(held_as)


def setup_inputs(seed: int = 0) -> dict:
    streams_of = jax.random.split(jax.random.key(seed), 15)
    tokens = bell_draw_with(streams_of[0], (TOKENS, MODEL_WIDTH), 1.0, 6.0, ((0, 32),), (0, 1, 32, 2.75))
    query_weight = gaussian(streams_of[1], (MODEL_WIDTH, QUERY_HEADS * HEAD_SIZE), (MODEL_WIDTH // 4) ** -0.5, 0.375, ((0, 32),))
    key_projection_weight = gaussian(streams_of[2], (MODEL_WIDTH, KEY_VALUE_HEADS * HEAD_SIZE), MODEL_WIDTH ** -0.5, 0.1875, ((0, 32),))
    value_projection_weight = gaussian(streams_of[3], (MODEL_WIDTH, KEY_VALUE_HEADS * HEAD_SIZE), MODEL_WIDTH ** -0.5, 0.1875, ((0, 32),))
    output_weight = gaussian(streams_of[4], (QUERY_HEADS * HEAD_SIZE, MODEL_WIDTH), (QUERY_HEADS * HEAD_SIZE // 64) ** -0.5, 1.5, ((1, 32),))
    first_gain = jnp.clip(1.0 + 0.1 * jax.random.normal(streams_of[5], (MODEL_WIDTH,), jnp.float32), 0.5, 1.5).astype(jnp.bfloat16)
    second_gain = jnp.clip(1.0 + 0.1 * jax.random.normal(streams_of[6], (MODEL_WIDTH,), jnp.float32), 0.5, 1.5).astype(jnp.bfloat16)
    router_weight = gaussian(streams_of[7], (MODEL_WIDTH, EXPERTS), (4 * MODEL_WIDTH) ** -0.5, 0.09375, ((0, 32),))
    gate_weight = gaussian(streams_of[8], (EXPERTS, MODEL_WIDTH, FF), MODEL_WIDTH ** -0.5, 0.1875, ((1, 32),))
    up_weight = gaussian(streams_of[9], (EXPERTS, MODEL_WIDTH, FF), MODEL_WIDTH ** -0.5, 0.1875, ((1, 32),))
    down_weight = gaussian(streams_of[10], (EXPERTS, FF, MODEL_WIDTH), (FF // 8) ** -0.5, 0.75, ((2, 32),))
    routes_keys = jax.random.split(jax.random.fold_in(streams_of[11], 1), TOKENS // TOK_DEV)
    routes_turns = jax.random.permutation(jax.random.fold_in(streams_of[11], 3), TOKENS // TOK_DEV)
    routes = jax.vmap(lambda own, number: assign_block(jax.random.fold_in(streams_of[11], 2), own, number, TOK_DEV, EXPERTS, TOP, CAP, 0))(routes_keys, routes_turns).reshape((TOKENS, TOP))
    segments = jax.vmap(lambda own: jnp.searchsorted(jnp.cumsum(ragged_sizes(own, DOCS, SEQUENCE_TOKENS, MOST_DOC, 1)), jnp.arange(SEQUENCE_TOKENS), side="right"))(jax.random.split(streams_of[12], SEQS)).reshape((SEQS, SEQUENCE_TOKENS)).astype(jnp.int32)
    cotangent = bell_draw_with(streams_of[13], (TOKENS, MODEL_WIDTH), 1.0, 6.0, ((0, 32),), (0, 1, 32, 2.75))
    return {"tokens": tokens, "query_weight": query_weight, "key_projection_weight": key_projection_weight, "value_projection_weight": value_projection_weight, "output_weight": output_weight, "first_gain": first_gain, "second_gain": second_gain, "router_weight": router_weight, "gate_weight": gate_weight, "up_weight": up_weight, "down_weight": down_weight, "routes": routes, "segments": segments, "cotangent": cotangent}


epsilon = 1e-06
neg_large = -1000000000.0

@jax.custom_vjp
def low(v):
    return lax.optimization_barrier(v.astype(jnp.bfloat16)).astype(jnp.float32)

@jax.custom_vjp
def low_back(v):
    return v

def low_keep(v):
    return (low(v), None)

def low_pass(kept, grad):
    return (grad,)

def back_keep(v):
    return (v, None)

def back_low(kept, grad):
    return (low(grad),)
low.defvjp(low_keep, low_pass)
low_back.defvjp(back_keep, back_low)

def matrix_product(left, right):
    return jnp.dot(left, right, precision=lax.Precision.HIGHEST, preferred_element_type=jnp.float32)

def rms_scale(values):
    return lax.rsqrt(lax.optimization_barrier(jnp.mean(values * values, axis=-1, keepdims=True)) + epsilon)

def rope_tables(sequence_length, head_dim, copies):
    positions = jnp.arange(sequence_length, dtype=jnp.float32)
    frequency = 10000.0 ** (-2.0 * jnp.arange(head_dim // 2, dtype=jnp.float32) / head_dim)
    angles = jnp.tile(positions[:, None] * frequency[None, :], (copies, 1))
    return (jnp.cos(angles), jnp.sin(angles))

def rotate(values, cosine_lookup, sine_lookup):
    half_dim = values.shape[-1] // 2
    first_half = values[..., :half_dim]
    second_half = values[..., half_dim:]
    cos_part = cosine_lookup[:, None, :]
    sin_part = sine_lookup[:, None, :]
    return jnp.concatenate([first_half * cos_part - second_half * sin_part, second_half * cos_part + first_half * sin_part], axis=-1)

def slot_tables(routes, experts, capacity):
    number_of_rows, picks = routes.shape
    flat_routes = routes.reshape(-1)
    one_hot = (flat_routes[:, None] == jnp.arange(experts, dtype=jnp.int32)[None, :]).astype(jnp.int32)
    slot_rank = lax.optimization_barrier(jnp.sum((jnp.cumsum(one_hot, axis=0) - 1) * one_hot, axis=1))
    slot_index = (flat_routes * capacity + slot_rank).astype(jnp.int32)
    owners = jnp.zeros((experts * capacity,), jnp.int32).at[slot_index].set(jnp.arange(number_of_rows * picks, dtype=jnp.int32) // picks)
    filled = jnp.zeros((experts * capacity,), jnp.int32).at[slot_index].set(1)
    return (slot_index.reshape(number_of_rows, picks), owners, filled)

def attend_packed_sequence(packed):
    query_sequence, key_seq, value_seq, seg_seq = packed
    sequence_length = seg_seq.shape[0]
    rows_per_block = min(512, sequence_length)
    number_of_blocks = sequence_length // rows_per_block
    score_scale = 1.0 / math.sqrt(HEAD_SIZE)
    positions = jnp.arange(sequence_length, dtype=jnp.int32)
    grouped_queries = query_sequence.reshape(number_of_blocks, rows_per_block, KEY_VALUE_HEADS, QUERY_HEADS // KEY_VALUE_HEADS, HEAD_SIZE)

    def one_block(piece):
        query_blk, seg_blk, place_blk = piece
        raw_scores = jnp.einsum('qgrd,kgd->grqk', query_blk, key_seq, precision=lax.Precision.HIGHEST)
        scores = low_back(raw_scores * score_scale)
        allowed = (seg_blk[:, None] == seg_seq[None, :]) & (place_blk[:, None] >= positions[None, :])
        scores = jnp.where(allowed[None, None], scores, neg_large)
        prob_low = low(jax.nn.softmax(scores, axis=-1))
        return jnp.einsum('grqk,kgd->qgrd', prob_low, value_seq, precision=lax.Precision.HIGHEST)
    mixed_heads = lax.map(jax.checkpoint(one_block), (grouped_queries, seg_seq.reshape(number_of_blocks, rows_per_block), positions.reshape(number_of_blocks, rows_per_block)))
    return mixed_heads.reshape(sequence_length, QUERY_HEADS * HEAD_SIZE)

def forward(inputs, query_w, key_matrix, value_w, out_w, gain_one, gain_two, router_w, gate_w, up_w, down_w, routes, tables, segment_rows, cosine_lookup, sine_lookup):
    slot_index, owners, filled = tables
    number_of_rows = inputs.shape[0]
    first_normed_input = low(inputs * rms_scale(inputs) * gain_one)
    queries = matrix_product(first_normed_input, query_w).reshape(number_of_rows, QUERY_HEADS, HEAD_SIZE)
    key_unrotated = matrix_product(first_normed_input, key_matrix).reshape(number_of_rows, KEY_VALUE_HEADS, HEAD_SIZE)
    value_raw = matrix_product(first_normed_input, value_w)
    query_rotated = low(rotate(low_back(queries), cosine_lookup, sine_lookup))
    key_rotated = low(rotate(low_back(key_unrotated), cosine_lookup, sine_lookup))
    value_reduced_precision = low(low_back(value_raw))
    mixed_heads = lax.map(attend_packed_sequence, (query_rotated.reshape(DEVICE_SEQUENCES, SEQUENCE_TOKENS, QUERY_HEADS, HEAD_SIZE), key_rotated.reshape(DEVICE_SEQUENCES, SEQUENCE_TOKENS, KEY_VALUE_HEADS, HEAD_SIZE), value_reduced_precision.reshape(DEVICE_SEQUENCES, SEQUENCE_TOKENS, KEY_VALUE_HEADS, HEAD_SIZE), segment_rows))
    attn_low = low(low_back(mixed_heads.reshape(number_of_rows, QUERY_HEADS * HEAD_SIZE)))
    resid = inputs + low_back(matrix_product(attn_low, out_w))
    normed_two = low(resid * rms_scale(resid) * gain_two)
    logits = low_back(matrix_product(normed_two, router_w))
    gates = jax.nn.softmax(jnp.take_along_axis(logits, routes, axis=1), axis=-1)
    gathered = jnp.where(filled[:, None] > 0, normed_two[owners], 0.0).reshape(EXPERTS, CAP, MODEL_WIDTH)
    gate_act = low_back(jnp.einsum('ecd,edf->ecf', gathered, gate_w, precision=lax.Precision.HIGHEST))
    up_act = low_back(jnp.einsum('ecd,edf->ecf', gathered, up_w, precision=lax.Precision.HIGHEST))
    hidden = low(jax.nn.silu(gate_act) * up_act)
    expert_out = low_back(jnp.einsum('ecf,efd->ecd', hidden, down_w, precision=lax.Precision.HIGHEST)).reshape(EXPERTS * CAP, MODEL_WIDTH)
    picked = expert_out[slot_index]
    return resid + lax.optimization_barrier(jnp.sum(gates[:, :, None] * picked, axis=1))

def reference(tokens, query_weight, key_projection_weight, value_projection_weight, output_weight, first_gain, second_gain, router_weight, gate_weight, up_weight, down_weight, routes, segments, cotangent):
    params = tuple((item.astype(jnp.float32) for item in (query_weight, key_projection_weight, value_projection_weight, output_weight, first_gain, second_gain, router_weight, gate_weight, up_weight, down_weight)))
    cosine_lookup, sine_lookup = rope_tables(SEQUENCE_TOKENS, HEAD_SIZE, DEVICE_SEQUENCES)
    token_blocks = tokens.astype(jnp.float32).reshape(N_DP, TOK_DEV, MODEL_WIDTH)
    route_blocks = routes.reshape(N_DP, TOK_DEV, TOP)
    seg_blocks = segments.reshape(N_DP, DEVICE_SEQUENCES, SEQUENCE_TOKENS)
    grad_blocks = cotangent.astype(jnp.float32).reshape(N_DP, TOK_DEV, MODEL_WIDTH)

    def step(totals, piece):
        token_blk, route_blk, seg_blk, grad_blk = piece
        tables = slot_tables(route_blk, EXPERTS, CAP)

        def local_forward(inputs, *weights):
            return forward(inputs, *weights, route_blk, tables, seg_blk, cosine_lookup, sine_lookup)
        result, pullback = jax.vjp(local_forward, token_blk, *params)
        grads = pullback(grad_blk)
        totals = tuple((total + grad for total, grad in zip(totals, grads[1:])))
        return (totals, (result.astype(jnp.bfloat16), grads[0]))
    zeros_init = tuple((jnp.zeros_like(item) for item in params))
    totals, (results, input_grads) = lax.scan(step, zeros_init, (token_blocks, route_blocks, seg_blocks, grad_blocks))
    output = results.reshape(TOKENS, MODEL_WIDTH)
    input_grad = input_grads.reshape(TOKENS, MODEL_WIDTH)
    return (output, input_grad, totals[0], totals[1], totals[2], totals[3], totals[4], totals[5], totals[6], totals[7], totals[8], totals[9])
```

```python
import math

import jax
import jax.numpy as jnp
from jax import lax
from jax.sharding import PartitionSpec as P

QUERY_HEADS = 16
KEY_VALUE_HEADS = 8
HEAD_SIZE = 64
EXPERTS = 16
PLANE = 8
MINE = EXPERTS // PLANE

epsilon = 1e-06
neg_large = -1000000000.0
BF = jnp.bfloat16
F32 = jnp.float32


def dot(a, b, ca, cb):
    return lax.dot_general(a, b, (((ca,), (cb,)), ((), ())), preferred_element_type=F32)


def rms_scale(values):
    return lax.rsqrt(jnp.mean(values * values, axis=-1, keepdims=True) + epsilon)


def norm_back(values, scale_rows, gain_full, grad_out):
    weighted = grad_out * gain_full
    gain_grad = jnp.sum(grad_out * values * scale_rows, axis=0)
    inner_mean = jnp.mean(weighted * values, axis=-1, keepdims=True)
    grad_in = scale_rows * weighted - values * (scale_rows * scale_rows * scale_rows) * inner_mean
    return (grad_in, gain_grad)


def rope_tables(sequence_length, head_dim, copies):
    positions = jnp.arange(sequence_length, dtype=jnp.float32)
    frequency = 10000.0 ** (-2.0 * jnp.arange(head_dim // 2, dtype=jnp.float32) / head_dim)
    angles = jnp.tile(positions[:, None] * frequency[None, :], (copies, 1))
    return (jnp.cos(angles), jnp.sin(angles))


def rotate(values, cosine_lookup, sine_lookup):
    half_dim = values.shape[-1] // 2
    first_half = values[..., :half_dim]
    second_half = values[..., half_dim:]
    cos_part = cosine_lookup[:, None, :]
    sin_part = sine_lookup[:, None, :]
    return jnp.concatenate(
        [
            first_half * cos_part - second_half * sin_part,
            second_half * cos_part + first_half * sin_part,
        ],
        axis=-1,
    )


def attention_forward(query, key, value, allowed, score_scale):
    raw_scores = jnp.einsum("qgrd,kgd->grqk", query, key, preferred_element_type=F32)
    scores = jnp.where(allowed, raw_scores * score_scale, neg_large)
    largest = jnp.max(scores, axis=-1, keepdims=True)
    exponent = jnp.exp(scores - largest)
    totals = jnp.sum(exponent, axis=-1, keepdims=True)
    prob_low = (exponent / totals).astype(BF)
    mixed = jnp.einsum("grqk,kgd->qgrd", prob_low, value, preferred_element_type=F32)
    return mixed, largest + jnp.log(totals)


def attention_backward(query, key, value, allowed, log_total, grad, score_scale):
    raw_scores = jnp.einsum("qgrd,kgd->grqk", query, key, preferred_element_type=F32)
    scores = jnp.where(allowed, raw_scores * score_scale, neg_large)
    prob = jnp.exp(scores - log_total)
    grad_probs = jnp.einsum("qgrd,kgd->grqk", grad, value, preferred_element_type=F32)
    inner = jnp.sum(prob * grad_probs, axis=-1, keepdims=True)
    grad_scores = (prob * (grad_probs - inner)).astype(BF)
    grad_query = jnp.einsum("grqk,kgd->qgrd", grad_scores, key, preferred_element_type=F32)
    grad_key = jnp.einsum("grqk,qgrd->kgd", grad_scores, query, preferred_element_type=F32)
    grad_value = jnp.einsum("grqk,qgrd->kgd", prob.astype(BF), grad, preferred_element_type=F32)
    return grad_query * score_scale, grad_key * score_scale, grad_value


def make_local(n):
    plane_groups = [[PLANE * z + i for i in range(PLANE)] for z in range(n // PLANE)]
    outer_groups = [[PLANE * z + i for z in range(n // PLANE)] for i in range(PLANE)]

    def swap(array, offset):
        return lax.ppermute(array, "dp", [(i, i ^ offset) for i in range(n)])

    def plane_gather(block):
        half = block.shape[0] // 2
        by_x, by_y = swap(block, 2), swap(block, 4)
        corner = jnp.concatenate([swap(by_y[:half], 2), swap(by_x[half:], 4)], axis=0)
        same_core = [block, by_x, by_y, corner]
        other_core = [swap(part, 1) for part in same_core]
        return [part for pair in zip(same_core, other_core) for part in pair]

    def plane_sum(parts):
        def up(v):
            return v.astype(F32)

        s0, s2, s4, s6 = (up(parts[k]) + up(swap(parts[k + 1], 1)) for k in (0, 2, 4, 6))
        half = s6.shape[0] // 2
        s6 = s6.astype(BF)
        s4 = jnp.concatenate([s4[:half] + up(swap(s6[:half], 2)), s4[half:]], axis=0)
        s2 = jnp.concatenate([s2[:half], s2[half:] + up(swap(s6[half:], 4))], axis=0)
        return s0 + up(swap(s2.astype(BF), 2)) + up(swap(s4.astype(BF), 4))

    def local(
        tokens,
        query_weight,
        key_projection_weight,
        value_projection_weight,
        output_weight,
        first_gain,
        second_gain,
        router_weight,
        gate_weight,
        up_weight,
        down_weight,
        routes,
        segments,
        cotangent,
    ):
        rows, width = tokens.shape
        ff = gate_weight.shape[2]
        share = query_weight.shape[0]
        me = lax.axis_index("dp")
        place = lax.rem(me, PLANE)

        dense_part = jnp.concatenate(
            [
                query_weight,
                key_projection_weight,
                value_projection_weight,
                output_weight.T,
                router_weight,
                first_gain[:, None],
                second_gain[:, None],
                jnp.zeros((share, 128 - EXPERTS - 2), BF),
            ],
            axis=1,
        )
        dense = lax.all_gather(dense_part, "dp", axis=0, tiled=True)
        query_full, key_full, value_full = dense[:, :1024], dense[:, 1024:1536], dense[:, 1536:2048]
        output_turned = dense[:, 2048:3072]
        router_full = dense[:, 3072 : 3072 + EXPERTS]
        gain_one = dense[:, 3072 + EXPERTS].astype(F32)
        gain_two = dense[:, 3073 + EXPERTS].astype(F32)

        def by_owner(w):
            return w.transpose(1, 0, 2).reshape(share, PLANE, MINE * ff)

        expert_part = jnp.concatenate(
            [by_owner(gate_weight), by_owner(up_weight), by_owner(down_weight.transpose(0, 2, 1))],
            axis=2,
        ).transpose(1, 0, 2)
        expert_part = lax.all_to_all(
            expert_part, "dp", split_axis=0, concat_axis=0, axis_index_groups=plane_groups
        ).reshape(PLANE * share, 3 * MINE * ff)
        expert_full = lax.all_gather(
            expert_part, "dp", axis=0, tiled=True, axis_index_groups=outer_groups
        )
        wide = MINE * ff
        gate_full, up_full, down_turned = (expert_full[:, k * wide : (k + 1) * wide] for k in range(3))

        route_mask = jnp.sum(
            routes[:, :, None] == jnp.arange(EXPERTS, dtype=jnp.int32)[None, None, :], axis=1
        ).astype(F32)
        grads_plane = jnp.concatenate(plane_gather(cotangent), axis=0)

        cosine, sine = rope_tables(rows, HEAD_SIZE, 1)
        inputs = tokens.astype(F32)
        first_scale = rms_scale(inputs)
        normed_one = (inputs * first_scale * gain_one).astype(BF)
        query = dot(normed_one, query_full, 1, 0).reshape(rows, QUERY_HEADS, HEAD_SIZE)
        key = dot(normed_one, key_full, 1, 0).reshape(rows, KEY_VALUE_HEADS, HEAD_SIZE)
        value = dot(normed_one, value_full, 1, 0).astype(BF).reshape(rows, KEY_VALUE_HEADS, HEAD_SIZE)
        query = rotate(query, cosine, sine).astype(BF)
        key = rotate(key, cosine, sine).astype(BF)
        query = query.reshape(rows, KEY_VALUE_HEADS, QUERY_HEADS // KEY_VALUE_HEADS, HEAD_SIZE)
        seg = segments[0]
        positions = jnp.arange(rows, dtype=jnp.int32)
        allowed = (seg[:, None] == seg[None, :]) & (positions[:, None] >= positions[None, :])
        score_scale = 1.0 / math.sqrt(HEAD_SIZE)
        mixed, log_total = attention_forward(query, key, value, allowed, score_scale)
        mixed = mixed.reshape(rows, QUERY_HEADS * HEAD_SIZE).astype(BF)
        resid = inputs + dot(mixed, output_turned, 1, 1)
        second_scale = rms_scale(resid)
        normed_two = (resid * second_scale * gain_two).astype(BF)
        logits = dot(normed_two, router_full, 1, 0)
        masked = jnp.where(route_mask > 0, logits, neg_large)
        top = jnp.max(masked, axis=-1, keepdims=True)
        weight = jnp.exp(masked - top) * route_mask
        gates = weight / jnp.sum(weight, axis=-1, keepdims=True)

        gate_rows = gates.T
        gate_high = gate_rows.astype(BF)
        gate_low = (gate_rows - gate_high.astype(F32)).astype(BF)
        packed = jnp.concatenate([gate_high, gate_low], axis=1).reshape(EXPERTS, 2 * rows)
        sent = jnp.concatenate([normed_two, packed.reshape(-1, width)], axis=0)
        got = plane_gather(sent)
        tokens_plane = jnp.concatenate([b[:rows] for b in got], axis=0)

        def my_gates(b):
            halves = b[rows:].reshape(EXPERTS, 2, rows)
            own = lax.dynamic_slice_in_dim(halves, place * MINE, MINE, axis=0).astype(F32)
            return own[:, 0] + own[:, 1]

        gates_mine = jnp.concatenate([my_gates(b) for b in got], axis=1)
        gate_cols = gates_mine.T
        gate_wide = jnp.repeat(gate_cols, ff, axis=1)

        act_a = dot(tokens_plane, gate_full, 1, 0)
        act_b = dot(tokens_plane, up_full, 1, 0)
        grad_down = dot(grads_plane, down_turned, 1, 0)
        sigma = jax.nn.sigmoid(act_a)
        silu = act_a * sigma
        hidden = (silu * act_b).astype(BF).astype(F32)
        gate_grad_rows = jnp.sum((hidden * grad_down).reshape(-1, MINE, ff), axis=2)
        hidden_gated = (hidden * gate_wide).astype(BF)
        grad_hidden = grad_down * gate_wide
        grad_a = (grad_hidden * act_b * (sigma * (1.0 + act_a * (1.0 - sigma)))).astype(BF)
        grad_b = (grad_hidden * silu).astype(BF)
        grad_tokens = (dot(grad_a, gate_full, 1, 1) + dot(grad_b, up_full, 1, 1)).astype(BF)
        expert_out = dot(hidden_gated, down_turned, 1, 1).astype(BF)
        gate_grad = dot(tokens_plane, grad_a, 0, 0)
        up_grad = dot(tokens_plane, grad_b, 0, 0)
        down_grad = dot(grads_plane, hidden_gated, 0, 0)

        back_rows = gate_grad_rows.reshape(PLANE, rows, MINE).transpose(0, 2, 1)
        back_high = back_rows.astype(BF)
        back_low = (back_rows - back_high.astype(F32)).astype(BF)
        back = jnp.concatenate([back_high, back_low], axis=2)
        back = lax.dynamic_update_slice_in_dim(
            jnp.zeros((PLANE, EXPERTS, 2 * rows), BF), back, place * MINE, axis=1
        ).reshape(PLANE, -1, width)
        blocks = [
            jnp.concatenate([grad_tokens[k * rows : (k + 1) * rows], back[k]], axis=0)
            for k in range(PLANE)
        ]
        returned = plane_sum(blocks)
        grad_normed_two = returned[:rows]
        halves = returned[rows:].reshape(EXPERTS, 2, rows)
        grad_gates = (halves[:, 0] + halves[:, 1]).T
        experts_sum = plane_sum([expert_out[k * rows : (k + 1) * rows] for k in range(PLANE)])
        output = (resid + experts_sum).astype(BF)

        expert_grads = jnp.concatenate([gate_grad, up_grad, down_grad], axis=1).astype(BF)
        expert_grads = lax.psum_scatter(
            expert_grads, "dp", scatter_dimension=0, tiled=True, axis_index_groups=outer_groups
        )
        expert_grads = lax.all_to_all(
            expert_grads.reshape(PLANE, share, 3 * wide),
            "dp",
            split_axis=0,
            concat_axis=0,
            axis_index_groups=plane_groups,
        )
        expert_grads = expert_grads.reshape(PLANE, share, 3, MINE, ff).astype(F32)
        gate_out, up_out, down_out = (
            expert_grads[:, :, k].transpose(0, 2, 1, 3).reshape(EXPERTS, share, ff) for k in range(3)
        )
        down_out = down_out.transpose(0, 2, 1)

        grad_final = cotangent.astype(F32)
        grad_chosen = gates * (grad_gates - jnp.sum(gates * grad_gates, axis=-1, keepdims=True))
        grad_logits = grad_chosen.astype(BF)
        grad_normed_two = grad_normed_two + dot(grad_logits, router_full, 1, 1)
        router_grad = dot(normed_two, grad_logits, 0, 0)
        grad_resid_norm, second_gain_grad = norm_back(resid, second_scale, gain_two, grad_normed_two)
        grad_resid = grad_final + grad_resid_norm
        grad_branch = grad_resid.astype(BF)
        output_turned_grad = dot(grad_branch, mixed, 0, 0)
        attention_gradient = dot(grad_branch, output_turned, 1, 0).astype(BF).reshape(query.shape)
        grad_query, grad_key, grad_value = attention_backward(
            query, key, value, allowed, log_total, attention_gradient, score_scale
        )
        grad_query = rotate(grad_query.reshape(rows, QUERY_HEADS, HEAD_SIZE), cosine, -sine)
        grad_key = rotate(grad_key.reshape(rows, KEY_VALUE_HEADS, HEAD_SIZE), cosine, -sine)
        grad_qkv = jnp.concatenate(
            [grad_query.reshape(rows, -1), grad_key.reshape(rows, -1), grad_value.reshape(rows, -1)],
            axis=1,
        ).astype(BF)
        qkv_grad = dot(normed_one, grad_qkv, 0, 0)
        grad_normed_one = dot(grad_qkv, dense[:, :2048], 1, 1)
        grad_input_norm, first_gain_grad = norm_back(inputs, first_scale, gain_one, grad_normed_one)
        input_grad = grad_resid + grad_input_norm

        dense_grads = jnp.concatenate(
            [
                qkv_grad,
                output_turned_grad,
                router_grad,
                first_gain_grad[:, None],
                second_gain_grad[:, None],
                jnp.zeros((width, 128 - EXPERTS - 2), F32),
            ],
            axis=1,
        ).astype(BF)
        dense_grads = lax.psum_scatter(dense_grads, "dp", scatter_dimension=0, tiled=True).astype(F32)
        return (
            output,
            input_grad,
            dense_grads[:, :1024],
            dense_grads[:, 1024:1536],
            dense_grads[:, 1536:2048],
            dense_grads[:, 2048:3072].T,
            dense_grads[:, 3072 + EXPERTS],
            dense_grads[:, 3073 + EXPERTS],
            dense_grads[:, 3072 : 3072 + EXPERTS],
            gate_out,
            up_out,
            down_out,
        )

    return local


def solution(mesh):
    in_specs = (
        P("dp", None),
        P("dp", None),
        P("dp", None),
        P("dp", None),
        P(None, "dp"),
        P("dp"),
        P("dp"),
        P("dp", None),
        P(None, "dp", None),
        P(None, "dp", None),
        P(None, None, "dp"),
        P("dp", None),
        P("dp", None),
        P("dp", None),
    )
    out_specs = (
        P("dp", None),
        P("dp", None),
        P("dp", None),
        P("dp", None),
        P("dp", None),
        P(None, "dp"),
        P("dp"),
        P("dp"),
        P("dp", None),
        P(None, "dp", None),
        P(None, "dp", None),
        P(None, None, "dp"),
    )
    return jax.shard_map(
        make_local(mesh.shape["dp"]), mesh=mesh, in_specs=in_specs, out_specs=out_specs, check_vma=False
    )
```

```python
import functools

import jax
import jax.numpy as jnp
from jax import lax
from jax.experimental import pallas as pl
from jax.experimental.pallas import tpu as pltpu
from jax.sharding import PartitionSpec as P

EXPERTS = 16
PLANE = 8
MINE = EXPERTS // PLANE
HEADS = 16
HEAD_SIZE = 64
BLOCK = 128
MOST_DOC = 256
MIB = 2**20
VMEM_ROOM = 60 * MIB
SMALL = pl.CostEstimate(flops=1, bytes_accessed=1, transcendentals=0)
epsilon = 1e-06
neg_large = -1000000000.0
BF = jnp.bfloat16
F32 = jnp.float32


def dot(a, b, ca, cb):
    return lax.dot_general(a, b, (((ca,), (cb,)), ((), ())), preferred_element_type=F32)

def rms_scale(values):
    return lax.rsqrt(jnp.mean(values * values, axis=-1, keepdims=True) + epsilon)

def swap_halves(u):
    lane = lax.broadcasted_iota(jnp.int32, u.shape, 1)
    return jnp.where(lane % 64 < 32, pltpu.roll(u, u.shape[1] - 32, 1), pltpu.roll(u, 32, 1))

def key_range(rows, qb):
    end = (qb + 1) * BLOCK
    return max(0, end - BLOCK - MOST_DOC), end

def fill_mask(mask_ref, seg_col_ref, seg_row_ref, rows):
    for qb in range(rows // BLOCK):
        low, high = key_range(rows, qb)
        keys = low + lax.broadcasted_iota(jnp.int32, (high - low, BLOCK), 0)
        queries = qb * BLOCK + lax.broadcasted_iota(jnp.int32, (high - low, BLOCK), 1)
        same = seg_col_ref[low:high, :1] == seg_row_ref[:1, qb * BLOCK : (qb + 1) * BLOCK]
        mask_ref[qb, : high - low] = jnp.where(same & (keys <= queries), 1.0, 0.0)

def masked_scores(mask_ref, k_c, q_pair, qb, span):
    s = dot(k_c, q_pair, 1, 1)
    m = mask_ref[qb, :span]
    return jnp.where(jnp.concatenate([m, m], axis=1) > 0, s, neg_large)

def piece_copies(me_ref, spots, pieces, whole_ref, sems, inward):
    copies = []
    for ref, (offsets, first) in zip(pieces, spots):
        if offsets is None:
            sides = [(ref, whole_ref)]
        else:
            share, cols = ref.shape[1:]
            sides = []
            for i, offset in enumerate(offsets):
                row = pl.multiple_of((me_ref[0] ^ offset) * share, share)
                sides.append((ref.at[i], whole_ref.at[pl.ds(row, share), first : first + cols]))
        for part, place in sides:
            source, target = (part, place) if inward else (place, part)
            copies.append(pltpu.make_async_copy(source, target, sems.at[len(copies)]))
    return copies


def piece_count(spots):
    return sum(1 if offsets is None else len(offsets) for offsets, _ in spots)


def forward_kernel(spots, me_ref, x_ref, routes_ref, seg_col_ref, seg_row_ref, cos_ref, sin_ref, *refs):
    pieces, refs = refs[: len(spots)], refs[len(spots) :]
    (h1_ref, q_ref, k_ref, v_ref, o_ref, lse_ref, r1_ref, h2_ref, dense_ref) = refs[:9]
    mask_ref, w_ref, sems, out_sem = refs[9:]
    copies = piece_copies(me_ref, spots, pieces, w_ref, sems, True)
    for copy in copies:
        copy.start()
    fill_mask(mask_ref, seg_col_ref, seg_row_ref, x_ref.shape[0])
    for copy in copies:
        copy.wait()
    keep = pltpu.make_async_copy(w_ref, dense_ref, out_sem)
    keep.start()
    rows, width = x_ref.shape
    x = x_ref[...].astype(F32)
    gains = w_ref[:, 3072:3200].astype(F32).T
    h1_ref[...] = (x * rms_scale(x) * gains[16:17]).astype(BF)

    @pl.loop(0, 4)
    def _(j):
        qs = pl.ds(pl.multiple_of(j * 256, 256), 256)
        ks = pl.ds(pl.multiple_of(j * 128, 128), 128)
        vs = pl.ds(pl.multiple_of(1536 + j * 128, 128), 128)
        kw = pl.ds(pl.multiple_of(1024 + j * 128, 128), 128)
        h1 = h1_ref[...]
        cos, sin = cos_ref[...], sin_ref[...]
        q2 = dot(h1, w_ref[:, qs], 1, 0)
        qa, qb_ = q2[:, :128], q2[:, 128:]
        qa = (qa * cos + swap_halves(qa) * sin).astype(BF) * BF(0.125)
        qb_ = (qb_ * cos + swap_halves(qb_) * sin).astype(BF) * BF(0.125)
        k = dot(h1, w_ref[:, kw], 1, 0)
        k = (k * cos + swap_halves(k) * sin).astype(BF)
        v32 = dot(h1, w_ref[:, vs], 1, 0)
        v = v32.astype(BF)
        q_ref[:, qs] = jnp.concatenate([qa, qb_], axis=1)
        k_ref[:, ks] = k
        v_ref[:, ks] = v
        vt = v32.T.astype(BF)
        lane = lax.broadcasted_iota(jnp.int32, (rows, 128), 1)
        sub = lax.broadcasted_iota(jnp.int32, (128, rows), 0)
        outs = []
        for qb in range(rows // BLOCK):
            low, high = key_range(rows, qb)
            blk = slice(qb * BLOCK, (qb + 1) * BLOCK)
            q_pair = jnp.concatenate([qa[blk], qb_[blk]], axis=0)
            total = None
            for c in range(2):
                k_c = jnp.where(lane[low:high] // 64 == c, k[low:high], BF(0))
                vt_c = jnp.where(sub[:, low:high] // 64 == c, vt[:, low:high], BF(0))
                s = masked_scores(mask_ref, k_c, q_pair, qb, high - low)
                top = jnp.max(s, axis=0, keepdims=True)
                e = jnp.exp(s - top)
                norm = jnp.sum(e, axis=0, keepdims=True)
                p = (e * (1.0 / norm)).astype(BF)
                part = dot(vt_c, p, 1, 0)
                total = part if total is None else total + part
                lse = top + jnp.log(norm)
                lse_ref[j, c : c + 1, blk] = lse[:, :128]
                lse_ref[j, 2 + c : 3 + c, blk] = lse[:, 128:]
            outs.append(total)
        a = jnp.concatenate([t[:, :128] for t in outs], axis=1).T.astype(BF)
        b = jnp.concatenate([t[:, 128:] for t in outs], axis=1).T.astype(BF)
        o_ref[:, qs] = jnp.concatenate([a, b], axis=1)

    r1 = x_ref[...].astype(F32) + dot(o_ref[...], w_ref[:, 2048:3072], 1, 1)
    r1_ref[...] = r1
    h2 = (r1 * rms_scale(r1) * gains[17:18]).astype(BF)
    h2_ref[:rows] = h2
    logits = dot(h2, w_ref[:, 3072:3200], 1, 0).T[:EXPERTS]
    at = lax.broadcasted_iota(jnp.int32, (EXPERTS, rows), 0)
    chosen = at < 0
    for t in range(routes_ref.shape[0]):
        chosen = chosen | (at == routes_ref[t : t + 1])
    logits = jnp.where(chosen, logits, neg_large)
    ex = jnp.where(chosen, jnp.exp(logits - jnp.max(logits, axis=0, keepdims=True)), 0.0)
    gates = ex / jnp.sum(ex, axis=0, keepdims=True)
    high = gates.astype(BF)
    low = (gates - high.astype(F32)).astype(BF)
    h2_ref[rows:] = jnp.concatenate([high, low], axis=1)
    keep.wait()

def forward_call(me, x, routes, seg_col, seg_row, cos, sin, pieces, spots):
    rows, width = x.shape
    s = jax.ShapeDtypeStruct
    vmem, anywhere = pl.BlockSpec(memory_space=pltpu.VMEM), pl.BlockSpec(memory_space=pl.ANY)
    return pl.pallas_call(
        functools.partial(forward_kernel, spots),
        in_specs=[pl.BlockSpec(memory_space=pltpu.SMEM)] + [vmem] * 6 + [anywhere] * len(pieces),
        out_specs=[vmem] * 8 + [anywhere],
        out_shape=[
            s((rows, width), BF),
            s((rows, 1024), BF),
            s((rows, 512), BF),
            s((rows, 512), BF),
            s((rows, 1024), BF),
            s((4, 4, rows), F32),
            s((rows, width), F32),
            s((rows + EXPERTS, width), BF),
            s((width, 3200), BF),
        ],
        scratch_shapes=[
            pltpu.VMEM((rows // BLOCK, BLOCK + MOST_DOC, BLOCK), F32),
            pltpu.VMEM((width, 3200), BF),
            pltpu.SemaphoreType.DMA((piece_count(spots),)),
            pltpu.SemaphoreType.DMA,
        ],
        cost_estimate=SMALL,
        compiler_params=pltpu.CompilerParams(vmem_limit_bytes=VMEM_ROOM),
    )(me, x, routes, seg_col, seg_row, cos, sin, *pieces)


def backward_kernel(
    spots, me_ref, p0, p1, p2, p3, p4_top, p4_low, x_ref, r1_ref, cot_ref, h1_ref, h2_ref, w_ref, q_ref, k_ref, v_ref, o_ref,
    lse_ref, seg_col_ref, seg_row_ref, cos_ref, sin_ref, ig_ref, *refs
):
    pieces, refs = refs[: len(spots)], refs[len(spots) :]
    mask_ref, do_ref, dqkv_ref, dr1_ref, wg_ref, sems = refs
    rows, width = x_ref.shape
    misc = w_ref[:, 3072:3200]
    gains = misc.astype(F32).T

    def up(ref, sl):
        return ref[sl].astype(F32)

    top, tail = slice(0, rows), slice(rows, rows + EXPERTS)
    dh2 = up(p0, top) + up(p1, top) + up(p2, top) + up(p3, top)
    half = p4_top.shape[0]
    dh2 = dh2 + jnp.concatenate([p4_top[...].astype(F32), up(p4_low, slice(0, rows - half))], axis=0)
    dg = up(p0, tail) + up(p1, tail) + up(p2, tail) + up(p3, tail) + up(p4_low, slice(rows - half, None))
    dg = dg[:, :rows] + dg[:, rows:]
    gates = up(h2_ref, tail)
    gates = gates[:, :rows] + gates[:, rows:]
    h2 = h2_ref[:rows]
    dlog = gates * (dg - jnp.sum(gates * dg, axis=0, keepdims=True))
    dlog = jnp.concatenate([dlog, jnp.zeros((128 - EXPERTS, rows), F32)], axis=0).T.astype(BF)
    dh2 = dh2 + dot(dlog, misc, 1, 1)
    r1 = r1_ref[...]
    s2 = rms_scale(r1)
    w2 = dh2 * gains[17:18]
    gain2_grad = jnp.sum(dh2 * r1 * s2, axis=0, keepdims=True)
    dr1 = cot_ref[...].astype(F32) + s2 * w2 - r1 * (s2 * s2 * s2) * jnp.mean(w2 * r1, axis=-1, keepdims=True)
    dr1_ref[...] = dr1
    dz = dr1.astype(BF)
    wg_ref[:, 2048:3072] = dot(dz, o_ref[...], 0, 0).astype(BF)
    do_ref[...] = dot(dz, w_ref[:, 2048:3072], 1, 0).astype(BF)
    router_t = dot(dlog, h2, 0, 0)
    fill_mask(mask_ref, seg_col_ref, seg_row_ref, rows)

    @pl.loop(0, 4)
    def _(j):
        qs = pl.ds(pl.multiple_of(j * 256, 256), 256)
        ks = pl.ds(pl.multiple_of(j * 128, 128), 128)
        vs = pl.ds(pl.multiple_of(1536 + j * 128, 128), 128)
        kw = pl.ds(pl.multiple_of(1024 + j * 128, 128), 128)
        cos, sin = cos_ref[...], sin_ref[...]
        def back(g):
            return (g * cos - swap_halves(g) * sin).astype(BF)
        q, k, v, do = q_ref[:, qs], k_ref[:, ks], v_ref[:, ks], do_ref[:, qs]
        kt = k.astype(F32).T.astype(BF)
        lane = lax.broadcasted_iota(jnp.int32, (rows, 128), 1)
        sub = lax.broadcasted_iota(jnp.int32, (128, rows), 0)
        dks = [jnp.zeros((BLOCK, 128), F32) for _ in range(rows // BLOCK)]
        dvs = [jnp.zeros((BLOCK, 128), F32) for _ in range(rows // BLOCK)]
        dqs = []
        for qb in range(rows // BLOCK):
            low, high = key_range(rows, qb)
            blk = slice(qb * BLOCK, (qb + 1) * BLOCK)
            q_pair = jnp.concatenate([q[blk, :128], q[blk, 128:]], axis=0)
            do_pair = jnp.concatenate([do[blk, :128], do[blk, 128:]], axis=0)
            dq_t = None
            for c in range(2):
                mine = lane[low:high] // 64 == c
                k_c = jnp.where(mine, k[low:high], BF(0))
                v_c = jnp.where(mine, v[low:high], BF(0))
                kt_c = jnp.where(sub[:, low:high] // 64 == c, kt[:, low:high], BF(0))
                s = masked_scores(mask_ref, k_c, q_pair, qb, high - low)
                lse = jnp.concatenate([lse_ref[j, c : c + 1, blk], lse_ref[j, 2 + c : 3 + c, blk]], axis=1)
                p = jnp.exp(s - lse)
                dp = dot(v_c, do_pair, 1, 1)
                inner = jnp.sum(p * dp, axis=0, keepdims=True)
                ds = (p * (dp - inner)).astype(BF)
                dk = dot(ds, q_pair, 1, 0)
                dv = dot(p.astype(BF), do_pair, 1, 0)
                t = dot(kt_c, ds, 1, 0)
                dq_t = t if dq_t is None else dq_t + t
                for i, kb in enumerate(range(low // BLOCK, high // BLOCK)):
                    sl = slice(i * BLOCK, (i + 1) * BLOCK)
                    dks[kb] = dks[kb] + jnp.where(mine[sl], dk[sl], 0.0)
                    dvs[kb] = dvs[kb] + jnp.where(mine[sl], dv[sl], 0.0)
            dqs.append(dq_t)
        dqa = jnp.concatenate([t[:, :128] for t in dqs], axis=1).T * 0.125
        dqb = jnp.concatenate([t[:, 128:] for t in dqs], axis=1).T * 0.125
        dqkv_ref[:, qs] = jnp.concatenate([back(dqa), back(dqb)], axis=1)
        dqkv_ref[:, kw] = back(jnp.concatenate(dks, axis=0))
        dqkv_ref[:, vs] = jnp.concatenate(dvs, axis=0).astype(BF)

    dqkv = dqkv_ref[...]
    wg_ref[:, :2048] = dot(h1_ref[...], dqkv, 0, 0).astype(BF)
    dh1 = dot(dqkv, w_ref[:, :2048], 1, 1)
    x = x_ref[...].astype(F32)
    s1 = rms_scale(x)
    w1 = dh1 * gains[16:17]
    gain1_grad = jnp.sum(dh1 * x * s1, axis=0, keepdims=True)
    ig_ref[...] = dr1_ref[...] + s1 * w1 - x * (s1 * s1 * s1) * jnp.mean(w1 * x, axis=-1, keepdims=True)
    at = lax.broadcasted_iota(jnp.int32, (128, width), 0)
    misc_t = jnp.where(at == 16, gain1_grad, jnp.where(at == 17, gain2_grad, router_t))
    wg_ref[:, 3072:3200] = misc_t.T.astype(BF)
    copies = piece_copies(me_ref, spots, pieces, wg_ref, sems, False)
    for copy in copies:
        copy.start()
    for copy in copies:
        copy.wait()

def backward_call(me, parts, x, r1, cot, h1, h2, w, q, k, v, o, lse, seg_col, seg_row, cos, sin, piece_shapes, spots):
    rows, width = x.shape
    s = jax.ShapeDtypeStruct
    vmem, anywhere = pl.BlockSpec(memory_space=pltpu.VMEM), pl.BlockSpec(memory_space=pl.ANY)
    return pl.pallas_call(
        functools.partial(backward_kernel, spots),
        in_specs=[pl.BlockSpec(memory_space=pltpu.SMEM)] + [vmem] * 21,
        out_specs=[vmem] + [anywhere] * len(spots),
        out_shape=[s((rows, width), F32)] + [s(shape, BF) for shape in piece_shapes],
        scratch_shapes=[
            pltpu.VMEM((rows // BLOCK, BLOCK + MOST_DOC, BLOCK), F32),
            pltpu.VMEM((rows, 1024), BF),
            pltpu.VMEM((rows, 2048), BF),
            pltpu.VMEM((rows, width), F32),
            pltpu.VMEM((width, 3200), BF),
            pltpu.SemaphoreType.DMA((piece_count(spots),)),
        ],
        cost_estimate=SMALL,
        compiler_params=pltpu.CompilerParams(vmem_limit_bytes=VMEM_ROOM),
    )(me, *parts, x, r1, cot, h1, h2, w, q, k, v, o, lse, seg_col, seg_row, cos, sin)


def expert_kernel(plan, count, place_ref, *refs):
    arrays, refs = refs[:count], refs[count:]
    w_refs = refs[:6]
    ug0, ug1, da0, da1, db0, db1, dg_ref, h_all, g_all, h_buf, g_buf, sems = refs[-12:]
    rows = g_buf.shape[1]
    step = pl.program_id(0)

    def copies(i):
        found = []
        for buf, parts in ((h_buf, plan[i][0]), (g_buf, plan[i][1])):
            for array, start, size, at in parts:
                sem = sems.at[i % 2, len(found)]
                found.append(
                    pltpu.make_async_copy(
                        arrays[array].at[pl.ds(start, size)], buf.at[i % 2, pl.ds(at, size)], sem
                    )
                )
        return found

    for i in range(len(plan)):

        @pl.when(step == i)
        def _(i=i):
            if i == 0:
                for copy in copies(0):
                    copy.start()
            if i + 1 < len(plan):
                for copy in copies(i + 1):
                    copy.start()
            for copy in copies(i):
                copy.wait()

    slot = lax.rem(step, 2)
    h = h_buf[slot, :rows]
    g = g_buf[slot]
    tail = h_buf[slot, rows:].astype(F32)
    tail = tail[:, :rows] + tail[:, rows:]
    gates = jnp.concatenate([tail, jnp.zeros((128 - EXPERTS, rows), F32)], axis=0).T
    h_all[...] = h
    g_all[...] = g
    lane = lax.broadcasted_iota(jnp.int32, (rows, 128), 1)
    totals = []
    for e, (ug_ref, da_ref, db_ref) in enumerate(((ug0, da0, db0), (ug1, da1, db1))):
        wg_ref, wu_ref, wd_ref = w_refs[3 * e : 3 * e + 3]
        ff = wg_ref.shape[2]
        gate = jnp.sum(jnp.where(lane == place_ref[0] * MINE + e, gates, 0.0), axis=1, keepdims=True)
        total = 0.0
        for half in range(2):
            sl = slice(half * ff // 2, (half + 1) * ff // 2)
            a = dot(h, wg_ref[0, :, sl], 1, 0)
            b = dot(h, wu_ref[0, :, sl], 1, 0)
            gd = dot(g, wd_ref[0, :, sl], 1, 0)
            sigma = 1.0 / (1.0 + jnp.exp(-a))
            silu = a * sigma
            u = (silu * b).astype(BF).astype(F32)
            total = total + jnp.sum(u * gd, axis=1, keepdims=True)
            ug_ref[:, sl] = (u * gate).astype(BF)
            du = gd * gate
            db_ref[:, sl] = (du * silu).astype(BF)
            da_ref[:, sl] = (du * b * (sigma * (1.0 + a * (1.0 - sigma)))).astype(BF)
        totals.append(total)
    dg_ref[0] = jnp.where(lane == 0, totals[0], totals[1]).T[:8]


def expert_call(place, arrays, plan, weights, first, kept):
    _, width, ff = weights.shape
    rows = sum(piece[2] for piece in plan[0][1])
    most = max(len(h) + len(g) for h, g in plan)
    s = jax.ShapeDtypeStruct
    at = lambda i: (first + i, 0)
    anywhere = pl.BlockSpec(memory_space=pl.ANY)
    tile, hidden = pl.BlockSpec((rows, width), at), pl.BlockSpec((rows, ff), at)
    held = 1 + len(arrays) + 6
    return pl.pallas_call(
        functools.partial(expert_kernel, plan, len(arrays)),
        grid=(len(plan),),
        in_specs=[pl.BlockSpec(memory_space=pltpu.SMEM)]
        + [anywhere] * len(arrays)
        + [pl.BlockSpec((1, width, ff), lambda i, k=k: (k, 0, 0), pipeline_mode=pl.Buffered(1)) for k in range(6)]
        + [anywhere] * len(kept),
        out_specs=[hidden] * 6 + [pl.BlockSpec((1, 8, rows), lambda i: (first + i, 0, 0))] + [tile] * 2,
        out_shape=[s((PLANE * rows, ff), BF)] * 6
        + [s((PLANE, 8, rows), F32)]
        + [s((PLANE * rows, width), BF)] * 2,
        input_output_aliases={held + i: i for i in range(len(kept))},
        scratch_shapes=[
            pltpu.VMEM((2, rows + EXPERTS, width), BF),
            pltpu.VMEM((2, rows, width), BF),
            pltpu.SemaphoreType.DMA((2, most)),
        ],
        cost_estimate=SMALL,
        compiler_params=pltpu.CompilerParams(vmem_limit_bytes=VMEM_ROOM),
    )(place, *arrays, *[weights] * 6, *kept)


def turn_back_kernel(pairs, count, tailed, *refs):
    refs = list(refs)
    if tailed:
        place_ref, dg_ref = refs[:2]
        refs = refs[2:]
    outs, buf, sems = refs[2 * pairs : 2 * pairs + count], refs[-2], refs[-1]
    step = pl.program_id(0)
    slot = lax.rem(step, 2)

    def copy(i):
        return pltpu.make_async_copy(buf.at[i % 2], outs[i], sems.at[i % 2])

    for i in range(2, count):

        @pl.when(step == i)
        def _(i=i):
            copy(i - 2).wait()

    total = 0.0
    for i in range(pairs):
        total = total + dot(refs[i][...], refs[pairs + i][0], 1, 1)
    rows = total.shape[0]
    buf[slot, :rows] = total.astype(BF)
    if tailed:
        place = place_ref[0]
        at = lax.broadcasted_iota(jnp.int32, (EXPERTS, rows), 0)
        dg = jnp.where(
            at == place * MINE, dg_ref[0, :1], jnp.where(at == place * MINE + 1, dg_ref[0, 1:2], 0.0)
        )
        high = dg.astype(BF)
        low = (dg - high.astype(F32)).astype(BF)
        buf[slot, rows:] = jnp.concatenate([high, low], axis=1)
    for i in range(count):

        @pl.when(step == i)
        def _(i=i):
            copy(i).start()
            if i == count - 1:
                copy(i - 1).wait()
                copy(i).wait()


def turn_back(first, count, acts, weights, kinds, tail):
    rows = acts[0].shape[0] // PLANE
    _, width, ff = weights.shape
    extra = EXPERTS if tail else 0
    in_specs, operands = [], []
    if tail:
        in_specs = [
            pl.BlockSpec(memory_space=pltpu.SMEM),
            pl.BlockSpec((1, 8, rows), lambda i: (first + i, 0, 0)),
        ]
        operands = list(tail)
    in_specs += [pl.BlockSpec((rows, ff), lambda i: (first + i, 0))] * len(acts)
    in_specs += [
        pl.BlockSpec((1, width, ff), lambda i, k=k: (k, 0, 0), pipeline_mode=pl.Buffered(1)) for k in kinds
    ]
    return pl.pallas_call(
        functools.partial(turn_back_kernel, len(acts), count, bool(tail)),
        grid=(count,),
        in_specs=in_specs,
        out_specs=[pl.BlockSpec(memory_space=pl.ANY)] * count,
        out_shape=[jax.ShapeDtypeStruct((rows + extra, width), BF)] * count,
        scratch_shapes=[pltpu.VMEM((2, rows + extra, width), BF), pltpu.SemaphoreType.DMA((2,))],
        cost_estimate=SMALL,
        compiler_params=pltpu.CompilerParams(vmem_limit_bytes=VMEM_ROOM),
    )(*operands, *acts, *[weights] * len(kinds))


def weight_grad_kernel(count, left_ref, *refs):
    rights, out_ref, acc_ref = refs[:count], refs[count], refs[count + 1]
    k = pl.program_id(0)
    ff = rights[0].shape[1]
    part = dot(left_ref[...], jnp.concatenate([r[...] for r in rights], axis=1), 0, 0)

    @pl.when(k == 0)
    def _():
        acc_ref[...] = part

    @pl.when(k > 0)
    def _():
        acc_ref[...] += part

    @pl.when(k == pl.num_programs(0) - 1)
    def _():
        for t in range(count):
            out_ref[t] = acc_ref[:, t * ff : (t + 1) * ff].astype(BF)


def weight_grads(left, rights):
    total, width = left.shape
    ff = rights[0].shape[1]
    count = len(rights)
    step = total // 4
    row = lambda i: (i, 0)
    return pl.pallas_call(
        functools.partial(weight_grad_kernel, count),
        grid=(4,),
        in_specs=[pl.BlockSpec((step, width), row)] + [pl.BlockSpec((step, ff), row)] * count,
        out_specs=pl.BlockSpec((count, width, ff), lambda i: (0, 0, 0), pipeline_mode=pl.Buffered(1)),
        out_shape=jax.ShapeDtypeStruct((count, width, ff), BF),
        scratch_shapes=[pltpu.VMEM((width, count * ff), F32)],
        cost_estimate=SMALL,
        compiler_params=pltpu.CompilerParams(vmem_limit_bytes=VMEM_ROOM),
    )(left, *rights)


def up(v):
    return v.astype(F32)


def after(value, *others):
    return lax.optimization_barrier((value, *others))[0]


CUT = 1536
COLUMNS = 3200


def make_local(n):
    outer = n // PLANE
    plane_groups = [[PLANE * z + i for i in range(PLANE)] for z in range(outer)]
    outer_groups = [[PLANE * z + i for z in range(outer)] for i in range(PLANE)]
    pieced = outer == 4

    def swap(array, offset):
        return lax.ppermute(array, "dp", [(i, i ^ offset) for i in range(n)])

    along_z = [PLANE * k for k in range(4)]

    def dense_gather(part, *earlier):
        if not pieced:
            return [lax.all_gather(part, "dp", axis=0, tiled=True)], [(None, 0)]
        line = after([part] + [swap(part, k) for k in along_z[1:]], *earlier)
        left, right = jnp.stack([t[:, :CUT] for t in line]), jnp.stack([t[:, CUT:] for t in line])
        left_x, right_y = swap(left, 2), swap(right, 4)
        left_y, right_x = swap(left, 4), swap(right, 2)
        left_xy, right_xy = swap(left_x, 4), swap(right_y, 2)
        found = [(left, 0, 0), (left_x, 2, 0), (left_y, 4, 0), (left_xy, 6, 0)]
        found += [(right, 0, CUT), (right_x, 2, CUT), (right_y, 4, CUT), (right_xy, 6, CUT)]
        found += [(swap(piece, 1), offset + 1, first) for piece, offset, first in found]
        return [f[0] for f in found], [([f[1] + k for k in along_z], f[2]) for f in found]

    def grad_spots(share):
        if not pieced:
            return [(n * share, COLUMNS)], [(None, 0)]
        shapes, spots = [], []
        for core in (1, 0):
            for major, minor, first, cols in ((2, 4, 0, CUT), (4, 2, CUT, COLUMNS - CUT)):
                for far in (0, major):
                    shapes.append((8, share, cols))
                    spots.append(([core + far + d + k for d in (0, minor) for k in along_z], first))
        return shapes, spots

    def dense_sum(pieces):
        if not pieced:
            return up(lax.psum_scatter(pieces[0], "dp", scatter_dimension=0, tiled=True)), (pieces[0],)

        def add(a, b):
            return (up(a) + up(b)).astype(BF)

        near_l, far_l, near_r, far_r = (add(keep, swap(sent, 1)) for sent, keep in zip(pieces[:4], pieces[4:]))
        got_l, got_r = swap(far_l, 2), swap(far_r, 4)
        sent_l, sent_r = add(near_l[4:], got_l[4:]), add(near_r[4:], got_r[4:])
        left = add(add(near_l[:4], got_l[:4]), swap(sent_l, 4))
        right = add(add(near_r[:4], got_r[:4]), swap(sent_r, 2))
        both = jnp.concatenate([left, right], axis=2)
        total = up(both[0])
        for k in range(1, 4):
            total = total + up(swap(both[k], PLANE * k))
        return total, (both,)

    def both_cores(same_core):
        return [b for part in same_core for b in (part, swap(part, 1))]

    def local(
        tokens,
        query_weight,
        key_projection_weight,
        value_projection_weight,
        output_weight,
        first_gain,
        second_gain,
        router_weight,
        gate_weight,
        up_weight,
        down_weight,
        routes,
        segments,
        cotangent,
    ):
        rows, width = tokens.shape
        ff = gate_weight.shape[2]
        share = query_weight.shape[0]
        me = lax.axis_index("dp").astype(jnp.int32).reshape(1)
        place = lax.rem(me, PLANE)

        def paired(w):
            return w.reshape(-1, 4, 2, 2, HEAD_SIZE).swapaxes(2, 3).reshape(-1, HEADS * HEAD_SIZE)

        expert_part = jnp.stack(
            [w.reshape(PLANE, MINE, share, ff) for w in (gate_weight, up_weight, down_weight.transpose(0, 2, 1))],
            axis=2,
        )
        dense_part = jnp.concatenate(
            [
                paired(query_weight),
                key_projection_weight,
                value_projection_weight,
                paired(output_weight.T),
                router_weight,
                first_gain[:, None],
                second_gain[:, None],
                jnp.zeros((share, 128 - EXPERTS - 2), BF),
            ],
            axis=1,
        )
        dense_part = after(dense_part, expert_part)
        expert_part = lax.all_to_all(
            expert_part, "dp", split_axis=0, concat_axis=0, axis_index_groups=plane_groups
        )

        expert_part = expert_part.transpose(1, 2, 0, 3, 4).reshape(3 * MINE, PLANE * share, ff)
        weights = lax.all_gather(expert_part, "dp", axis=1, tiled=True, axis_index_groups=outer_groups)

        positions = jnp.arange(rows, dtype=F32)
        frequency = 10000.0 ** (-2.0 * jnp.arange(HEAD_SIZE // 2, dtype=F32) / HEAD_SIZE)
        angles = positions[:, None] * frequency[None, :]
        cosine, sine = jnp.cos(angles), jnp.sin(angles)
        cosine = jnp.concatenate([cosine] * 4, axis=1)
        sine = jnp.concatenate([-sine, sine, -sine, sine], axis=1)
        seg_col = segments.reshape(rows, 1)
        seg_row = segments.reshape(1, rows)

        half = rows // 2
        pieces, spots = dense_gather(dense_part, cosine, sine, seg_col)
        late = after(cotangent, *pieces)
        cot_x, cot_y = swap(late, 2), swap(late, 4)

        h1, q, k, v, o, lse, r1, h2, dense = forward_call(
            me, tokens, routes.T, seg_col, seg_row, cosine, sine, pieces, spots
        )
        h2 = after(h2, cot_x, cot_y)
        h2_x, h2_y, h2_core = swap(h2, 2), swap(h2, 4), swap(h2, 1)
        cot_core = swap(cotangent, 1)
        h2_x, h2_y, cot_x, cot_y = after((h2_x, h2_y, cot_x, cot_y), h2_core, cot_core)
        corner_x = swap(jnp.concatenate([h2_y[:half], cot_y[:half]], axis=0), 2)
        corner_y = swap(jnp.concatenate([h2_x[half:], cot_x[half:]], axis=0), 4)
        cores = [swap(t, 1) for t in (h2_x, cot_x, h2_y, cot_y)]
        long = rows + EXPERTS

        def pieces_of(h, g):
            return ([(h, 0, long, 0)], [(g, 0, rows, 0)])

        near_arrays = [h2, h2_core, h2_x, cores[0], cotangent, cot_core, cot_x, cores[1]]
        near_plan = [pieces_of(i, 4 + i) for i in range(4)]
        kept = expert_call(after(place, *cores), near_arrays, near_plan, weights, 0, ())
        corner_x, corner_y = after((corner_x, corner_y), *cores)
        far_arrays = [h2_y, cores[2], cot_y, cores[3], corner_x, swap(corner_x, 1), corner_y, swap(corner_y, 1)]
        far_plan = [pieces_of(i, 2 + i) for i in range(2)]
        far_plan += [
            (
                [(i, 0, half, 0), (i + 2, 0, long - half, half)],
                [(i, half, half, 0), (i + 2, long - half, half, half)],
            )
            for i in (4, 5)
        ]
        kept = expert_call(place, far_arrays, far_plan, weights, 4, kept)
        ug0, ug1, da0, da1, db0, db1, dg, tokens_all, grads_all = kept

        def outer_sum(grads):
            return lax.psum_scatter(grads, "dp", scatter_dimension=1, tiled=True, axis_index_groups=outer_groups)

        back = functools.partial(turn_back, acts=[da0, db0, da1, db1], weights=weights, kinds=[0, 1, 3, 4])

        def with_core(block, other):
            return (up(block) + up(other)).astype(BF)

        top, low = slice(0, half), slice(half, None)

        def together(*values):
            return lax.optimization_barrier(values)

        far = back(4, 4, tail=(place, dg))
        place, far = together(place, far)

        near, far_core = back(0, 4, tail=(place, dg)), (swap(far[1], 1), swap(far[3], 1))
        near, far, far_core = together(near, far, far_core)
        sum_y = with_core(far[0], far_core[0])
        sum_xy = [with_core(far[2][part], far_core[1][part]) for part in (top, low)]
        sum_y, sum_xy, near, grads_all = together(sum_y, sum_xy, near, grads_all)

        grads_d, got_top = weight_grads(grads_all, [ug0, ug1]), swap(sum_xy[0], 6)
        near_core = swap(near[1], 1), swap(near[3], 1)
        grads_d, got_top, near_core, near, sum_xy, sum_y = together(grads_d, got_top, near_core, near, sum_xy, sum_y)
        sums_d = outer_sum(grads_d)
        sum_x = with_core(near[2], near_core[1])
        sum_x, sum_xy, ug0 = together(sum_x, sum_xy, ug0)

        out, got_low = turn_back(0, PLANE, [ug0, ug1], weights, [2, 5], None), swap(sum_xy[1], 6)
        out, got_low, sum_x, sum_y, tokens_all = together(out, got_low, sum_x, sum_y, tokens_all)

        grads_gu, got_x, got_y = weight_grads(tokens_all, [da0, da1, db0, db1]), swap(sum_x, 2), swap(sum_y, 4)
        out_core = [swap(out[i], 1) for i in (1, 3, 5, 7)]
        grads_gu, got_x, got_y, out, out_core = together(grads_gu, got_x, got_y, out, out_core)
        sums_gu = outer_sum(grads_gu)
        out_x, out_y = with_core(out[2], out_core[1]), with_core(out[4], out_core[2])
        out_xy = [with_core(out[6][part], out_core[3][part]) for part in (top, low)]
        got = [near[0], near_core[0], got_x, got_y, got_top, got_low]
        got, out_x, out_y, out_xy = together(got, out_x, out_y, out_xy)

        shapes, grad_places = grad_spots(share)
        input_grad, *grad_pieces = backward_call(
            me, got, tokens, r1, cotangent, h1, h2, dense, q, k, v, o, lse, seg_col, seg_row, cosine, sine,
            shapes, grad_places,
        )
        out_got = swap(out_x, 2), swap(out_y, 4), swap(out_xy[0], 6)
        input_grad, grad_pieces, out_got, out_xy = together(input_grad, grad_pieces, out_got, out_xy)

        dense_grads, moment = dense_sum(grad_pieces)
        out_low = swap(after(out_xy[1], *moment), 6)
        output = r1 + up(out[0]) + up(out_core[0]) + up(out_got[0]) + up(out_got[1])
        output = (output + jnp.concatenate([up(out_got[2]), up(out_low)], axis=0)).astype(BF)

        def to_owner(grads):
            grads = grads.reshape(-1, PLANE, share, ff).transpose(1, 0, 2, 3)
            return lax.all_to_all(grads, "dp", split_axis=0, concat_axis=0, axis_index_groups=plane_groups)

        owned_d = to_owner(after(sums_d, *moment))
        owned_gu = to_owner(after(sums_gu, owned_d))

        def experts_of(first, second):
            return up(jnp.stack([first, second], axis=1)).reshape(EXPERTS, share, ff)

        gate_out = experts_of(owned_gu[:, 0], owned_gu[:, 1])
        up_out = experts_of(owned_gu[:, 2], owned_gu[:, 3])
        down_out = experts_of(owned_d[:, 0], owned_d[:, 1]).transpose(0, 2, 1)

        return (
            output,
            input_grad,
            paired(dense_grads[:, :1024]),
            dense_grads[:, 1024:1536],
            dense_grads[:, 1536:2048],
            paired(dense_grads[:, 2048:3072]).T,
            dense_grads[:, 3072 + EXPERTS],
            dense_grads[:, 3073 + EXPERTS],
            dense_grads[:, 3072 : 3072 + EXPERTS],
            gate_out,
            up_out,
            down_out,
        )

    return local


def solution(mesh):
    row, col, one = P("dp", None), P(None, "dp"), P("dp")
    middle, last = P(None, "dp", None), P(None, None, "dp")
    in_specs = (row, row, row, row, col, one, one, row, middle, middle, last, row, row, row)
    out_specs = (row, row, row, row, row, col, one, one, row, middle, middle, last)
    return jax.shard_map(
        make_local(mesh.shape["dp"]), mesh=mesh, in_specs=in_specs, out_specs=out_specs, check_vma=False
    )
```

```python
import functools

import jax
import jax.numpy as jnp
from jax import lax
from jax.experimental import pallas as pl
from jax.experimental.pallas import tpu as pltpu
from jax.sharding import PartitionSpec as P

EXPERTS = 16
PLANE = 8
MINE = EXPERTS // PLANE
HEADS = 16
HEAD_SIZE = 64
BLOCK = 128
MOST_DOC = 256
MIB = 2**20
VMEM_ROOM = 60 * MIB
SMALL = pl.CostEstimate(flops=1, bytes_accessed=1, transcendentals=0)
epsilon = 1e-06
neg_large = -1000000000.0
BF = jnp.bfloat16
F32 = jnp.float32


def dot(a, b, ca, cb):
    return lax.dot_general(a, b, (((ca,), (cb,)), ((), ())), preferred_element_type=F32)

def rms_scale(values):
    return lax.rsqrt(jnp.mean(values * values, axis=-1, keepdims=True) + epsilon)

def swap_halves(u):
    lane = lax.broadcasted_iota(jnp.int32, u.shape, 1)
    return jnp.where(lane % 64 < 32, pltpu.roll(u, u.shape[1] - 32, 1), pltpu.roll(u, 32, 1))

def crossed(u, w):
    lane = lax.broadcasted_iota(jnp.int32, u.shape, 1)
    return (
        jnp.where(lane < 64, u, pltpu.roll(w, 64, 1)),
        jnp.where(lane < 64, pltpu.roll(u, 64, 1), w),
    )


def key_range(rows, qb):
    end = (qb + 1) * BLOCK
    return max(0, end - BLOCK - MOST_DOC), end

def fill_mask(mask_ref, seg_col_ref, seg_row_ref, rows):
    for qb in range(rows // BLOCK):
        low, high = key_range(rows, qb)
        keys = low + lax.broadcasted_iota(jnp.int32, (high - low, BLOCK), 0)
        queries = qb * BLOCK + lax.broadcasted_iota(jnp.int32, (high - low, BLOCK), 1)
        same = seg_col_ref[low:high, :1] == seg_row_ref[:1, qb * BLOCK : (qb + 1) * BLOCK]
        mask_ref[qb, : high - low] = jnp.where(same & (keys <= queries), 1.0, 0.0)

def masked_scores(mask_ref, k_c, q_pair, qb, span):
    s = dot(k_c, q_pair, 1, 1)
    m = mask_ref[qb, :span]
    return jnp.where(jnp.concatenate([m, m], axis=1) > 0, s, neg_large)

def piece_copies(me_ref, spots, pieces, whole_ref, sems, inward):
    copies = []
    for ref, (offsets, first) in zip(pieces, spots):
        if offsets is None:
            sides = [(ref, whole_ref)]
        else:
            share, cols = ref.shape[1:]
            sides = []
            for i, offset in enumerate(offsets):
                row = pl.multiple_of((me_ref[0] ^ offset) * share, share)
                sides.append((ref.at[i], whole_ref.at[pl.ds(row, share), first : first + cols]))
        for part, place in sides:
            source, target = (part, place) if inward else (place, part)
            copies.append(pltpu.make_async_copy(source, target, sems.at[len(copies)]))
    return copies


def spot_columns(spots):
    return [first if offsets else -1 for offsets, first in spots for _ in (offsets or [None])]


def piece_count(spots):
    return sum(1 if offsets is None else len(offsets) for offsets, _ in spots)


def forward_kernel(spots, me_ref, x_ref, routes_ref, seg_col_ref, seg_row_ref, cos_ref, sin_ref, *refs):
    pieces, refs = refs[: len(spots)], refs[len(spots) :]
    lse_ref, h2_ref, *outs = refs[:9]
    mask_ref, w_ref, h1_ref, q_ref, k_ref, v_ref, o_ref, r1_ref, sems, out_sems = refs[9:]

    def leave(i, source):
        copy = pltpu.make_async_copy(source, outs[i], out_sems.at[i])
        copy.start()
        return copy

    copies = piece_copies(me_ref, spots, pieces, w_ref, sems, True)
    for copy in copies:
        copy.start()
    fill_mask(mask_ref, seg_col_ref, seg_row_ref, x_ref.shape[0])
    for copy in copies:
        copy.wait()
    leaving = [leave(0, w_ref)]
    rows, width = x_ref.shape
    x = x_ref[...].astype(F32)
    gains = w_ref[:, 3072:3200].astype(F32).T
    h1_ref[...] = (x * rms_scale(x) * gains[16:17]).astype(BF)
    leaving.append(leave(1, h1_ref))

    @pl.loop(0, 4)
    def _(j):
        qs = pl.ds(pl.multiple_of(j * 256, 256), 256)
        ks = pl.ds(pl.multiple_of(j * 128, 128), 128)
        vs = pl.ds(pl.multiple_of(1536 + j * 128, 128), 128)
        kw = pl.ds(pl.multiple_of(1024 + j * 128, 128), 128)
        h1 = h1_ref[...]
        cos, sin = cos_ref[...], sin_ref[...]
        q2 = dot(h1, w_ref[:, qs], 1, 0)
        qa, qb_ = crossed(q2[:, :128], q2[:, 128:])
        qa = (qa * cos + swap_halves(qa) * sin).astype(BF) * BF(0.125)
        qb_ = (qb_ * cos + swap_halves(qb_) * sin).astype(BF) * BF(0.125)
        k = dot(h1, w_ref[:, kw], 1, 0)
        k = (k * cos + swap_halves(k) * sin).astype(BF)
        v32 = dot(h1, w_ref[:, vs], 1, 0)
        v = v32.astype(BF)
        q_ref[:, qs] = jnp.concatenate([qa, qb_], axis=1)
        k_ref[:, ks] = k
        v_ref[:, ks] = v
        vt = v32.T.astype(BF)
        lane = lax.broadcasted_iota(jnp.int32, (rows, 128), 1)
        sub = lax.broadcasted_iota(jnp.int32, (128, rows), 0)
        outs = []
        for qb in range(rows // BLOCK):
            low, high = key_range(rows, qb)
            blk = slice(qb * BLOCK, (qb + 1) * BLOCK)
            q_pair = jnp.concatenate([qa[blk], qb_[blk]], axis=0)
            total = None
            for c in range(2):
                k_c = jnp.where(lane[low:high] // 64 == c, k[low:high], BF(0))
                vt_c = jnp.where(sub[:, low:high] // 64 == c, vt[:, low:high], BF(0))
                s = masked_scores(mask_ref, k_c, q_pair, qb, high - low)
                top = jnp.max(s, axis=0, keepdims=True)
                e = jnp.exp(s - top)
                norm = jnp.sum(e, axis=0, keepdims=True)
                p = (e * (1.0 / norm)).astype(BF)
                part = dot(vt_c, p, 1, 0)
                total = part if total is None else total + part
                lse = top + jnp.log(norm)
                lse_ref[j, c : c + 1, blk] = lse[:, :128]
                lse_ref[j, 2 + c : 3 + c, blk] = lse[:, 128:]
            outs.append(total)
        a = jnp.concatenate([t[:, :128] for t in outs], axis=1).T
        b = jnp.concatenate([t[:, 128:] for t in outs], axis=1).T
        o_ref[:, qs] = jnp.concatenate(crossed(a, b), axis=1).astype(BF)

    leaving += [leave(i, ref) for i, ref in ((2, q_ref), (3, k_ref), (4, v_ref), (5, o_ref))]
    r1 = x_ref[...].astype(F32) + dot(o_ref[...], w_ref[:, 2048:3072], 1, 1)
    r1_ref[...] = r1
    leaving.append(leave(6, r1_ref))
    h2 = (r1 * rms_scale(r1) * gains[17:18]).astype(BF)
    h2_ref[:rows] = h2
    logits = dot(h2, w_ref[:, 3072:3200], 1, 0).T[:EXPERTS]
    at = lax.broadcasted_iota(jnp.int32, (EXPERTS, rows), 0)
    chosen = at < 0
    for t in range(routes_ref.shape[0]):
        chosen = chosen | (at == routes_ref[t : t + 1])
    logits = jnp.where(chosen, logits, neg_large)
    ex = jnp.where(chosen, jnp.exp(logits - jnp.max(logits, axis=0, keepdims=True)), 0.0)
    gates = ex / jnp.sum(ex, axis=0, keepdims=True)
    high = gates.astype(BF)
    low = (gates - high.astype(F32)).astype(BF)
    h2_ref[rows:] = jnp.concatenate([high, low], axis=1)
    for copy in leaving:
        copy.wait()

def forward_call(me, x, routes, seg_col, seg_row, cos, sin, pieces, spots):
    rows, width = x.shape
    s = jax.ShapeDtypeStruct
    vmem, anywhere = pl.BlockSpec(memory_space=pltpu.VMEM), pl.BlockSpec(memory_space=pl.ANY)
    return pl.pallas_call(
        functools.partial(forward_kernel, spots),
        in_specs=[pl.BlockSpec(memory_space=pltpu.SMEM)] + [vmem] * 6 + [anywhere] * len(pieces),
        out_specs=[vmem] * 2 + [anywhere] * 7,
        out_shape=[
            s((4, 4, rows), F32),
            s((rows + EXPERTS, width), BF),
            s((width, 3200), BF),
            s((rows, width), BF),
            s((rows, 1024), BF),
            s((rows, 512), BF),
            s((rows, 512), BF),
            s((rows, 1024), BF),
            s((rows, width), F32),
        ],
        scratch_shapes=[
            pltpu.VMEM((rows // BLOCK, BLOCK + MOST_DOC, BLOCK), F32),
            pltpu.VMEM((width, 3200), BF),
            pltpu.VMEM((rows, width), BF),
            pltpu.VMEM((rows, 1024), BF),
            pltpu.VMEM((rows, 512), BF),
            pltpu.VMEM((rows, 512), BF),
            pltpu.VMEM((rows, 1024), BF),
            pltpu.VMEM((rows, width), F32),
            pltpu.SemaphoreType.DMA((piece_count(spots),)),
            pltpu.SemaphoreType.DMA((7,)),
        ],
        cost_estimate=SMALL,
        compiler_params=pltpu.CompilerParams(vmem_limit_bytes=VMEM_ROOM),
    )(me, x, routes, seg_col, seg_row, cos, sin, *pieces)


ARRIVING = 14


def backward_kernel(spots, me_ref, *refs):
    given, refs = refs[:ARRIVING], refs[ARRIVING:]
    lse_ref, seg_col_ref, seg_row_ref, cos_ref, sin_ref, ig_ref = refs[:6]
    pieces, refs = refs[6 : 6 + len(spots)], refs[6 + len(spots) :]
    held, refs = refs[:ARRIVING], refs[ARRIVING:]
    mask_ref, do_ref, dqkv_ref, dr1_ref, wg_ref, sems, in_sems = refs
    p0, p1, p2, p3, r1_ref, cot_ref, h2_ref, w_ref, o_ref, q_ref, k_ref, v_ref, h1_ref, x_ref = held
    parts = [(given[i], held[i]) for i in range(7)]
    for cols in (slice(3072, 3200), slice(2048, 3072), slice(0, 2048)):
        parts.append((given[7].at[:, cols], w_ref.at[:, cols]))
        if cols.start == 2048:
            parts += [(given[i], held[i]) for i in range(8, 12)]
    parts += [(given[12], h1_ref), (given[13], x_ref)]
    copies = [pltpu.make_async_copy(source, target, in_sems.at[i]) for i, (source, target) in enumerate(parts)]
    for copy in copies:
        copy.start()
    fill_mask(mask_ref, seg_col_ref, seg_row_ref, r1_ref.shape[0])
    for copy in copies[:8]:
        copy.wait()
    rows, width = x_ref.shape
    misc = w_ref[:, 3072:3200]
    gains = misc.astype(F32).T

    def up(ref, sl):
        return ref[sl].astype(F32)

    top, tail = slice(0, rows), slice(rows, rows + EXPERTS)
    dh2 = up(p0, top) + up(p1, top) + up(p2, top) + up(p3, top)
    dg = up(p0, tail) + up(p1, tail) + up(p2, tail) + up(p3, tail)
    dg = dg[:, :rows] + dg[:, rows:]
    gates = up(h2_ref, tail)
    gates = gates[:, :rows] + gates[:, rows:]
    h2 = h2_ref[:rows]
    dlog = gates * (dg - jnp.sum(gates * dg, axis=0, keepdims=True))
    dlog = jnp.concatenate([dlog, jnp.zeros((128 - EXPERTS, rows), F32)], axis=0).T.astype(BF)
    dh2 = dh2 + dot(dlog, misc, 1, 1)
    r1 = r1_ref[...]
    s2 = rms_scale(r1)
    w2 = dh2 * gains[17:18]
    gain2_grad = jnp.sum(dh2 * r1 * s2, axis=0, keepdims=True)
    dr1 = cot_ref[...].astype(F32) + s2 * w2 - r1 * (s2 * s2 * s2) * jnp.mean(w2 * r1, axis=-1, keepdims=True)
    dr1_ref[...] = dr1
    dz = dr1.astype(BF)
    for copy in copies[8:13]:
        copy.wait()
    wg_ref[:, 2048:3072] = dot(dz, o_ref[...], 0, 0).astype(BF)
    do_ref[...] = dot(dz, w_ref[:, 2048:3072], 1, 0).astype(BF)
    router_t = dot(dlog, h2, 0, 0)

    @pl.loop(0, 4)
    def _(j):
        qs = pl.ds(pl.multiple_of(j * 256, 256), 256)
        ks = pl.ds(pl.multiple_of(j * 128, 128), 128)
        vs = pl.ds(pl.multiple_of(1536 + j * 128, 128), 128)
        kw = pl.ds(pl.multiple_of(1024 + j * 128, 128), 128)
        cos, sin = cos_ref[...], sin_ref[...]
        def back(g):
            return g * cos - swap_halves(g) * sin
        q, k, v = q_ref[:, qs], k_ref[:, ks], v_ref[:, ks]
        do = do_ref[:, qs].astype(F32)
        do = jnp.concatenate(crossed(do[:, :128], do[:, 128:]), axis=1).astype(BF)
        kt = k.astype(F32).T.astype(BF)
        lane = lax.broadcasted_iota(jnp.int32, (rows, 128), 1)
        sub = lax.broadcasted_iota(jnp.int32, (128, rows), 0)
        dks = [jnp.zeros((BLOCK, 128), F32) for _ in range(rows // BLOCK)]
        dvs = [jnp.zeros((BLOCK, 128), F32) for _ in range(rows // BLOCK)]
        dqs = []
        for qb in range(rows // BLOCK):
            low, high = key_range(rows, qb)
            blk = slice(qb * BLOCK, (qb + 1) * BLOCK)
            q_pair = jnp.concatenate([q[blk, :128], q[blk, 128:]], axis=0)
            do_pair = jnp.concatenate([do[blk, :128], do[blk, 128:]], axis=0)
            dq_t = None
            for c in range(2):
                mine = lane[low:high] // 64 == c
                k_c = jnp.where(mine, k[low:high], BF(0))
                v_c = jnp.where(mine, v[low:high], BF(0))
                kt_c = jnp.where(sub[:, low:high] // 64 == c, kt[:, low:high], BF(0))
                s = masked_scores(mask_ref, k_c, q_pair, qb, high - low)
                lse = jnp.concatenate([lse_ref[j, c : c + 1, blk], lse_ref[j, 2 + c : 3 + c, blk]], axis=1)
                p = jnp.exp(s - lse)
                dp = dot(v_c, do_pair, 1, 1)
                inner = jnp.sum(p * dp, axis=0, keepdims=True)
                ds = (p * (dp - inner)).astype(BF)
                dk = dot(ds, q_pair, 1, 0)
                dv = dot(p.astype(BF), do_pair, 1, 0)
                t = dot(kt_c, ds, 1, 0)
                dq_t = t if dq_t is None else dq_t + t
                for i, kb in enumerate(range(low // BLOCK, high // BLOCK)):
                    sl = slice(i * BLOCK, (i + 1) * BLOCK)
                    dks[kb] = dks[kb] + jnp.where(mine[sl], dk[sl], 0.0)
                    dvs[kb] = dvs[kb] + jnp.where(mine[sl], dv[sl], 0.0)
            dqs.append(dq_t)
        dqa = jnp.concatenate([t[:, :128] for t in dqs], axis=1).T * 0.125
        dqb = jnp.concatenate([t[:, 128:] for t in dqs], axis=1).T * 0.125
        dqkv_ref[:, qs] = jnp.concatenate(crossed(back(dqa), back(dqb)), axis=1).astype(BF)
        dqkv_ref[:, kw] = back(jnp.concatenate(dks, axis=0)).astype(BF)
        dqkv_ref[:, vs] = jnp.concatenate(dvs, axis=0).astype(BF)

    for copy in copies[13:]:
        copy.wait()
    leaving = piece_copies(me_ref, spots, pieces, wg_ref, sems, False)
    wg_ref[:, :1536] = dot(h1_ref[...], dqkv_ref[:, :1536], 0, 0).astype(BF)
    early = [i for i, first in enumerate(spot_columns(spots)) if first == 0]
    for i in early:
        leaving[i].start()
    wg_ref[:, 1536:2048] = dot(h1_ref[...], dqkv_ref[:, 1536:], 0, 0).astype(BF)
    dh1 = dot(dqkv_ref[...], w_ref[:, :2048], 1, 1)
    x = x_ref[...].astype(F32)
    s1 = rms_scale(x)
    w1 = dh1 * gains[16:17]
    gain1_grad = jnp.sum(dh1 * x * s1, axis=0, keepdims=True)
    at = lax.broadcasted_iota(jnp.int32, (128, width), 0)
    misc_t = jnp.where(at == 16, gain1_grad, jnp.where(at == 17, gain2_grad, router_t))
    wg_ref[:, 3072:3200] = misc_t.T.astype(BF)
    for i in range(len(leaving)):
        if i not in early:
            leaving[i].start()
    ig_ref[...] = dr1_ref[...] + s1 * w1 - x * (s1 * s1 * s1) * jnp.mean(w1 * x, axis=-1, keepdims=True)
    for copy in leaving:
        copy.wait()


def backward_call(me, parts, x, r1, cot, h1, h2, w, q, k, v, o, lse, seg_col, seg_row, cos, sin, piece_shapes, spots):
    rows, width = x.shape
    s = jax.ShapeDtypeStruct
    vmem, anywhere = pl.BlockSpec(memory_space=pltpu.VMEM), pl.BlockSpec(memory_space=pl.ANY)
    arriving = [*parts, r1, cot, h2, w, o, q, k, v, h1, x]
    return pl.pallas_call(
        functools.partial(backward_kernel, spots),
        in_specs=[pl.BlockSpec(memory_space=pltpu.SMEM)] + [anywhere] * ARRIVING + [vmem] * 5,
        out_specs=[vmem] + [anywhere] * len(spots),
        out_shape=[s((rows, width), F32)] + [s(shape, BF) for shape in piece_shapes],
        scratch_shapes=[pltpu.VMEM(a.shape, a.dtype) for a in arriving]
        + [
            pltpu.VMEM((rows // BLOCK, BLOCK + MOST_DOC, BLOCK), F32),
            pltpu.VMEM((rows, 1024), BF),
            pltpu.VMEM((rows, 2048), BF),
            pltpu.VMEM((rows, width), F32),
            pltpu.VMEM((width, 3200), BF),
            pltpu.SemaphoreType.DMA((piece_count(spots),)),
            pltpu.SemaphoreType.DMA((ARRIVING + 2,)),
        ],
        cost_estimate=SMALL,
        compiler_params=pltpu.CompilerParams(vmem_limit_bytes=VMEM_ROOM),
    )(me, *arriving, lse, seg_col, seg_row, cos, sin)


def expert_kernel(plan, count, place_ref, *refs):
    blocks = len(plan)
    arrays, refs = refs[:count], refs[count:]
    w_refs = refs[:6]
    refs = refs[-(8 + 2 * blocks + 6) :]
    ug0, ug1, da0, da1, db0, db1, h_all, g_all = refs[:8]
    backs, forths = refs[8 : 8 + blocks], refs[8 + blocks : 8 + 2 * blocks]
    h_buf, g_buf, back_buf, forth_buf, sems, out_sems = refs[8 + 2 * blocks :]
    rows = g_buf.shape[1]
    step = pl.program_id(0)
    slot = lax.rem(step, 2)

    def copies(i):
        found = []
        for buf, parts in ((h_buf, plan[i][0]), (g_buf, plan[i][1])):
            for array, start, size, at in parts:
                sem = sems.at[i % 2, len(found)]
                found.append(
                    pltpu.make_async_copy(
                        arrays[array].at[pl.ds(start, size)], buf.at[i % 2, pl.ds(at, size)], sem
                    )
                )
        return found

    def results(i):
        return (
            pltpu.make_async_copy(back_buf.at[i % 2], backs[i], out_sems.at[i % 2, 0]),
            pltpu.make_async_copy(forth_buf.at[i % 2], forths[i], out_sems.at[i % 2, 1]),
        )

    for i in range(blocks):

        @pl.when(step == i)
        def _(i=i):
            if i == 0:
                for copy in copies(0):
                    copy.start()
            if i + 1 < blocks:
                for copy in copies(i + 1):
                    copy.start()
            if i >= 2:
                for copy in results(i - 2):
                    copy.wait()
            for copy in copies(i):
                copy.wait()

    h = h_buf[slot, :rows]
    g = g_buf[slot]
    tail = h_buf[slot, rows:].astype(F32)
    tail = tail[:, :rows] + tail[:, rows:]
    gates = jnp.concatenate([tail, jnp.zeros((128 - EXPERTS, rows), F32)], axis=0).T
    h_all[...] = h
    g_all[...] = g
    place = place_ref[0]
    lane = lax.broadcasted_iota(jnp.int32, (rows, 128), 1)
    totals = []
    for e, (ug_ref, da_ref, db_ref) in enumerate(((ug0, da0, db0), (ug1, da1, db1))):
        wg_ref, wu_ref, wd_ref = w_refs[3 * e : 3 * e + 3]
        ff = wg_ref.shape[2]
        gate = jnp.sum(jnp.where(lane == place * MINE + e, gates, 0.0), axis=1, keepdims=True)
        total = 0.0
        for half in range(2):
            sl = slice(half * ff // 2, (half + 1) * ff // 2)
            a = dot(h, wg_ref[0, :, sl], 1, 0)
            b = dot(h, wu_ref[0, :, sl], 1, 0)
            gd = dot(g, wd_ref[0, :, sl], 1, 0)
            sigma = 1.0 / (1.0 + jnp.exp(-a))
            silu = a * sigma
            u = (silu * b).astype(BF).astype(F32)
            total = total + jnp.sum(u * gd, axis=1, keepdims=True)
            ug_ref[:, sl] = (u * gate).astype(BF)
            du = gd * gate
            db_ref[:, sl] = (du * silu).astype(BF)
            da_ref[:, sl] = (du * b * (sigma * (1.0 + a * (1.0 - sigma)))).astype(BF)
        totals.append(total)
    back = dot(da0[...], w_refs[0][0], 1, 1) + dot(db0[...], w_refs[1][0], 1, 1)
    back = back + dot(da1[...], w_refs[3][0], 1, 1) + dot(db1[...], w_refs[4][0], 1, 1)
    back_buf[slot, :rows] = back.astype(BF)
    forth = dot(ug0[...], w_refs[2][0], 1, 1) + dot(ug1[...], w_refs[5][0], 1, 1)
    forth_buf[slot] = forth.astype(BF)
    dg = jnp.where(lane == 0, totals[0], totals[1]).T
    at = lax.broadcasted_iota(jnp.int32, (EXPERTS, rows), 0)
    dg = jnp.where(at == place * MINE, dg[0:1], jnp.where(at == place * MINE + 1, dg[1:2], 0.0))
    high = dg.astype(BF)
    low = (dg - high.astype(F32)).astype(BF)
    back_buf[slot, rows:] = jnp.concatenate([high, low], axis=1)

    for i in range(blocks):

        @pl.when(step == i)
        def _(i=i):
            for copy in results(i):
                copy.start()
            if i == blocks - 1:
                for copy in (*results(i - 1), *results(i)):
                    copy.wait()


def expert_call(place, arrays, plan, weights):
    _, width, ff = weights.shape
    blocks = len(plan)
    rows = sum(piece[2] for piece in plan[0][1])
    most = max(len(h) + len(g) for h, g in plan)
    s = jax.ShapeDtypeStruct
    at = lambda i: (i, 0)
    anywhere = pl.BlockSpec(memory_space=pl.ANY)
    tile, hidden = pl.BlockSpec((rows, width), at), pl.BlockSpec((rows, ff), at)
    out = pl.pallas_call(
        functools.partial(expert_kernel, plan, len(arrays)),
        grid=(blocks,),
        in_specs=[pl.BlockSpec(memory_space=pltpu.SMEM)]
        + [anywhere] * len(arrays)
        + [pl.BlockSpec((1, width, ff), lambda i, k=k: (k, 0, 0), pipeline_mode=pl.Buffered(1)) for k in range(6)],
        out_specs=[hidden] * 6 + [tile] * 2 + [anywhere] * (2 * blocks),
        out_shape=[s((PLANE * rows, ff), BF)] * 6
        + [s((PLANE * rows, width), BF)] * 2
        + [s((rows + EXPERTS, width), BF)] * blocks
        + [s((rows, width), BF)] * blocks,
        scratch_shapes=[
            pltpu.VMEM((2, rows + EXPERTS, width), BF),
            pltpu.VMEM((2, rows, width), BF),
            pltpu.VMEM((2, rows + EXPERTS, width), BF),
            pltpu.VMEM((2, rows, width), BF),
            pltpu.SemaphoreType.DMA((2, most)),
            pltpu.SemaphoreType.DMA((2, 2)),
        ],
        cost_estimate=SMALL,
        compiler_params=pltpu.CompilerParams(vmem_limit_bytes=44 * MIB),
    )(place, *arrays, *[weights] * 6)
    return out[:8], out[8 : 8 + blocks], out[8 + blocks :]


STEPS = 4


def weight_grad_kernel(count, sums, sum_steps, left_ref, *refs):
    rights, refs = refs[:count], refs[count:]
    terms, refs = refs[: 2 * sums], refs[2 * sums :]
    out_ref, totals, acc_ref = refs[0], refs[1:-1], refs[-1]
    k = pl.program_id(0)
    ff = rights[0].shape[1]
    part = dot(left_ref[...], jnp.concatenate([r[...] for r in rights], axis=1), 0, 0)

    @pl.when(k < sum_steps)
    def _():
        for i in range(sums):
            totals[i][...] = (terms[2 * i][...].astype(F32) + terms[2 * i + 1][...].astype(F32)).astype(BF)

    @pl.when(k == 0)
    def _():
        acc_ref[...] = part

    @pl.when(k > 0)
    def _():
        acc_ref[...] += part

    @pl.when(k == STEPS - 1)
    def _():
        for t in range(count):
            out_ref[t] = acc_ref[:, t * ff : (t + 1) * ff].astype(BF)


def weight_grads(left, rights, pairs=()):
    total, width = left.shape
    ff = rights[0].shape[1]
    count = len(rights)
    step = total // STEPS
    row = lambda i: (i, 0)
    rows = pairs[0][0].shape[0] if pairs else 0
    sum_steps = next(n for n in (4, 3, 2, 1) if rows % (16 * n) == 0)
    tile = pl.BlockSpec((rows // sum_steps, width), lambda i: (jnp.minimum(i, sum_steps - 1), 0))
    s = jax.ShapeDtypeStruct
    out = pl.pallas_call(
        functools.partial(weight_grad_kernel, count, len(pairs), sum_steps),
        grid=(STEPS,),
        in_specs=[pl.BlockSpec((step, width), row)]
        + [pl.BlockSpec((step, ff), row)] * count
        + [tile] * (2 * len(pairs)),
        out_specs=[pl.BlockSpec((count, width, ff), lambda i: (0, 0, 0), pipeline_mode=pl.Buffered(1))]
        + [tile] * len(pairs),
        out_shape=[s((count, width, ff), BF)] + [s((rows, width), BF)] * len(pairs),
        scratch_shapes=[pltpu.VMEM((width, count * ff), F32)],
        cost_estimate=SMALL,
        compiler_params=pltpu.CompilerParams(vmem_limit_bytes=VMEM_ROOM),
    )(left, *rights, *[term for pair in pairs for term in pair])
    return out[0], out[1:]


def up(v):
    return v.astype(F32)


def after(value, *others):
    return lax.optimization_barrier((value, *others))[0]


CUT = 1536
COLUMNS = 3200


def make_local(n):
    outer = n // PLANE
    plane_groups = [[PLANE * z + i for i in range(PLANE)] for z in range(outer)]
    outer_groups = [[PLANE * z + i for z in range(outer)] for i in range(PLANE)]
    pieced = outer == 4

    def swap(array, offset):
        return lax.ppermute(array, "dp", [(i, i ^ offset) for i in range(n)])

    along_z = [PLANE * k for k in range(4)]

    def dense_gather(part, *earlier):
        if not pieced:
            return [lax.all_gather(part, "dp", axis=0, tiled=True)], [(None, 0)]
        line = after([part] + [swap(part, k) for k in along_z[1:]], *earlier)
        left, right = jnp.stack([t[:, :CUT] for t in line]), jnp.stack([t[:, CUT:] for t in line])
        left_x, right_y = swap(left, 2), swap(right, 4)
        left_y, right_x = swap(left, 4), swap(right, 2)
        left_xy, right_xy = swap(left_x, 4), swap(right_y, 2)
        found = [(left, 0, 0), (left_x, 2, 0), (left_y, 4, 0), (left_xy, 6, 0)]
        found += [(right, 0, CUT), (right_x, 2, CUT), (right_y, 4, CUT), (right_xy, 6, CUT)]
        found += [(swap(piece, 1), offset + 1, first) for piece, offset, first in found]
        return [f[0] for f in found], [([f[1] + k for k in along_z], f[2]) for f in found]

    def grad_spots(share):
        if not pieced:
            return [(n * share, COLUMNS)], [(None, 0)]
        shapes, spots = [], []
        for core in (1, 0):
            for major, minor, first, cols in ((2, 4, 0, CUT), (4, 2, CUT, COLUMNS - CUT)):
                for far in (0, major):
                    shapes.append((8, share, cols))
                    spots.append(([core + far + d + k for d in (0, minor) for k in along_z], first))
        return shapes, spots

    def dense_sum(pieces, earlier):
        if not pieced:
            return up(lax.psum_scatter(pieces[0], "dp", scatter_dimension=0, tiled=True))

        def add(a, b):
            return (up(a) + up(b)).astype(BF)

        near_l, far_l, near_r, far_r = (add(keep, swap(sent, 1)) for sent, keep in zip(pieces[:4], pieces[4:]))
        far_l, far_r = after((far_l, far_r), earlier)
        got_l, got_r = swap(far_l, 2), swap(far_r, 4)
        sent_l, sent_r = add(near_l[4:], got_l[4:]), add(near_r[4:], got_r[4:])
        left = add(add(near_l[:4], got_l[:4]), swap(sent_l, 4))
        right = add(add(near_r[:4], got_r[:4]), swap(sent_r, 2))
        both = jnp.concatenate([left, right], axis=2)
        total = up(both[0])
        for k in range(1, 4):
            total = total + up(swap(both[k], PLANE * k))
        return total

    def both_cores(same_core):
        return [b for part in same_core for b in (part, swap(part, 1))]

    def local(
        tokens,
        query_weight,
        key_projection_weight,
        value_projection_weight,
        output_weight,
        first_gain,
        second_gain,
        router_weight,
        gate_weight,
        up_weight,
        down_weight,
        routes,
        segments,
        cotangent,
    ):
        rows, width = tokens.shape
        ff = gate_weight.shape[2]
        share = query_weight.shape[0]
        me = lax.axis_index("dp").astype(jnp.int32).reshape(1)
        place = lax.rem(me, PLANE)

        expert_part = jnp.stack(
            [w.reshape(PLANE, MINE, share, ff) for w in (gate_weight, up_weight, down_weight.transpose(0, 2, 1))],
            axis=2,
        )
        dense_part = jnp.concatenate(
            [
                query_weight,
                key_projection_weight,
                value_projection_weight,
                output_weight.T,
                router_weight,
                first_gain[:, None],
                second_gain[:, None],
                jnp.zeros((share, 128 - EXPERTS - 2), BF),
            ],
            axis=1,
        )
        dense_part = after(dense_part, expert_part)
        expert_part = lax.all_to_all(
            expert_part, "dp", split_axis=0, concat_axis=0, axis_index_groups=plane_groups
        )

        expert_part = expert_part.transpose(1, 2, 0, 3, 4).reshape(3 * MINE, PLANE * share, ff)
        weights = lax.all_gather(expert_part, "dp", axis=1, tiled=True, axis_index_groups=outer_groups)

        positions = jnp.arange(rows, dtype=F32)
        frequency = 10000.0 ** (-2.0 * jnp.arange(HEAD_SIZE // 2, dtype=F32) / HEAD_SIZE)
        angles = positions[:, None] * frequency[None, :]
        cosine, sine = jnp.cos(angles), jnp.sin(angles)
        cosine = jnp.concatenate([cosine] * 4, axis=1)
        sine = jnp.concatenate([-sine, sine, -sine, sine], axis=1)
        seg_col = segments.reshape(rows, 1)
        seg_row = segments.reshape(1, rows)

        half = rows // 2
        pieces, spots = dense_gather(dense_part, cosine, sine, seg_col, expert_part)
        late = after(cotangent, *pieces)
        cot_x, cot_y = swap(late, 2), swap(late, 4)

        lse, h2, dense, h1, q, k, v, o, r1 = forward_call(
            me, tokens, routes.T, seg_col, seg_row, cosine, sine, pieces, spots
        )
        h2 = after(h2, cot_x, cot_y)
        h2_x, h2_y, h2_core = swap(h2, 2), swap(h2, 4), swap(h2, 1)
        cot_core = swap(cotangent, 1)
        h2_x, h2_y, cot_x, cot_y = after((h2_x, h2_y, cot_x, cot_y), h2_core, cot_core)
        corner_x = swap(jnp.concatenate([h2_y[:half], cot_y[:half]], axis=0), 2)
        corner_y = swap(jnp.concatenate([h2_x[half:], cot_x[half:]], axis=0), 4)
        cores = [swap(t, 1) for t in (h2_x, cot_x, h2_y, cot_y)]
        corner_x, corner_y = after((corner_x, corner_y), *cores)
        long = rows + EXPERTS

        def pieces_of(h, g):
            return ([(h, 0, long, 0)], [(g, 0, rows, 0)])

        first_arrays = [corner_x, swap(corner_x, 1), corner_y, swap(corner_y, 1), h2_x, cores[0], cot_x, cores[1]]
        first_plan = [
            (
                [(i, 0, half, 0), (i + 2, 0, long - half, half)],
                [(i, half, half, 0), (i + 2, long - half, half, half)],
            )
            for i in range(2)
        ]
        first_plan += [pieces_of(i, 2 + i) for i in (4, 5)]
        second_arrays = [h2, h2_core, h2_y, cores[2], cotangent, cot_core, cot_y, cores[3]]
        second_plan = [pieces_of(8 + i, 12 + i) for i in range(4)]

        def outer_sum(grads):
            return lax.psum_scatter(grads, "dp", scatter_dimension=1, tiled=True, axis_index_groups=outer_groups)

        def with_core(block, other):
            return (up(block) + up(other)).astype(BF)

        def together(*values):
            return lax.optimization_barrier(values)

        top, low = slice(0, half), slice(half, None)

        kept, back, out = expert_call(place, first_arrays + second_arrays, first_plan + second_plan, weights)
        core_xy, core_x, core_y = swap(back[1], 1), swap(back[3], 1), swap(back[7], 1)
        sum_xy = [with_core(back[0][part], core_xy[part]) for part in (top, low)]
        sum_xy, core_x, core_y, kept, back, out = together(sum_xy, core_x, core_y, kept, back, out)

        ug0, ug1, da0, da1, db0, db1, tokens_all, grads_all = kept
        grads_d, (sum_x, sum_y) = weight_grads(grads_all, [ug0, ug1], [(back[2], core_x), (back[6], core_y)])
        via_x, via_y, out_core = swap(sum_xy[0], 2), swap(sum_xy[1], 4), [swap(out[i], 1) for i in (1, 3, 7)]
        grads_d, sum_x, sum_y, via_x, via_y, out_core, kept, out, back = together(
            grads_d, sum_x, sum_y, via_x, via_y, out_core, kept, out, back
        )
        sums_d = outer_sum(grads_d)
        sum_y = jnp.concatenate([with_core(sum_y[top], via_x), sum_y[low]], axis=0)
        sum_x = jnp.concatenate([sum_x[top], with_core(sum_x[low], via_y)], axis=0)
        sum_x, sum_y, kept, back, out, out_core = together(sum_x, sum_y, kept, back, out, out_core)

        _, _, da0, da1, db0, db1, tokens_all, _ = kept
        grads_gu, (out_xy, out_x, out_y) = weight_grads(
            tokens_all,
            [da0, da1, db0, db1],
            [(out[0], out_core[0]), (out[2], out_core[1]), (out[6], out_core[2])],
        )
        got_x, got_y, core_own, out_core_own = swap(sum_x, 2), swap(sum_y, 4), swap(back[5], 1), swap(out[5], 1)
        grads_gu, got_x, got_y, core_own, out_core_own, out_xy, out_x, out_y = together(
            grads_gu, got_x, got_y, core_own, out_core_own, out_xy, out_x, out_y
        )
        sums_gu = outer_sum(grads_gu)
        got = [back[4], core_own, got_x, got_y]
        got, out_x, out_y, out_xy = together(got, out_x, out_y, [out_xy[top], out_xy[low]])

        shapes, grad_places = grad_spots(share)
        input_grad, *grad_pieces = backward_call(
            me, got, tokens, r1, cotangent, h1, h2, dense, q, k, v, o, lse, seg_col, seg_row, cosine, sine,
            shapes, grad_places,
        )
        got_out = [swap(out_x, 2), swap(out_y, 4), swap(out_xy[0], 6)]
        input_grad, grad_pieces, got_out, out_xy = together(input_grad, grad_pieces, got_out, out_xy)
        got_out_low = swap(out_xy[1], 6)
        output = r1 + up(out[4]) + up(out_core_own) + up(got_out[0]) + up(got_out[1])
        output_top, output_low = (output[top] + up(got_out[2])).astype(BF), output[low]
        owned = jnp.concatenate([sums_d, sums_gu], axis=0).reshape(3 * MINE, PLANE, share, ff).transpose(1, 0, 2, 3)
        dense_grads = dense_sum(grad_pieces, (got_out_low, output_top, output_low))
        output = jnp.concatenate([output_top, (output_low + up(got_out_low)).astype(BF)], axis=0)
        owned = lax.all_to_all(owned, "dp", split_axis=0, concat_axis=0, axis_index_groups=plane_groups)

        def experts_of(kind):
            return up(owned[:, MINE * kind : MINE * (kind + 1)]).reshape(EXPERTS, share, ff)

        down_out, gate_out, up_out = experts_of(0).transpose(0, 2, 1), experts_of(1), experts_of(2)
        return (
            output,
            input_grad,
            dense_grads[:, :1024],
            dense_grads[:, 1024:1536],
            dense_grads[:, 1536:2048],
            dense_grads[:, 2048:3072].T,
            dense_grads[:, 3072 + EXPERTS],
            dense_grads[:, 3073 + EXPERTS],
            dense_grads[:, 3072 : 3072 + EXPERTS],
            gate_out,
            up_out,
            down_out,
        )

    return local


def solution(mesh):
    row, col, one = P("dp", None), P(None, "dp"), P("dp")
    middle, last = P(None, "dp", None), P(None, None, "dp")
    in_specs = (row, row, row, row, col, one, one, row, middle, middle, last, row, row, row)
    out_specs = (row, row, row, row, row, col, one, one, row, middle, middle, last)
    return jax.shard_map(
        make_local(mesh.shape["dp"]), mesh=mesh, in_specs=in_specs, out_specs=out_specs, check_vma=False
    )
```

```python
import functools

import jax
import jax.numpy as jnp
from jax import lax
from jax.experimental import pallas as pl
from jax.experimental.pallas import tpu as pltpu
from jax.sharding import PartitionSpec as P

EXPERTS = 16
PLANE = 8
MINE = EXPERTS // PLANE
HEADS = 16
HEAD_SIZE = 64
BLOCK = 128
MOST_DOC = 256
MIB = 2**20
VMEM_ROOM = 60 * MIB
SMALL = pl.CostEstimate(flops=1, bytes_accessed=1, transcendentals=0)
epsilon = 1e-06
neg_large = -1000000000.0
BF = jnp.bfloat16
F32 = jnp.float32


def dot(a, b, ca, cb):
    return lax.dot_general(a, b, (((ca,), (cb,)), ((), ())), preferred_element_type=F32)

def rms_scale(values):
    return lax.rsqrt(jnp.mean(values * values, axis=-1, keepdims=True) + epsilon)

def swap_halves(u):
    lane = lax.broadcasted_iota(jnp.int32, u.shape, 1)
    return jnp.where(lane % 64 < 32, pltpu.roll(u, u.shape[1] - 32, 1), pltpu.roll(u, 32, 1))

def crossed(u, w):
    lane = lax.broadcasted_iota(jnp.int32, u.shape, 1)
    return (
        jnp.where(lane < 64, u, pltpu.roll(w, 64, 1)),
        jnp.where(lane < 64, pltpu.roll(u, 64, 1), w),
    )


def key_range(rows, qb):
    end = (qb + 1) * BLOCK
    return max(0, end - BLOCK - MOST_DOC), end

def fill_mask(mask_ref, seg_col_ref, seg_row_ref, rows):
    for qb in range(rows // BLOCK):
        low, high = key_range(rows, qb)
        keys = low + lax.broadcasted_iota(jnp.int32, (high - low, BLOCK), 0)
        queries = qb * BLOCK + lax.broadcasted_iota(jnp.int32, (high - low, BLOCK), 1)
        same = seg_col_ref[low:high, :1] == seg_row_ref[:1, qb * BLOCK : (qb + 1) * BLOCK]
        mask_ref[qb, : high - low] = jnp.where(same & (keys <= queries), 1.0, 0.0)

def masked_scores(mask_ref, k_c, q_pair, qb, span):
    s = dot(k_c, q_pair, 1, 1)
    m = mask_ref[qb, :span]
    return jnp.where(jnp.concatenate([m, m], axis=1) > 0, s, neg_large)

def piece_copies(me_ref, spots, pieces, whole_ref, sems, inward):
    copies = []
    for ref, (offsets, first) in zip(pieces, spots):
        if offsets is None:
            sides = [(ref, whole_ref)]
        else:
            share, cols = ref.shape[1:]
            sides = []
            for i, offset in enumerate(offsets):
                row = pl.multiple_of((me_ref[0] ^ offset) * share, share)
                sides.append((ref.at[i], whole_ref.at[pl.ds(row, share), first : first + cols]))
        for part, place in sides:
            source, target = (part, place) if inward else (place, part)
            copies.append(pltpu.make_async_copy(source, target, sems.at[len(copies)]))
    return copies


def spot_columns(spots):
    return [first if offsets else -1 for offsets, first in spots for _ in (offsets or [None])]


def piece_count(spots):
    return sum(1 if offsets is None else len(offsets) for offsets, _ in spots)


def forward_kernel(spots, me_ref, x_ref, routes_ref, seg_col_ref, seg_row_ref, cos_ref, sin_ref, *refs):
    pieces, refs = refs[: len(spots)], refs[len(spots) :]
    lse_ref, h2_ref, *outs = refs[:9]
    mask_ref, w_ref, h1_ref, q_ref, k_ref, v_ref, o_ref, r1_ref, sems, out_sems = refs[9:]

    def leave(i, source):
        copy = pltpu.make_async_copy(source, outs[i], out_sems.at[i])
        copy.start()
        return copy

    copies = piece_copies(me_ref, spots, pieces, w_ref, sems, True)
    for copy in copies:
        copy.start()
    fill_mask(mask_ref, seg_col_ref, seg_row_ref, x_ref.shape[0])
    for copy in copies:
        copy.wait()
    leaving = [leave(0, w_ref)]
    rows, width = x_ref.shape
    x = x_ref[...].astype(F32)
    gains = w_ref[:, 3072:3200].astype(F32).T
    h1_ref[...] = (x * rms_scale(x) * gains[16:17]).astype(BF)
    leaving.append(leave(1, h1_ref))

    @pl.loop(0, 4)
    def _(j):
        qs = pl.ds(pl.multiple_of(j * 256, 256), 256)
        ks = pl.ds(pl.multiple_of(j * 128, 128), 128)
        vs = pl.ds(pl.multiple_of(1536 + j * 128, 128), 128)
        kw = pl.ds(pl.multiple_of(1024 + j * 128, 128), 128)
        h1 = h1_ref[...]
        cos, sin = cos_ref[...], sin_ref[...]
        q2 = dot(h1, w_ref[:, qs], 1, 0)
        qa, qb_ = crossed(q2[:, :128], q2[:, 128:])
        qa = (qa * cos + swap_halves(qa) * sin).astype(BF) * BF(0.125)
        qb_ = (qb_ * cos + swap_halves(qb_) * sin).astype(BF) * BF(0.125)
        k = dot(h1, w_ref[:, kw], 1, 0)
        k = (k * cos + swap_halves(k) * sin).astype(BF)
        v32 = dot(h1, w_ref[:, vs], 1, 0)
        v = v32.astype(BF)
        q_ref[:, qs] = jnp.concatenate([qa, qb_], axis=1)
        k_ref[:, ks] = k
        v_ref[:, ks] = v
        vt = v32.T.astype(BF)
        lane = lax.broadcasted_iota(jnp.int32, (rows, 128), 1)
        sub = lax.broadcasted_iota(jnp.int32, (128, rows), 0)
        outs = []
        for qb in range(rows // BLOCK):
            low, high = key_range(rows, qb)
            blk = slice(qb * BLOCK, (qb + 1) * BLOCK)
            q_pair = jnp.concatenate([qa[blk], qb_[blk]], axis=0)
            total = None
            for c in range(2):
                k_c = jnp.where(lane[low:high] // 64 == c, k[low:high], BF(0))
                vt_c = jnp.where(sub[:, low:high] // 64 == c, vt[:, low:high], BF(0))
                s = masked_scores(mask_ref, k_c, q_pair, qb, high - low)
                top = jnp.max(s, axis=0, keepdims=True)
                e = jnp.exp(s - top)
                norm = jnp.sum(e, axis=0, keepdims=True)
                p = (e * (1.0 / norm)).astype(BF)
                part = dot(vt_c, p, 1, 0)
                total = part if total is None else total + part
                lse = top + jnp.log(norm)
                lse_ref[j, c : c + 1, blk] = lse[:, :128]
                lse_ref[j, 2 + c : 3 + c, blk] = lse[:, 128:]
            outs.append(total)
        a = jnp.concatenate([t[:, :128] for t in outs], axis=1).T
        b = jnp.concatenate([t[:, 128:] for t in outs], axis=1).T
        o_ref[:, qs] = jnp.concatenate(crossed(a, b), axis=1).astype(BF)

    leaving += [leave(i, ref) for i, ref in ((2, q_ref), (3, k_ref), (4, v_ref), (5, o_ref))]
    r1 = x_ref[...].astype(F32) + dot(o_ref[...], w_ref[:, 2048:3072], 1, 1)
    r1_ref[...] = r1
    leaving.append(leave(6, r1_ref))
    h2 = (r1 * rms_scale(r1) * gains[17:18]).astype(BF)
    h2_ref[:rows] = h2
    logits = dot(h2, w_ref[:, 3072:3200], 1, 0).T[:EXPERTS]
    at = lax.broadcasted_iota(jnp.int32, (EXPERTS, rows), 0)
    chosen = at < 0
    for t in range(routes_ref.shape[0]):
        chosen = chosen | (at == routes_ref[t : t + 1])
    logits = jnp.where(chosen, logits, neg_large)
    ex = jnp.where(chosen, jnp.exp(logits - jnp.max(logits, axis=0, keepdims=True)), 0.0)
    gates = ex / jnp.sum(ex, axis=0, keepdims=True)
    high = gates.astype(BF)
    low = (gates - high.astype(F32)).astype(BF)
    h2_ref[rows:] = jnp.concatenate([high, low], axis=1)
    for copy in leaving:
        copy.wait()

def forward_call(me, x, routes, seg_col, seg_row, cos, sin, pieces, spots):
    rows, width = x.shape
    s = jax.ShapeDtypeStruct
    vmem, anywhere = pl.BlockSpec(memory_space=pltpu.VMEM), pl.BlockSpec(memory_space=pl.ANY)
    return pl.pallas_call(
        functools.partial(forward_kernel, spots),
        in_specs=[pl.BlockSpec(memory_space=pltpu.SMEM)] + [vmem] * 6 + [anywhere] * len(pieces),
        out_specs=[vmem] * 2 + [anywhere] * 7,
        out_shape=[
            s((4, 4, rows), F32),
            s((rows + EXPERTS, width), BF),
            s((width, 3200), BF),
            s((rows, width), BF),
            s((rows, 1024), BF),
            s((rows, 512), BF),
            s((rows, 512), BF),
            s((rows, 1024), BF),
            s((rows, width), F32),
        ],
        scratch_shapes=[
            pltpu.VMEM((rows // BLOCK, BLOCK + MOST_DOC, BLOCK), F32),
            pltpu.VMEM((width, 3200), BF),
            pltpu.VMEM((rows, width), BF),
            pltpu.VMEM((rows, 1024), BF),
            pltpu.VMEM((rows, 512), BF),
            pltpu.VMEM((rows, 512), BF),
            pltpu.VMEM((rows, 1024), BF),
            pltpu.VMEM((rows, width), F32),
            pltpu.SemaphoreType.DMA((piece_count(spots),)),
            pltpu.SemaphoreType.DMA((7,)),
        ],
        cost_estimate=SMALL,
        compiler_params=pltpu.CompilerParams(vmem_limit_bytes=VMEM_ROOM),
    )(me, x, routes, seg_col, seg_row, cos, sin, *pieces)


ARRIVING = 14


def backward_kernel(spots, me_ref, *refs):
    given, refs = refs[:ARRIVING], refs[ARRIVING:]
    lse_ref, seg_col_ref, seg_row_ref, cos_ref, sin_ref, ig_ref = refs[:6]
    pieces, refs = refs[6 : 6 + len(spots)], refs[6 + len(spots) :]
    held, refs = refs[:ARRIVING], refs[ARRIVING:]
    mask_ref, do_ref, dqkv_ref, dr1_ref, wg_ref, sems, in_sems = refs
    p0, p1, p2, p3, r1_ref, cot_ref, h2_ref, w_ref, o_ref, q_ref, k_ref, v_ref, h1_ref, x_ref = held
    parts = [(given[i], held[i]) for i in range(7)]
    for cols in (slice(3072, 3200), slice(2048, 3072), slice(0, 2048)):
        parts.append((given[7].at[:, cols], w_ref.at[:, cols]))
        if cols.start == 2048:
            parts += [(given[i], held[i]) for i in range(8, 12)]
    parts += [(given[12], h1_ref), (given[13], x_ref)]
    copies = [pltpu.make_async_copy(source, target, in_sems.at[i]) for i, (source, target) in enumerate(parts)]
    for copy in copies:
        copy.start()
    fill_mask(mask_ref, seg_col_ref, seg_row_ref, r1_ref.shape[0])
    for copy in copies[:8]:
        copy.wait()
    rows, width = x_ref.shape
    misc = w_ref[:, 3072:3200]
    gains = misc.astype(F32).T

    def up(ref, sl):
        return ref[sl].astype(F32)

    top, tail = slice(0, rows), slice(rows, rows + EXPERTS)
    dh2 = up(p0, top) + up(p1, top) + up(p2, top) + up(p3, top)
    dg = up(p0, tail) + up(p1, tail) + up(p2, tail) + up(p3, tail)
    dg = dg[:, :rows] + dg[:, rows:]
    gates = up(h2_ref, tail)
    gates = gates[:, :rows] + gates[:, rows:]
    h2 = h2_ref[:rows]
    dlog = gates * (dg - jnp.sum(gates * dg, axis=0, keepdims=True))
    dlog = jnp.concatenate([dlog, jnp.zeros((128 - EXPERTS, rows), F32)], axis=0).T.astype(BF)
    dh2 = dh2 + dot(dlog, misc, 1, 1)
    r1 = r1_ref[...]
    s2 = rms_scale(r1)
    w2 = dh2 * gains[17:18]
    gain2_grad = jnp.sum(dh2 * r1 * s2, axis=0, keepdims=True)
    dr1 = cot_ref[...].astype(F32) + s2 * w2 - r1 * (s2 * s2 * s2) * jnp.mean(w2 * r1, axis=-1, keepdims=True)
    dr1_ref[...] = dr1
    dz = dr1.astype(BF)
    for copy in copies[8:13]:
        copy.wait()
    wg_ref[:, 2048:3072] = dot(dz, o_ref[...], 0, 0).astype(BF)
    do_ref[...] = dot(dz, w_ref[:, 2048:3072], 1, 0).astype(BF)
    router_t = dot(dlog, h2, 0, 0)

    @pl.loop(0, 4)
    def _(j):
        qs = pl.ds(pl.multiple_of(j * 256, 256), 256)
        ks = pl.ds(pl.multiple_of(j * 128, 128), 128)
        vs = pl.ds(pl.multiple_of(1536 + j * 128, 128), 128)
        kw = pl.ds(pl.multiple_of(1024 + j * 128, 128), 128)
        cos, sin = cos_ref[...], sin_ref[...]
        def back(g):
            return g * cos - swap_halves(g) * sin
        q, k, v = q_ref[:, qs], k_ref[:, ks], v_ref[:, ks]
        do = do_ref[:, qs].astype(F32)
        do = jnp.concatenate(crossed(do[:, :128], do[:, 128:]), axis=1).astype(BF)
        kt = k.astype(F32).T.astype(BF)
        lane = lax.broadcasted_iota(jnp.int32, (rows, 128), 1)
        sub = lax.broadcasted_iota(jnp.int32, (128, rows), 0)
        dks = [jnp.zeros((BLOCK, 128), F32) for _ in range(rows // BLOCK)]
        dvs = [jnp.zeros((BLOCK, 128), F32) for _ in range(rows // BLOCK)]
        dqs = []
        for qb in range(rows // BLOCK):
            low, high = key_range(rows, qb)
            blk = slice(qb * BLOCK, (qb + 1) * BLOCK)
            q_pair = jnp.concatenate([q[blk, :128], q[blk, 128:]], axis=0)
            do_pair = jnp.concatenate([do[blk, :128], do[blk, 128:]], axis=0)
            dq_t = None
            for c in range(2):
                mine = lane[low:high] // 64 == c
                k_c = jnp.where(mine, k[low:high], BF(0))
                v_c = jnp.where(mine, v[low:high], BF(0))
                kt_c = jnp.where(sub[:, low:high] // 64 == c, kt[:, low:high], BF(0))
                s = masked_scores(mask_ref, k_c, q_pair, qb, high - low)
                lse = jnp.concatenate([lse_ref[j, c : c + 1, blk], lse_ref[j, 2 + c : 3 + c, blk]], axis=1)
                p = jnp.exp(s - lse)
                dp = dot(v_c, do_pair, 1, 1)
                inner = jnp.sum(p * dp, axis=0, keepdims=True)
                ds = (p * (dp - inner)).astype(BF)
                dk = dot(ds, q_pair, 1, 0)
                dv = dot(p.astype(BF), do_pair, 1, 0)
                t = dot(kt_c, ds, 1, 0)
                dq_t = t if dq_t is None else dq_t + t
                for i, kb in enumerate(range(low // BLOCK, high // BLOCK)):
                    sl = slice(i * BLOCK, (i + 1) * BLOCK)
                    dks[kb] = dks[kb] + jnp.where(mine[sl], dk[sl], 0.0)
                    dvs[kb] = dvs[kb] + jnp.where(mine[sl], dv[sl], 0.0)
            dqs.append(dq_t)
        dqa = jnp.concatenate([t[:, :128] for t in dqs], axis=1).T * 0.125
        dqb = jnp.concatenate([t[:, 128:] for t in dqs], axis=1).T * 0.125
        dqkv_ref[:, qs] = jnp.concatenate(crossed(back(dqa), back(dqb)), axis=1).astype(BF)
        dqkv_ref[:, kw] = back(jnp.concatenate(dks, axis=0)).astype(BF)
        dqkv_ref[:, vs] = jnp.concatenate(dvs, axis=0).astype(BF)

    for copy in copies[13:]:
        copy.wait()
    leaving = piece_copies(me_ref, spots, pieces, wg_ref, sems, False)
    wg_ref[:, :1536] = dot(h1_ref[...], dqkv_ref[:, :1536], 0, 0).astype(BF)
    early = [i for i, first in enumerate(spot_columns(spots)) if first == 0]
    for i in early:
        leaving[i].start()
    wg_ref[:, 1536:2048] = dot(h1_ref[...], dqkv_ref[:, 1536:], 0, 0).astype(BF)
    dh1 = dot(dqkv_ref[...], w_ref[:, :2048], 1, 1)
    x = x_ref[...].astype(F32)
    s1 = rms_scale(x)
    w1 = dh1 * gains[16:17]
    gain1_grad = jnp.sum(dh1 * x * s1, axis=0, keepdims=True)
    at = lax.broadcasted_iota(jnp.int32, (128, width), 0)
    misc_t = jnp.where(at == 16, gain1_grad, jnp.where(at == 17, gain2_grad, router_t))
    wg_ref[:, 3072:3200] = misc_t.T.astype(BF)
    for i in range(len(leaving)):
        if i not in early:
            leaving[i].start()
    ig_ref[...] = dr1_ref[...] + s1 * w1 - x * (s1 * s1 * s1) * jnp.mean(w1 * x, axis=-1, keepdims=True)
    for copy in leaving:
        copy.wait()


def backward_call(me, parts, x, r1, cot, h1, h2, w, q, k, v, o, lse, seg_col, seg_row, cos, sin, piece_shapes, spots):
    rows, width = x.shape
    s = jax.ShapeDtypeStruct
    vmem, anywhere = pl.BlockSpec(memory_space=pltpu.VMEM), pl.BlockSpec(memory_space=pl.ANY)
    arriving = [*parts, r1, cot, h2, w, o, q, k, v, h1, x]
    return pl.pallas_call(
        functools.partial(backward_kernel, spots),
        in_specs=[pl.BlockSpec(memory_space=pltpu.SMEM)] + [anywhere] * ARRIVING + [vmem] * 5,
        out_specs=[vmem] + [anywhere] * len(spots),
        out_shape=[s((rows, width), F32)] + [s(shape, BF) for shape in piece_shapes],
        scratch_shapes=[pltpu.VMEM(a.shape, a.dtype) for a in arriving]
        + [
            pltpu.VMEM((rows // BLOCK, BLOCK + MOST_DOC, BLOCK), F32),
            pltpu.VMEM((rows, 1024), BF),
            pltpu.VMEM((rows, 2048), BF),
            pltpu.VMEM((rows, width), F32),
            pltpu.VMEM((width, 3200), BF),
            pltpu.SemaphoreType.DMA((piece_count(spots),)),
            pltpu.SemaphoreType.DMA((ARRIVING + 2,)),
        ],
        cost_estimate=SMALL,
        compiler_params=pltpu.CompilerParams(vmem_limit_bytes=VMEM_ROOM),
    )(me, *arriving, lse, seg_col, seg_row, cos, sin)


def expert_kernel(plan, count, place_ref, *refs):
    blocks = len(plan)
    arrays, refs = refs[:count], refs[count:]
    w_refs = refs[:6]
    ug0, ug1, da0, da1, db0, db1 = refs[6:12]
    backs, forths = refs[12 : 12 + blocks], refs[12 + blocks : 12 + 2 * blocks]
    h_buf, g_buf, back_buf, forth_buf, gates_buf, dg_buf, sems, out_sems = refs[12 + 2 * blocks :]
    rows = g_buf.shape[1]
    step = pl.program_id(0)
    slot = lax.rem(step, 2)

    def copies(i):
        found = []
        for buf, parts in ((h_buf, plan[i][0]), (g_buf, plan[i][1])):
            for array, start, size, at in parts:
                sem = sems.at[i % 2, len(found)]
                found.append(
                    pltpu.make_async_copy(
                        arrays[array].at[pl.ds(start, size)], buf.at[i % 2, pl.ds(at, size)], sem
                    )
                )
        return found

    def results(i):
        return (
            pltpu.make_async_copy(back_buf.at[i % 2], backs[i], out_sems.at[i % 2, 0]),
            pltpu.make_async_copy(forth_buf.at[i % 2], forths[i], out_sems.at[i % 2, 1]),
        )

    for i in range(blocks):

        @pl.when(step == i)
        def _(i=i):
            if i == 0:
                for copy in copies(0):
                    copy.start()
            if i + 1 < blocks:
                for copy in copies(i + 1):
                    copy.start()
            if i >= 2:
                for copy in results(i - 2):
                    copy.wait()
            for copy in copies(i):
                copy.wait()

    tail = h_buf[slot, rows:].astype(F32)
    tail = tail[:, :rows] + tail[:, rows:]
    gates_buf[...] = jnp.concatenate([tail, jnp.zeros((128 - EXPERTS, rows), F32)], axis=0).T
    place = place_ref[0]
    tile = rows // 2
    lane = lax.broadcasted_iota(jnp.int32, (tile, 128), 1)

    @pl.loop(0, 2)
    def _(r):
        part = pl.ds(pl.multiple_of(r * tile, tile), tile)
        h, g, gates = h_buf[slot, part], g_buf[slot, part], gates_buf[part]
        totals = []
        for e, (ug_ref, da_ref, db_ref) in enumerate(((ug0, da0, db0), (ug1, da1, db1))):
            wg_ref, wu_ref, wd_ref = w_refs[3 * e : 3 * e + 3]
            ff = wg_ref.shape[2]
            gate = jnp.sum(jnp.where(lane == place * MINE + e, gates, 0.0), axis=1, keepdims=True)
            total = 0.0
            for half in range(2):
                sl = slice(half * ff // 2, (half + 1) * ff // 2)
                a = dot(h, wg_ref[0, :, sl], 1, 0)
                b = dot(h, wu_ref[0, :, sl], 1, 0)
                gd = dot(g, wd_ref[0, :, sl], 1, 0)
                sigma = 1.0 / (1.0 + jnp.exp(-a))
                silu = a * sigma
                u = (silu * b).astype(BF).astype(F32)
                total = total + jnp.sum(u * gd, axis=1, keepdims=True)
                ug_ref[part, sl] = (u * gate).astype(BF)
                du = gd * gate
                db_ref[part, sl] = (du * silu).astype(BF)
                da_ref[part, sl] = (du * b * (sigma * (1.0 + a * (1.0 - sigma)))).astype(BF)
            totals.append(total)
        back = dot(da0[part], w_refs[0][0], 1, 1) + dot(db0[part], w_refs[1][0], 1, 1)
        back = back + dot(da1[part], w_refs[3][0], 1, 1) + dot(db1[part], w_refs[4][0], 1, 1)
        back_buf[slot, part] = back.astype(BF)
        forth = dot(ug0[part], w_refs[2][0], 1, 1) + dot(ug1[part], w_refs[5][0], 1, 1)
        forth_buf[slot, part] = forth.astype(BF)
        dg_buf[part] = jnp.where(lane == 0, totals[0], totals[1])

    dg = dg_buf[...].T
    at = lax.broadcasted_iota(jnp.int32, (EXPERTS, rows), 0)
    dg = jnp.where(at == place * MINE, dg[0:1], jnp.where(at == place * MINE + 1, dg[1:2], 0.0))
    high = dg.astype(BF)
    low = (dg - high.astype(F32)).astype(BF)
    back_buf[slot, rows:] = jnp.concatenate([high, low], axis=1)

    for i in range(blocks):

        @pl.when(step == i)
        def _(i=i):
            for copy in results(i):
                copy.start()
            if i == blocks - 1:
                for copy in (*results(i - 1), *results(i)):
                    copy.wait()


def expert_call(place, arrays, plan, weights):
    _, width, ff = weights.shape
    blocks = len(plan)
    rows = sum(piece[2] for piece in plan[0][1])
    most = max(len(h) + len(g) for h, g in plan)
    s = jax.ShapeDtypeStruct
    at = lambda i: (i, 0)
    anywhere = pl.BlockSpec(memory_space=pl.ANY)
    hidden = pl.BlockSpec((rows, ff), at)
    out = pl.pallas_call(
        functools.partial(expert_kernel, plan, len(arrays)),
        grid=(blocks,),
        in_specs=[pl.BlockSpec(memory_space=pltpu.SMEM)]
        + [anywhere] * len(arrays)
        + [pl.BlockSpec((1, width, ff), lambda i, k=k: (k, 0, 0), pipeline_mode=pl.Buffered(1)) for k in range(6)],
        out_specs=[hidden] * 6 + [anywhere] * (2 * blocks),
        out_shape=[s((PLANE * rows, ff), BF)] * 6
        + [s((rows + EXPERTS, width), BF)] * blocks
        + [s((rows, width), BF)] * blocks,
        scratch_shapes=[
            pltpu.VMEM((2, rows + EXPERTS, width), BF),
            pltpu.VMEM((2, rows, width), BF),
            pltpu.VMEM((2, rows + EXPERTS, width), BF),
            pltpu.VMEM((2, rows, width), BF),
            pltpu.VMEM((rows, 128), F32),
            pltpu.VMEM((rows, 128), F32),
            pltpu.SemaphoreType.DMA((2, most)),
            pltpu.SemaphoreType.DMA((2, 2)),
        ],
        cost_estimate=SMALL,
        compiler_params=pltpu.CompilerParams(vmem_limit_bytes=44 * MIB),
    )(place, *arrays, *[weights] * 6)
    return out[:6], out[6 : 6 + blocks], out[6 + blocks :]


STEPS = 4


def weight_grad_kernel(plan, given, count, sums, sum_steps, *refs):
    arrays, refs = refs[:given], refs[given:]
    rights, refs = refs[:count], refs[count:]
    terms, refs = refs[: 2 * sums], refs[2 * sums :]
    out_ref, totals = refs[0], refs[1 : 1 + sums]
    acc_ref, left_buf, sems = refs[1 + sums :]
    k = pl.program_id(0)
    ff = rights[0].shape[1]

    def copies(i):
        return [
            pltpu.make_async_copy(
                arrays[array].at[pl.ds(start, size)], left_buf.at[i % 2, pl.ds(at, size)], sems.at[i % 2, j]
            )
            for j, (array, start, size, at) in enumerate(plan[i])
        ]

    for i in range(STEPS):

        @pl.when(k == i)
        def _(i=i):
            if i == 0:
                for copy in copies(0):
                    copy.start()
            if i + 1 < STEPS:
                for copy in copies(i + 1):
                    copy.start()
            for copy in copies(i):
                copy.wait()

    left = left_buf[lax.rem(k, 2)]
    part = dot(left, jnp.concatenate([r[...] for r in rights], axis=1), 0, 0)

    @pl.when(k < sum_steps)
    def _():
        for i in range(sums):
            totals[i][...] = (terms[2 * i][...].astype(F32) + terms[2 * i + 1][...].astype(F32)).astype(BF)

    @pl.when(k == 0)
    def _():
        acc_ref[...] = part

    @pl.when(k > 0)
    def _():
        acc_ref[...] += part

    @pl.when(k == STEPS - 1)
    def _():
        for t in range(count):
            out_ref[t] = acc_ref[:, t * ff : (t + 1) * ff].astype(BF)


def weight_grads(arrays, blocks, rights, pairs):
    total, ff = rights[0].shape
    width = arrays[0].shape[1]
    count = len(rights)
    size = total // len(blocks)
    each = len(blocks) // STEPS
    plan = [
        [
            (array, start, min(rows, size - at), at + j * size)
            for j in range(each)
            for array, start, rows, at in blocks[i * each + j]
        ]
        for i in range(STEPS)
    ]
    step = total // STEPS
    rows = pairs[0][0].shape[0]
    sum_steps = next(n for n in (4, 3, 2, 1) if rows % (16 * n) == 0)
    tile = pl.BlockSpec((rows // sum_steps, width), lambda i: (jnp.minimum(i, sum_steps - 1), 0))
    s = jax.ShapeDtypeStruct
    out = pl.pallas_call(
        functools.partial(weight_grad_kernel, plan, len(arrays), count, len(pairs), sum_steps),
        grid=(STEPS,),
        in_specs=[pl.BlockSpec(memory_space=pl.ANY)] * len(arrays)
        + [pl.BlockSpec((step, ff), lambda i: (i, 0))] * count
        + [tile] * (2 * len(pairs)),
        out_specs=[pl.BlockSpec((count, width, ff), lambda i: (0, 0, 0), pipeline_mode=pl.Buffered(1))]
        + [tile] * len(pairs),
        out_shape=[s((count, width, ff), BF)] + [s((rows, width), BF)] * len(pairs),
        scratch_shapes=[
            pltpu.VMEM((width, count * ff), F32),
            pltpu.VMEM((2, step, width), BF),
            pltpu.SemaphoreType.DMA((2, max(len(p) for p in plan))),
        ],
        cost_estimate=SMALL,
        compiler_params=pltpu.CompilerParams(vmem_limit_bytes=VMEM_ROOM),
    )(*arrays, *rights, *[term for pair in pairs for term in pair])
    return out[0], out[1:]


def up(v):
    return v.astype(F32)


def after(value, *others):
    return lax.optimization_barrier((value, *others))[0]


CUT = 1536
COLUMNS = 3200


def make_local(n):
    outer = n // PLANE
    plane_groups = [[PLANE * z + i for i in range(PLANE)] for z in range(outer)]
    outer_groups = [[PLANE * z + i for z in range(outer)] for i in range(PLANE)]
    pieced = outer == 4

    def swap(array, offset):
        return lax.ppermute(array, "dp", [(i, i ^ offset) for i in range(n)])

    along_z = [PLANE * k for k in range(4)]

    def dense_gather(part, *earlier):
        if not pieced:
            return [lax.all_gather(part, "dp", axis=0, tiled=True)], [(None, 0)]
        line = after([part] + [swap(part, k) for k in along_z[1:]], *earlier)
        left, right = jnp.stack([t[:, :CUT] for t in line]), jnp.stack([t[:, CUT:] for t in line])
        left_x, right_y = swap(left, 2), swap(right, 4)
        left_y, right_x = swap(left, 4), swap(right, 2)
        left_xy, right_xy = swap(left_x, 4), swap(right_y, 2)
        found = [(left, 0, 0), (left_x, 2, 0), (left_y, 4, 0), (left_xy, 6, 0)]
        found += [(right, 0, CUT), (right_x, 2, CUT), (right_y, 4, CUT), (right_xy, 6, CUT)]
        found += [(swap(piece, 1), offset + 1, first) for piece, offset, first in found]
        return [f[0] for f in found], [([f[1] + k for k in along_z], f[2]) for f in found]

    def grad_spots(share):
        if not pieced:
            return [(n * share, COLUMNS)], [(None, 0)]
        shapes, spots = [], []
        for core in (1, 0):
            for major, minor, first, cols in ((2, 4, 0, CUT), (4, 2, CUT, COLUMNS - CUT)):
                for far in (0, major):
                    shapes.append((8, share, cols))
                    spots.append(([core + far + d + k for d in (0, minor) for k in along_z], first))
        return shapes, spots

    def dense_sum(pieces, earlier):
        if not pieced:
            return up(lax.psum_scatter(pieces[0], "dp", scatter_dimension=0, tiled=True))

        def add(a, b):
            return (up(a) + up(b)).astype(BF)

        near_l, far_l, near_r, far_r = (add(keep, swap(sent, 1)) for sent, keep in zip(pieces[:4], pieces[4:]))
        far_l, far_r = after((far_l, far_r), earlier)
        got_l, got_r = swap(far_l, 2), swap(far_r, 4)
        sent_l, sent_r = add(near_l[4:], got_l[4:]), add(near_r[4:], got_r[4:])
        left = add(add(near_l[:4], got_l[:4]), swap(sent_l, 4))
        right = add(add(near_r[:4], got_r[:4]), swap(sent_r, 2))
        both = jnp.concatenate([left, right], axis=2)
        total = up(both[0])
        for k in range(1, 4):
            total = total + up(swap(both[k], PLANE * k))
        return total

    def both_cores(same_core):
        return [b for part in same_core for b in (part, swap(part, 1))]

    def local(
        tokens,
        query_weight,
        key_projection_weight,
        value_projection_weight,
        output_weight,
        first_gain,
        second_gain,
        router_weight,
        gate_weight,
        up_weight,
        down_weight,
        routes,
        segments,
        cotangent,
    ):
        rows, width = tokens.shape
        ff = gate_weight.shape[2]
        share = query_weight.shape[0]
        me = lax.axis_index("dp").astype(jnp.int32).reshape(1)
        place = lax.rem(me, PLANE)

        expert_part = jnp.stack(
            [w.reshape(PLANE, MINE, share, ff) for w in (gate_weight, up_weight, down_weight.transpose(0, 2, 1))],
            axis=2,
        )
        dense_part = jnp.concatenate(
            [
                query_weight,
                key_projection_weight,
                value_projection_weight,
                output_weight.T,
                router_weight,
                first_gain[:, None],
                second_gain[:, None],
                jnp.zeros((share, 128 - EXPERTS - 2), BF),
            ],
            axis=1,
        )
        dense_part = after(dense_part, expert_part)
        expert_part = lax.all_to_all(
            expert_part, "dp", split_axis=0, concat_axis=0, axis_index_groups=plane_groups
        )

        expert_part = expert_part.transpose(1, 2, 0, 3, 4).reshape(3 * MINE, PLANE * share, ff)
        weights = lax.all_gather(expert_part, "dp", axis=1, tiled=True, axis_index_groups=outer_groups)

        positions = jnp.arange(rows, dtype=F32)
        frequency = 10000.0 ** (-2.0 * jnp.arange(HEAD_SIZE // 2, dtype=F32) / HEAD_SIZE)
        angles = positions[:, None] * frequency[None, :]
        cosine, sine = jnp.cos(angles), jnp.sin(angles)
        cosine = jnp.concatenate([cosine] * 4, axis=1)
        sine = jnp.concatenate([-sine, sine, -sine, sine], axis=1)
        seg_col = segments.reshape(rows, 1)
        seg_row = segments.reshape(1, rows)

        half = rows // 2
        pieces, spots = dense_gather(dense_part, cosine, sine, seg_col, expert_part)
        late = after(cotangent, *pieces)
        cot_x, cot_y = swap(late, 2), swap(late, 4)

        lse, h2, dense, h1, q, k, v, o, r1 = forward_call(
            me, tokens, routes.T, seg_col, seg_row, cosine, sine, pieces, spots
        )
        h2 = after(h2, cot_x, cot_y)
        h2_x, h2_y, h2_core = swap(h2, 2), swap(h2, 4), swap(h2, 1)
        cot_core = swap(cotangent, 1)
        h2_x, h2_y, cot_x, cot_y = after((h2_x, h2_y, cot_x, cot_y), h2_core, cot_core)
        corner_x = swap(jnp.concatenate([h2_y[:half], cot_y[:half]], axis=0), 2)
        corner_y = swap(jnp.concatenate([h2_x[half:], cot_x[half:]], axis=0), 4)
        cores = [swap(t, 1) for t in (h2_x, cot_x, h2_y, cot_y)]
        corner_x, corner_y = after((corner_x, corner_y), *cores)
        long = rows + EXPERTS

        def pieces_of(h, g):
            return ([(h, 0, long, 0)], [(g, 0, rows, 0)])

        first_arrays = [corner_x, swap(corner_x, 1), corner_y, swap(corner_y, 1), h2_x, cores[0], cot_x, cores[1]]
        first_plan = [
            (
                [(i, 0, half, 0), (i + 2, 0, long - half, half)],
                [(i, half, half, 0), (i + 2, long - half, half, half)],
            )
            for i in range(2)
        ]
        first_plan += [pieces_of(i, 2 + i) for i in (4, 5)]
        second_arrays = [h2, h2_core, h2_y, cores[2], cotangent, cot_core, cot_y, cores[3]]
        second_plan = [pieces_of(8 + i, 12 + i) for i in range(4)]

        def outer_sum(grads):
            return lax.psum_scatter(grads, "dp", scatter_dimension=1, tiled=True, axis_index_groups=outer_groups)

        def with_core(block, other):
            return (up(block) + up(other)).astype(BF)

        def together(*values):
            return lax.optimization_barrier(values)

        top, low = slice(0, half), slice(half, None)

        arrays, plan = first_arrays + second_arrays, first_plan + second_plan
        kept, back, out = expert_call(place, arrays, plan, weights)
        core_xy, core_x, core_y = swap(back[1], 1), swap(back[3], 1), swap(back[7], 1)
        sum_xy = [with_core(back[0][part], core_xy[part]) for part in (top, low)]
        sum_xy, core_x, core_y, kept, back, out = together(sum_xy, core_x, core_y, kept, back, out)

        ug0, ug1, da0, da1, db0, db1 = kept
        grads_d, (sum_x, sum_y) = weight_grads(
            arrays, [g for _, g in plan], [ug0, ug1], [(back[2], core_x), (back[6], core_y)]
        )
        via_x, via_y, out_core = swap(sum_xy[0], 2), swap(sum_xy[1], 4), [swap(out[i], 1) for i in (1, 3, 7)]
        grads_d, sum_x, sum_y, via_x, via_y, out_core, kept, out, back = together(
            grads_d, sum_x, sum_y, via_x, via_y, out_core, kept, out, back
        )
        sums_d = outer_sum(grads_d)
        sum_y = jnp.concatenate([with_core(sum_y[top], via_x), sum_y[low]], axis=0)
        sum_x = jnp.concatenate([sum_x[top], with_core(sum_x[low], via_y)], axis=0)
        sum_x, sum_y, kept, back, out, out_core = together(sum_x, sum_y, kept, back, out, out_core)

        _, _, da0, da1, db0, db1 = kept
        grads_gu, (out_xy, out_x, out_y) = weight_grads(
            arrays,
            [h for h, _ in plan],
            [da0, da1, db0, db1],
            [(out[0], out_core[0]), (out[2], out_core[1]), (out[6], out_core[2])],
        )
        got_x, got_y, core_own, out_core_own = swap(sum_x, 2), swap(sum_y, 4), swap(back[5], 1), swap(out[5], 1)
        grads_gu, got_x, got_y, core_own, out_core_own, out_xy, out_x, out_y = together(
            grads_gu, got_x, got_y, core_own, out_core_own, out_xy, out_x, out_y
        )
        sums_gu = outer_sum(grads_gu)
        got = [back[4], core_own, got_x, got_y]
        got, out_x, out_y, out_xy = together(got, out_x, out_y, [out_xy[top], out_xy[low]])

        shapes, grad_places = grad_spots(share)
        input_grad, *grad_pieces = backward_call(
            me, got, tokens, r1, cotangent, h1, h2, dense, q, k, v, o, lse, seg_col, seg_row, cosine, sine,
            shapes, grad_places,
        )
        got_out = [swap(out_x, 2), swap(out_y, 4), swap(out_xy[0], 6)]
        input_grad, grad_pieces, got_out, out_xy = together(input_grad, grad_pieces, got_out, out_xy)
        got_out_low = swap(out_xy[1], 6)
        output = r1 + up(out[4]) + up(out_core_own) + up(got_out[0]) + up(got_out[1])
        output_top, output_low = (output[top] + up(got_out[2])).astype(BF), output[low]
        owned = jnp.concatenate([sums_d, sums_gu], axis=0).reshape(3 * MINE, PLANE, share, ff).transpose(1, 0, 2, 3)
        dense_grads = dense_sum(grad_pieces, (got_out_low, output_top, output_low))
        output = jnp.concatenate([output_top, (output_low + up(got_out_low)).astype(BF)], axis=0)
        owned = lax.all_to_all(owned, "dp", split_axis=0, concat_axis=0, axis_index_groups=plane_groups)

        def experts_of(kind):
            return up(owned[:, MINE * kind : MINE * (kind + 1)]).reshape(EXPERTS, share, ff)

        down_out, gate_out, up_out = experts_of(0).transpose(0, 2, 1), experts_of(1), experts_of(2)
        return (
            output,
            input_grad,
            dense_grads[:, :1024],
            dense_grads[:, 1024:1536],
            dense_grads[:, 1536:2048],
            dense_grads[:, 2048:3072].T,
            dense_grads[:, 3072 + EXPERTS],
            dense_grads[:, 3073 + EXPERTS],
            dense_grads[:, 3072 : 3072 + EXPERTS],
            gate_out,
            up_out,
            down_out,
        )

    return local


def solution(mesh):
    row, col, one = P("dp", None), P(None, "dp"), P("dp")
    middle, last = P(None, "dp", None), P(None, None, "dp")
    in_specs = (row, row, row, row, col, one, one, row, middle, middle, last, row, row, row)
    out_specs = (row, row, row, row, row, col, one, one, row, middle, middle, last)
    return jax.shard_map(
        make_local(mesh.shape["dp"]), mesh=mesh, in_specs=in_specs, out_specs=out_specs, check_vma=False
    )
```

```python
import functools

import jax
import jax.numpy as jnp
from jax import lax
from jax.experimental import pallas as pl
from jax.experimental.pallas import tpu as pltpu
from jax.sharding import PartitionSpec as P

EXPERTS = 16
PLANE = 8
MINE = EXPERTS // PLANE
HEADS = 16
HEAD_SIZE = 64
BLOCK = 128
MOST_DOC = 256
MIB = 2**20
VMEM_ROOM = 60 * MIB
SMALL = pl.CostEstimate(flops=1, bytes_accessed=1, transcendentals=0)
epsilon = 1e-06
neg_large = -1000000000.0
BF = jnp.bfloat16
F32 = jnp.float32


def dot(a, b, ca, cb):
    return lax.dot_general(a, b, (((ca,), (cb,)), ((), ())), preferred_element_type=F32)

def rms_scale(values):
    return lax.rsqrt(jnp.mean(values * values, axis=-1, keepdims=True) + epsilon)

def swap_halves(u):
    lane = lax.broadcasted_iota(jnp.int32, u.shape, 1)
    return jnp.where(lane % 64 < 32, pltpu.roll(u, u.shape[1] - 32, 1), pltpu.roll(u, 32, 1))

def crossed(u, w):
    lane = lax.broadcasted_iota(jnp.int32, u.shape, 1)
    return (
        jnp.where(lane < 64, u, pltpu.roll(w, 64, 1)),
        jnp.where(lane < 64, pltpu.roll(u, 64, 1), w),
    )


def key_range(rows, qb):
    end = (qb + 1) * BLOCK
    return max(0, end - BLOCK - MOST_DOC), end

def fill_mask(mask_ref, seg_col_ref, seg_row_ref, rows):
    for qb in range(rows // BLOCK):
        low, high = key_range(rows, qb)
        keys = low + lax.broadcasted_iota(jnp.int32, (high - low, BLOCK), 0)
        queries = qb * BLOCK + lax.broadcasted_iota(jnp.int32, (high - low, BLOCK), 1)
        same = seg_col_ref[low:high, :1] == seg_row_ref[:1, qb * BLOCK : (qb + 1) * BLOCK]
        mask_ref[qb, : high - low] = jnp.where(same & (keys <= queries), 1.0, 0.0)

def masked_scores(mask_ref, k_c, q_pair, qb, span):
    s = dot(k_c, q_pair, 1, 1)
    m = mask_ref[qb, :span]
    return jnp.where(jnp.concatenate([m, m], axis=1) > 0, s, neg_large)

def piece_copies(me_ref, spots, pieces, whole_ref, sems, inward):
    copies = []
    for ref, (offsets, first) in zip(pieces, spots):
        if offsets is None:
            sides = [(ref, whole_ref)]
        else:
            share, cols = ref.shape[1:]
            sides = []
            for i, offset in enumerate(offsets):
                row = pl.multiple_of((me_ref[0] ^ offset) * share, share)
                sides.append((ref.at[i], whole_ref.at[pl.ds(row, share), first : first + cols]))
        for part, place in sides:
            source, target = (part, place) if inward else (place, part)
            copies.append(pltpu.make_async_copy(source, target, sems.at[len(copies)]))
    return copies


def spot_columns(spots):
    return [first if offsets else -1 for offsets, first in spots for _ in (offsets or [None])]


def piece_count(spots):
    return sum(1 if offsets is None else len(offsets) for offsets, _ in spots)


def forward_kernel(spots, me_ref, x_ref, routes_ref, seg_col_ref, seg_row_ref, cos_ref, sin_ref, *refs):
    pieces, refs = refs[: len(spots)], refs[len(spots) :]
    lse_ref, h2_ref, *outs = refs[:9]
    mask_ref, w_ref, h1_ref, q_ref, k_ref, v_ref, o_ref, r1_ref, sems, out_sems = refs[9:]

    def leave(i, source):
        copy = pltpu.make_async_copy(source, outs[i], out_sems.at[i])
        copy.start()
        return copy

    copies = piece_copies(me_ref, spots, pieces, w_ref, sems, True)
    for copy in copies:
        copy.start()
    fill_mask(mask_ref, seg_col_ref, seg_row_ref, x_ref.shape[0])
    for copy in copies:
        copy.wait()
    leaving = [leave(0, w_ref)]
    rows, width = x_ref.shape
    x = x_ref[...].astype(F32)
    gains = w_ref[:, 3072:3200].astype(F32).T
    h1_ref[...] = (x * rms_scale(x) * gains[16:17]).astype(BF)
    leaving.append(leave(1, h1_ref))

    @pl.loop(0, 4)
    def _(j):
        qs = pl.ds(pl.multiple_of(j * 256, 256), 256)
        ks = pl.ds(pl.multiple_of(j * 128, 128), 128)
        vs = pl.ds(pl.multiple_of(1536 + j * 128, 128), 128)
        kw = pl.ds(pl.multiple_of(1024 + j * 128, 128), 128)
        h1 = h1_ref[...]
        cos, sin = cos_ref[...], sin_ref[...]
        q2 = dot(h1, w_ref[:, qs], 1, 0)
        qa, qb_ = crossed(q2[:, :128], q2[:, 128:])
        qa = (qa * cos + swap_halves(qa) * sin).astype(BF) * BF(0.125)
        qb_ = (qb_ * cos + swap_halves(qb_) * sin).astype(BF) * BF(0.125)
        k = dot(h1, w_ref[:, kw], 1, 0)
        k = (k * cos + swap_halves(k) * sin).astype(BF)
        v32 = dot(h1, w_ref[:, vs], 1, 0)
        v = v32.astype(BF)
        q_ref[:, qs] = jnp.concatenate([qa, qb_], axis=1)
        k_ref[:, ks] = k
        v_ref[:, ks] = v
        vt = v32.T.astype(BF)
        lane = lax.broadcasted_iota(jnp.int32, (rows, 128), 1)
        sub = lax.broadcasted_iota(jnp.int32, (128, rows), 0)
        outs = []
        for qb in range(rows // BLOCK):
            low, high = key_range(rows, qb)
            blk = slice(qb * BLOCK, (qb + 1) * BLOCK)
            q_pair = jnp.concatenate([qa[blk], qb_[blk]], axis=0)
            total = None
            for c in range(2):
                k_c = jnp.where(lane[low:high] // 64 == c, k[low:high], BF(0))
                vt_c = jnp.where(sub[:, low:high] // 64 == c, vt[:, low:high], BF(0))
                s = masked_scores(mask_ref, k_c, q_pair, qb, high - low)
                top = jnp.max(s, axis=0, keepdims=True)
                e = jnp.exp(s - top)
                norm = jnp.sum(e, axis=0, keepdims=True)
                p = (e * (1.0 / norm)).astype(BF)
                part = dot(vt_c, p, 1, 0)
                total = part if total is None else total + part
                lse = top + jnp.log(norm)
                lse_ref[j, c : c + 1, blk] = lse[:, :128]
                lse_ref[j, 2 + c : 3 + c, blk] = lse[:, 128:]
            outs.append(total)
        a = jnp.concatenate([t[:, :128] for t in outs], axis=1).T
        b = jnp.concatenate([t[:, 128:] for t in outs], axis=1).T
        o_ref[:, qs] = jnp.concatenate(crossed(a, b), axis=1).astype(BF)

    leaving += [leave(i, ref) for i, ref in ((2, q_ref), (3, k_ref), (4, v_ref), (5, o_ref))]
    r1 = x_ref[...].astype(F32) + dot(o_ref[...], w_ref[:, 2048:3072], 1, 1)
    r1_ref[...] = r1
    leaving.append(leave(6, r1_ref))
    h2 = (r1 * rms_scale(r1) * gains[17:18]).astype(BF)
    h2_ref[:rows] = h2
    logits = dot(h2, w_ref[:, 3072:3200], 1, 0).T[:EXPERTS]
    at = lax.broadcasted_iota(jnp.int32, (EXPERTS, rows), 0)
    chosen = at < 0
    for t in range(routes_ref.shape[0]):
        chosen = chosen | (at == routes_ref[t : t + 1])
    logits = jnp.where(chosen, logits, neg_large)
    ex = jnp.where(chosen, jnp.exp(logits - jnp.max(logits, axis=0, keepdims=True)), 0.0)
    gates = ex / jnp.sum(ex, axis=0, keepdims=True)
    high = gates.astype(BF)
    low = (gates - high.astype(F32)).astype(BF)
    h2_ref[rows:] = jnp.concatenate([high, low], axis=1)
    for copy in leaving:
        copy.wait()

def forward_call(me, x, routes, seg_col, seg_row, cos, sin, pieces, spots):
    rows, width = x.shape
    s = jax.ShapeDtypeStruct
    vmem, anywhere = pl.BlockSpec(memory_space=pltpu.VMEM), pl.BlockSpec(memory_space=pl.ANY)
    return pl.pallas_call(
        functools.partial(forward_kernel, spots),
        in_specs=[pl.BlockSpec(memory_space=pltpu.SMEM)] + [vmem] * 6 + [anywhere] * len(pieces),
        out_specs=[vmem] * 2 + [anywhere] * 7,
        out_shape=[
            s((4, 4, rows), F32),
            s((rows + EXPERTS, width), BF),
            s((width, 3200), BF),
            s((rows, width), BF),
            s((rows, 1024), BF),
            s((rows, 512), BF),
            s((rows, 512), BF),
            s((rows, 1024), BF),
            s((rows, width), F32),
        ],
        scratch_shapes=[
            pltpu.VMEM((rows // BLOCK, BLOCK + MOST_DOC, BLOCK), F32),
            pltpu.VMEM((width, 3200), BF),
            pltpu.VMEM((rows, width), BF),
            pltpu.VMEM((rows, 1024), BF),
            pltpu.VMEM((rows, 512), BF),
            pltpu.VMEM((rows, 512), BF),
            pltpu.VMEM((rows, 1024), BF),
            pltpu.VMEM((rows, width), F32),
            pltpu.SemaphoreType.DMA((piece_count(spots),)),
            pltpu.SemaphoreType.DMA((7,)),
        ],
        cost_estimate=SMALL,
        compiler_params=pltpu.CompilerParams(vmem_limit_bytes=VMEM_ROOM),
    )(me, x, routes, seg_col, seg_row, cos, sin, *pieces)


ARRIVING = 14


def backward_kernel(spots, me_ref, *refs):
    given, refs = refs[:ARRIVING], refs[ARRIVING:]
    lse_ref, seg_col_ref, seg_row_ref, cos_ref, sin_ref, ig_ref = refs[:6]
    pieces, refs = refs[6 : 6 + len(spots)], refs[6 + len(spots) :]
    held, refs = refs[:ARRIVING], refs[ARRIVING:]
    mask_ref, do_ref, dqkv_ref, dr1_ref, wg_ref, sems, in_sems = refs
    p0, p1, p2, p3, r1_ref, cot_ref, h2_ref, w_ref, o_ref, q_ref, k_ref, v_ref, h1_ref, x_ref = held
    parts = [(given[i], held[i]) for i in range(7)]
    for cols in (slice(3072, 3200), slice(2048, 3072), slice(0, 2048)):
        parts.append((given[7].at[:, cols], w_ref.at[:, cols]))
        if cols.start == 2048:
            parts += [(given[i], held[i]) for i in range(8, 12)]
    parts += [(given[12], h1_ref), (given[13], x_ref)]
    copies = [pltpu.make_async_copy(source, target, in_sems.at[i]) for i, (source, target) in enumerate(parts)]
    for copy in copies:
        copy.start()
    fill_mask(mask_ref, seg_col_ref, seg_row_ref, r1_ref.shape[0])
    for copy in copies[:8]:
        copy.wait()
    rows, width = x_ref.shape
    misc = w_ref[:, 3072:3200]
    gains = misc.astype(F32).T

    def up(ref, sl):
        return ref[sl].astype(F32)

    top, tail = slice(0, rows), slice(rows, rows + EXPERTS)
    dh2 = up(p0, top) + up(p1, top) + up(p2, top) + up(p3, top)
    dg = up(p0, tail) + up(p1, tail) + up(p2, tail) + up(p3, tail)
    dg = dg[:, :rows] + dg[:, rows:]
    gates = up(h2_ref, tail)
    gates = gates[:, :rows] + gates[:, rows:]
    h2 = h2_ref[:rows]
    dlog = gates * (dg - jnp.sum(gates * dg, axis=0, keepdims=True))
    dlog = jnp.concatenate([dlog, jnp.zeros((128 - EXPERTS, rows), F32)], axis=0).T.astype(BF)
    dh2 = dh2 + dot(dlog, misc, 1, 1)
    r1 = r1_ref[...]
    s2 = rms_scale(r1)
    w2 = dh2 * gains[17:18]
    gain2_grad = jnp.sum(dh2 * r1 * s2, axis=0, keepdims=True)
    dr1 = cot_ref[...].astype(F32) + s2 * w2 - r1 * (s2 * s2 * s2) * jnp.mean(w2 * r1, axis=-1, keepdims=True)
    dr1_ref[...] = dr1
    dz = dr1.astype(BF)
    for copy in copies[8:13]:
        copy.wait()
    wg_ref[:, 2048:3072] = dot(dz, o_ref[...], 0, 0).astype(BF)
    do_ref[...] = dot(dz, w_ref[:, 2048:3072], 1, 0).astype(BF)
    router_t = dot(dlog, h2, 0, 0)

    @pl.loop(0, 4)
    def _(j):
        qs = pl.ds(pl.multiple_of(j * 256, 256), 256)
        ks = pl.ds(pl.multiple_of(j * 128, 128), 128)
        vs = pl.ds(pl.multiple_of(1536 + j * 128, 128), 128)
        kw = pl.ds(pl.multiple_of(1024 + j * 128, 128), 128)
        cos, sin = cos_ref[...], sin_ref[...]
        def back(g):
            return g * cos - swap_halves(g) * sin
        q, k, v = q_ref[:, qs], k_ref[:, ks], v_ref[:, ks]
        do = do_ref[:, qs].astype(F32)
        do = jnp.concatenate(crossed(do[:, :128], do[:, 128:]), axis=1).astype(BF)
        kt = k.astype(F32).T.astype(BF)
        lane = lax.broadcasted_iota(jnp.int32, (rows, 128), 1)
        sub = lax.broadcasted_iota(jnp.int32, (128, rows), 0)
        dks = [jnp.zeros((BLOCK, 128), F32) for _ in range(rows // BLOCK)]
        dvs = [jnp.zeros((BLOCK, 128), F32) for _ in range(rows // BLOCK)]
        dqs = []
        for qb in range(rows // BLOCK):
            low, high = key_range(rows, qb)
            blk = slice(qb * BLOCK, (qb + 1) * BLOCK)
            q_pair = jnp.concatenate([q[blk, :128], q[blk, 128:]], axis=0)
            do_pair = jnp.concatenate([do[blk, :128], do[blk, 128:]], axis=0)
            dq_t = None
            for c in range(2):
                mine = lane[low:high] // 64 == c
                k_c = jnp.where(mine, k[low:high], BF(0))
                v_c = jnp.where(mine, v[low:high], BF(0))
                kt_c = jnp.where(sub[:, low:high] // 64 == c, kt[:, low:high], BF(0))
                s = masked_scores(mask_ref, k_c, q_pair, qb, high - low)
                lse = jnp.concatenate([lse_ref[j, c : c + 1, blk], lse_ref[j, 2 + c : 3 + c, blk]], axis=1)
                p = jnp.exp(s - lse)
                dp = dot(v_c, do_pair, 1, 1)
                inner = jnp.sum(p * dp, axis=0, keepdims=True)
                ds = (p * (dp - inner)).astype(BF)
                dk = dot(ds, q_pair, 1, 0)
                dv = dot(p.astype(BF), do_pair, 1, 0)
                t = dot(kt_c, ds, 1, 0)
                dq_t = t if dq_t is None else dq_t + t
                for i, kb in enumerate(range(low // BLOCK, high // BLOCK)):
                    sl = slice(i * BLOCK, (i + 1) * BLOCK)
                    dks[kb] = dks[kb] + jnp.where(mine[sl], dk[sl], 0.0)
                    dvs[kb] = dvs[kb] + jnp.where(mine[sl], dv[sl], 0.0)
            dqs.append(dq_t)
        dqa = jnp.concatenate([t[:, :128] for t in dqs], axis=1).T * 0.125
        dqb = jnp.concatenate([t[:, 128:] for t in dqs], axis=1).T * 0.125
        dqkv_ref[:, qs] = jnp.concatenate(crossed(back(dqa), back(dqb)), axis=1).astype(BF)
        dqkv_ref[:, kw] = back(jnp.concatenate(dks, axis=0)).astype(BF)
        dqkv_ref[:, vs] = jnp.concatenate(dvs, axis=0).astype(BF)

    for copy in copies[13:]:
        copy.wait()
    leaving = piece_copies(me_ref, spots, pieces, wg_ref, sems, False)
    wg_ref[:, :1536] = dot(h1_ref[...], dqkv_ref[:, :1536], 0, 0).astype(BF)
    early = [i for i, first in enumerate(spot_columns(spots)) if first == 0]
    for i in early:
        leaving[i].start()
    wg_ref[:, 1536:2048] = dot(h1_ref[...], dqkv_ref[:, 1536:], 0, 0).astype(BF)
    dh1 = dot(dqkv_ref[...], w_ref[:, :2048], 1, 1)
    x = x_ref[...].astype(F32)
    s1 = rms_scale(x)
    w1 = dh1 * gains[16:17]
    gain1_grad = jnp.sum(dh1 * x * s1, axis=0, keepdims=True)
    at = lax.broadcasted_iota(jnp.int32, (128, width), 0)
    misc_t = jnp.where(at == 16, gain1_grad, jnp.where(at == 17, gain2_grad, router_t))
    wg_ref[:, 3072:3200] = misc_t.T.astype(BF)
    for i in range(len(leaving)):
        if i not in early:
            leaving[i].start()
    ig_ref[...] = dr1_ref[...] + s1 * w1 - x * (s1 * s1 * s1) * jnp.mean(w1 * x, axis=-1, keepdims=True)
    for copy in leaving:
        copy.wait()


def backward_call(me, parts, x, r1, cot, h1, h2, w, q, k, v, o, lse, seg_col, seg_row, cos, sin, piece_shapes, spots):
    rows, width = x.shape
    s = jax.ShapeDtypeStruct
    vmem, anywhere = pl.BlockSpec(memory_space=pltpu.VMEM), pl.BlockSpec(memory_space=pl.ANY)
    arriving = [*parts, r1, cot, h2, w, o, q, k, v, h1, x]
    return pl.pallas_call(
        functools.partial(backward_kernel, spots),
        in_specs=[pl.BlockSpec(memory_space=pltpu.SMEM)] + [anywhere] * ARRIVING + [vmem] * 5,
        out_specs=[vmem] + [anywhere] * len(spots),
        out_shape=[s((rows, width), F32)] + [s(shape, BF) for shape in piece_shapes],
        scratch_shapes=[pltpu.VMEM(a.shape, a.dtype) for a in arriving]
        + [
            pltpu.VMEM((rows // BLOCK, BLOCK + MOST_DOC, BLOCK), F32),
            pltpu.VMEM((rows, 1024), BF),
            pltpu.VMEM((rows, 2048), BF),
            pltpu.VMEM((rows, width), F32),
            pltpu.VMEM((width, 3200), BF),
            pltpu.SemaphoreType.DMA((piece_count(spots),)),
            pltpu.SemaphoreType.DMA((ARRIVING + 2,)),
        ],
        cost_estimate=SMALL,
        compiler_params=pltpu.CompilerParams(vmem_limit_bytes=VMEM_ROOM),
    )(me, *arriving, lse, seg_col, seg_row, cos, sin)


def expert_kernel(plan, count, place_ref, *refs):
    blocks = len(plan)
    arrays, refs = refs[:count], refs[count:]
    w_refs = refs[:6]
    ug0, ug1, da0, da1, db0, db1, h_all, g_all = refs[6:14]
    backs, forths = refs[14 : 14 + blocks], refs[14 + blocks : 14 + 2 * blocks]
    h_buf, g_buf, back_buf, forth_buf, gates_buf, dg_buf, sems, out_sems = refs[14 + 2 * blocks :]
    rows = g_buf.shape[1]
    step = pl.program_id(0)
    slot = lax.rem(step, 2)

    def copies(i):
        found = []
        for buf, parts in ((h_buf, plan[i][0]), (g_buf, plan[i][1])):
            for array, start, size, at in parts:
                sem = sems.at[i % 2, len(found)]
                found.append(
                    pltpu.make_async_copy(
                        arrays[array].at[pl.ds(start, size)], buf.at[i % 2, pl.ds(at, size)], sem
                    )
                )
        return found

    def results(i):
        return (
            pltpu.make_async_copy(back_buf.at[i % 2], backs[i], out_sems.at[i % 2, 0]),
            pltpu.make_async_copy(forth_buf.at[i % 2], forths[i], out_sems.at[i % 2, 1]),
        )

    for i in range(blocks):

        @pl.when(step == i)
        def _(i=i):
            if i == 0:
                for copy in copies(0):
                    copy.start()
            if i + 1 < blocks:
                for copy in copies(i + 1):
                    copy.start()
            if i >= 2:
                for copy in results(i - 2):
                    copy.wait()
            for copy in copies(i):
                copy.wait()

    tail = h_buf[slot, rows:].astype(F32)
    tail = tail[:, :rows] + tail[:, rows:]
    gates_buf[...] = jnp.concatenate([tail, jnp.zeros((128 - EXPERTS, rows), F32)], axis=0).T
    place = place_ref[0]
    tile = rows // 2
    lane = lax.broadcasted_iota(jnp.int32, (tile, 128), 1)

    @pl.loop(0, 2)
    def _(r):
        part = pl.ds(pl.multiple_of(r * tile, tile), tile)
        h, g, gates = h_buf[slot, part], g_buf[slot, part], gates_buf[part]
        h_all[part], g_all[part] = h, g
        totals = []
        for e, (ug_ref, da_ref, db_ref) in enumerate(((ug0, da0, db0), (ug1, da1, db1))):
            wg_ref, wu_ref, wd_ref = w_refs[3 * e : 3 * e + 3]
            ff = wg_ref.shape[2]
            gate = jnp.sum(jnp.where(lane == place * MINE + e, gates, 0.0), axis=1, keepdims=True)
            total = 0.0
            for half in range(2):
                sl = slice(half * ff // 2, (half + 1) * ff // 2)
                a = dot(h, wg_ref[0, :, sl], 1, 0)
                b = dot(h, wu_ref[0, :, sl], 1, 0)
                gd = dot(g, wd_ref[0, :, sl], 1, 0)
                sigma = 0.5 * jnp.tanh(0.5 * a) + 0.5
                silu = a * sigma
                u = (silu * b).astype(BF).astype(F32)
                total = total + jnp.sum(u * gd, axis=1, keepdims=True)
                ug_ref[part, sl] = (u * gate).astype(BF)
                du = gd * gate
                db_ref[part, sl] = (du * silu).astype(BF)
                da_ref[part, sl] = (du * b * (sigma * (1.0 + a * (1.0 - sigma)))).astype(BF)
            totals.append(total)
        back = dot(da0[part], w_refs[0][0], 1, 1) + dot(db0[part], w_refs[1][0], 1, 1)
        back = back + dot(da1[part], w_refs[3][0], 1, 1) + dot(db1[part], w_refs[4][0], 1, 1)
        back_buf[slot, part] = back.astype(BF)
        forth = dot(ug0[part], w_refs[2][0], 1, 1) + dot(ug1[part], w_refs[5][0], 1, 1)
        forth_buf[slot, part] = forth.astype(BF)
        dg_buf[part] = jnp.where(lane == 0, totals[0], totals[1])

    dg = dg_buf[...].T
    at = lax.broadcasted_iota(jnp.int32, (EXPERTS, rows), 0)
    dg = jnp.where(at == place * MINE, dg[0:1], jnp.where(at == place * MINE + 1, dg[1:2], 0.0))
    high = dg.astype(BF)
    low = (dg - high.astype(F32)).astype(BF)
    back_buf[slot, rows:] = jnp.concatenate([high, low], axis=1)

    for i in range(blocks):

        @pl.when(step == i)
        def _(i=i):
            for copy in results(i):
                copy.start()
            if i == blocks - 1:
                for copy in (*results(i - 1), *results(i)):
                    copy.wait()


def expert_call(place, arrays, plan, weights):
    _, width, ff = weights.shape
    blocks = len(plan)
    rows = sum(piece[2] for piece in plan[0][1])
    most = max(len(h) + len(g) for h, g in plan)
    s = jax.ShapeDtypeStruct
    at = lambda i: (i, 0)
    anywhere = pl.BlockSpec(memory_space=pl.ANY)
    hidden, tile = pl.BlockSpec((rows, ff), at), pl.BlockSpec((rows, width), at)
    out = pl.pallas_call(
        functools.partial(expert_kernel, plan, len(arrays)),
        grid=(blocks,),
        in_specs=[pl.BlockSpec(memory_space=pltpu.SMEM)]
        + [anywhere] * len(arrays)
        + [pl.BlockSpec((1, width, ff), lambda i, k=k: (k, 0, 0), pipeline_mode=pl.Buffered(1)) for k in range(6)],
        out_specs=[hidden] * 6 + [tile] * 2 + [anywhere] * (2 * blocks),
        out_shape=[s((PLANE * rows, ff), BF)] * 6
        + [s((PLANE * rows, width), BF)] * 2
        + [s((rows + EXPERTS, width), BF)] * blocks
        + [s((rows, width), BF)] * blocks,
        scratch_shapes=[
            pltpu.VMEM((2, rows + EXPERTS, width), BF),
            pltpu.VMEM((2, rows, width), BF),
            pltpu.VMEM((2, rows + EXPERTS, width), BF),
            pltpu.VMEM((2, rows, width), BF),
            pltpu.VMEM((rows, 128), F32),
            pltpu.VMEM((rows, 128), F32),
            pltpu.SemaphoreType.DMA((2, most)),
            pltpu.SemaphoreType.DMA((2, 2)),
        ],
        cost_estimate=SMALL,
        compiler_params=pltpu.CompilerParams(vmem_limit_bytes=44 * MIB),
    )(place, *arrays, *[weights] * 6)
    return out[:8], out[8 : 8 + blocks], out[8 + blocks :]


STEPS = 4


def weight_grad_kernel(count, sums, sum_steps, left_ref, *refs):
    rights, refs = refs[:count], refs[count:]
    terms, refs = refs[: 2 * sums], refs[2 * sums :]
    out_ref, totals, acc_ref = refs[0], refs[1:-1], refs[-1]
    k = pl.program_id(0)
    ff = rights[0].shape[1]
    part = dot(left_ref[...], jnp.concatenate([r[...] for r in rights], axis=1), 0, 0)

    @pl.when(k < sum_steps)
    def _():
        for i in range(sums):
            totals[i][...] = (terms[2 * i][...].astype(F32) + terms[2 * i + 1][...].astype(F32)).astype(BF)

    @pl.when(k == 0)
    def _():
        acc_ref[...] = part

    @pl.when(k > 0)
    def _():
        acc_ref[...] += part

    @pl.when(k == STEPS - 1)
    def _():
        for t in range(count):
            out_ref[t] = acc_ref[:, t * ff : (t + 1) * ff].astype(BF)


def weight_grads(left, rights, pairs=()):
    total, width = left.shape
    ff = rights[0].shape[1]
    count = len(rights)
    step = total // STEPS
    row = lambda i: (i, 0)
    rows = pairs[0][0].shape[0] if pairs else 0
    sum_steps = next(n for n in (4, 3, 2, 1) if rows % (16 * n) == 0)
    tile = pl.BlockSpec((rows // sum_steps, width), lambda i: (jnp.minimum(i, sum_steps - 1), 0))
    s = jax.ShapeDtypeStruct
    out = pl.pallas_call(
        functools.partial(weight_grad_kernel, count, len(pairs), sum_steps),
        grid=(STEPS,),
        in_specs=[pl.BlockSpec((step, width), row)]
        + [pl.BlockSpec((step, ff), row)] * count
        + [tile] * (2 * len(pairs)),
        out_specs=[pl.BlockSpec((count, width, ff), lambda i: (0, 0, 0), pipeline_mode=pl.Buffered(1))]
        + [tile] * len(pairs),
        out_shape=[s((count, width, ff), BF)] + [s((rows, width), BF)] * len(pairs),
        scratch_shapes=[pltpu.VMEM((width, count * ff), F32)],
        cost_estimate=SMALL,
        compiler_params=pltpu.CompilerParams(vmem_limit_bytes=VMEM_ROOM),
    )(left, *rights, *[term for pair in pairs for term in pair])
    return out[0], out[1:]


def up(v):
    return v.astype(F32)


def after(value, *others):
    return lax.optimization_barrier((value, *others))[0]


CUT = 1536
COLUMNS = 3200


def make_local(n):
    outer = n // PLANE
    plane_groups = [[PLANE * z + i for i in range(PLANE)] for z in range(outer)]
    outer_groups = [[PLANE * z + i for z in range(outer)] for i in range(PLANE)]
    pieced = outer == 4

    def swap(array, offset):
        return lax.ppermute(array, "dp", [(i, i ^ offset) for i in range(n)])

    along_z = [PLANE * k for k in range(4)]

    def dense_gather(part, *earlier):
        if not pieced:
            return [lax.all_gather(part, "dp", axis=0, tiled=True)], [(None, 0)]
        line = after([part] + [swap(part, k) for k in along_z[1:]], *earlier)
        left, right = jnp.stack([t[:, :CUT] for t in line]), jnp.stack([t[:, CUT:] for t in line])
        left_x, right_y = swap(left, 2), swap(right, 4)
        left_y, right_x = swap(left, 4), swap(right, 2)
        left_xy, right_xy = swap(left_x, 4), swap(right_y, 2)
        found = [(left, 0, 0), (left_x, 2, 0), (left_y, 4, 0), (left_xy, 6, 0)]
        found += [(right, 0, CUT), (right_x, 2, CUT), (right_y, 4, CUT), (right_xy, 6, CUT)]
        found += [(swap(piece, 1), offset + 1, first) for piece, offset, first in found]
        return [f[0] for f in found], [([f[1] + k for k in along_z], f[2]) for f in found]

    def grad_spots(share):
        if not pieced:
            return [(n * share, COLUMNS)], [(None, 0)]
        shapes, spots = [], []
        for core in (1, 0):
            for major, minor, first, cols in ((2, 4, 0, CUT), (4, 2, CUT, COLUMNS - CUT)):
                for far in (0, major):
                    shapes.append((8, share, cols))
                    spots.append(([core + far + d + k for d in (0, minor) for k in along_z], first))
        return shapes, spots

    def dense_sum(pieces, earlier):
        if not pieced:
            return up(lax.psum_scatter(pieces[0], "dp", scatter_dimension=0, tiled=True))

        def add(a, b):
            return (up(a) + up(b)).astype(BF)

        near_l, far_l, near_r, far_r = (add(keep, swap(sent, 1)) for sent, keep in zip(pieces[:4], pieces[4:]))
        far_l, far_r = after((far_l, far_r), earlier)
        got_l, got_r = swap(far_l, 2), swap(far_r, 4)
        sent_l, sent_r = add(near_l[4:], got_l[4:]), add(near_r[4:], got_r[4:])
        left = add(add(near_l[:4], got_l[:4]), swap(sent_l, 4))
        right = add(add(near_r[:4], got_r[:4]), swap(sent_r, 2))
        both = jnp.concatenate([left, right], axis=2)
        total = up(both[0])
        for k in range(1, 4):
            total = total + up(swap(both[k], PLANE * k))
        return total

    def both_cores(same_core):
        return [b for part in same_core for b in (part, swap(part, 1))]

    def local(
        tokens,
        query_weight,
        key_projection_weight,
        value_projection_weight,
        output_weight,
        first_gain,
        second_gain,
        router_weight,
        gate_weight,
        up_weight,
        down_weight,
        routes,
        segments,
        cotangent,
    ):
        rows, width = tokens.shape
        ff = gate_weight.shape[2]
        share = query_weight.shape[0]
        me = lax.axis_index("dp").astype(jnp.int32).reshape(1)
        place = lax.rem(me, PLANE)

        expert_part = jnp.stack(
            [w.reshape(PLANE, MINE, share, ff) for w in (gate_weight, up_weight, down_weight.transpose(0, 2, 1))],
            axis=2,
        )
        dense_part = jnp.concatenate(
            [
                query_weight,
                key_projection_weight,
                value_projection_weight,
                output_weight.T,
                router_weight,
                first_gain[:, None],
                second_gain[:, None],
                jnp.zeros((share, 128 - EXPERTS - 2), BF),
            ],
            axis=1,
        )
        dense_part = after(dense_part, expert_part)
        expert_part = lax.all_to_all(
            expert_part, "dp", split_axis=0, concat_axis=0, axis_index_groups=plane_groups
        )

        expert_part = expert_part.transpose(1, 2, 0, 3, 4).reshape(3 * MINE, PLANE * share, ff)
        weights = lax.all_gather(expert_part, "dp", axis=1, tiled=True, axis_index_groups=outer_groups)

        positions = jnp.arange(rows, dtype=F32)
        frequency = 10000.0 ** (-2.0 * jnp.arange(HEAD_SIZE // 2, dtype=F32) / HEAD_SIZE)
        angles = positions[:, None] * frequency[None, :]
        cosine, sine = jnp.cos(angles), jnp.sin(angles)
        cosine = jnp.concatenate([cosine] * 4, axis=1)
        sine = jnp.concatenate([-sine, sine, -sine, sine], axis=1)
        seg_col = segments.reshape(rows, 1)
        seg_row = segments.reshape(1, rows)

        half = rows // 2
        pieces, spots = dense_gather(dense_part, cosine, sine, seg_col, expert_part)
        late = after(cotangent, *pieces)
        cot_x, cot_y = swap(late, 2), swap(late, 4)

        lse, h2, dense, h1, q, k, v, o, r1 = forward_call(
            me, tokens, routes.T, seg_col, seg_row, cosine, sine, pieces, spots
        )
        h2 = after(h2, cot_x, cot_y)
        h2_x, h2_y, h2_core = swap(h2, 2), swap(h2, 4), swap(h2, 1)
        cot_core = swap(cotangent, 1)
        h2_x, h2_y, cot_x, cot_y = after((h2_x, h2_y, cot_x, cot_y), h2_core, cot_core)
        corner_x = swap(jnp.concatenate([h2_y[:half], cot_y[:half]], axis=0), 2)
        corner_y = swap(jnp.concatenate([h2_x[half:], cot_x[half:]], axis=0), 4)
        cores = [swap(t, 1) for t in (h2_x, cot_x, h2_y, cot_y)]
        corner_x, corner_y = after((corner_x, corner_y), *cores)
        long = rows + EXPERTS

        def pieces_of(h, g):
            return ([(h, 0, long, 0)], [(g, 0, rows, 0)])

        first_arrays = [corner_x, swap(corner_x, 1), corner_y, swap(corner_y, 1), h2_x, cores[0], cot_x, cores[1]]
        first_plan = [
            (
                [(i, 0, half, 0), (i + 2, 0, long - half, half)],
                [(i, half, half, 0), (i + 2, long - half, half, half)],
            )
            for i in range(2)
        ]
        first_plan += [pieces_of(i, 2 + i) for i in (4, 5)]
        second_arrays = [h2, h2_core, h2_y, cores[2], cotangent, cot_core, cot_y, cores[3]]
        second_plan = [pieces_of(8 + i, 12 + i) for i in range(4)]

        def outer_sum(grads):
            return lax.psum_scatter(grads, "dp", scatter_dimension=1, tiled=True, axis_index_groups=outer_groups)

        def with_core(block, other):
            return (up(block) + up(other)).astype(BF)

        def together(*values):
            return lax.optimization_barrier(values)

        top, low = slice(0, half), slice(half, None)

        kept, back, out = expert_call(place, first_arrays + second_arrays, first_plan + second_plan, weights)
        core_xy, core_x, core_y = swap(back[1], 1), swap(back[3], 1), swap(back[7], 1)
        sum_xy = [with_core(back[0][part], core_xy[part]) for part in (top, low)]
        sum_xy, core_x, core_y, kept, back, out = together(sum_xy, core_x, core_y, kept, back, out)

        ug0, ug1, da0, da1, db0, db1, tokens_all, grads_all = kept
        grads_d, (sum_x, sum_y) = weight_grads(grads_all, [ug0, ug1], [(back[2], core_x), (back[6], core_y)])
        via_x, via_y, out_core = swap(sum_xy[0], 2), swap(sum_xy[1], 4), [swap(out[i], 1) for i in (1, 3, 7)]
        grads_d, sum_x, sum_y, via_x, via_y, out_core, kept, out, back = together(
            grads_d, sum_x, sum_y, via_x, via_y, out_core, kept, out, back
        )
        sums_d = outer_sum(grads_d)
        sum_y = with_core(sum_y, jnp.pad(via_x, ((0, sum_y.shape[0] - half), (0, 0))))
        sum_x = with_core(sum_x, jnp.pad(via_y, ((half, 0), (0, 0))))
        sum_x, sum_y, kept, back, out, out_core = together(sum_x, sum_y, kept, back, out, out_core)

        _, _, da0, da1, db0, db1, tokens_all, _ = kept
        grads_gu, (out_xy, out_x, out_y) = weight_grads(
            tokens_all,
            [da0, da1, db0, db1],
            [(out[0], out_core[0]), (out[2], out_core[1]), (out[6], out_core[2])],
        )
        got_x, got_y, core_own, out_core_own = swap(sum_x, 2), swap(sum_y, 4), swap(back[5], 1), swap(out[5], 1)
        grads_gu, got_x, got_y, core_own, out_core_own, out_xy, out_x, out_y, _ = together(
            grads_gu, got_x, got_y, core_own, out_core_own, out_xy, out_x, out_y, (first_arrays, second_arrays)
        )
        sums_gu = outer_sum(grads_gu)
        got = [back[4], core_own, got_x, got_y]
        got, out_x, out_y, out_xy = together(got, out_x, out_y, [out_xy[top], out_xy[low]])

        shapes, grad_places = grad_spots(share)
        input_grad, *grad_pieces = backward_call(
            me, got, tokens, r1, cotangent, h1, h2, dense, q, k, v, o, lse, seg_col, seg_row, cosine, sine,
            shapes, grad_places,
        )
        got_out = [swap(out_x, 2), swap(out_y, 4), swap(out_xy[0], 6)]
        input_grad, grad_pieces, got_out, out_xy = together(input_grad, grad_pieces, got_out, out_xy)
        got_out_low = swap(out_xy[1], 6)
        output = r1 + up(out[4]) + up(out_core_own) + up(got_out[0]) + up(got_out[1])
        output_top, output_low = (output[top] + up(got_out[2])).astype(BF), output[low]
        owned = jnp.concatenate([sums_d, sums_gu], axis=0).reshape(3 * MINE, PLANE, share, ff).transpose(1, 0, 2, 3)
        dense_grads = dense_sum(grad_pieces, (got_out_low, output_top, output_low))
        output = jnp.concatenate([output_top, (output_low + up(got_out_low)).astype(BF)], axis=0)
        owned = lax.all_to_all(owned, "dp", split_axis=0, concat_axis=0, axis_index_groups=plane_groups)

        def experts_of(kind):
            return up(owned[:, MINE * kind : MINE * (kind + 1)]).reshape(EXPERTS, share, ff)

        down_out, gate_out, up_out = experts_of(0).transpose(0, 2, 1), experts_of(1), experts_of(2)
        return (
            output,
            input_grad,
            dense_grads[:, :1024],
            dense_grads[:, 1024:1536],
            dense_grads[:, 1536:2048],
            dense_grads[:, 2048:3072].T,
            dense_grads[:, 3072 + EXPERTS],
            dense_grads[:, 3073 + EXPERTS],
            dense_grads[:, 3072 : 3072 + EXPERTS],
            gate_out,
            up_out,
            down_out,
        )

    return local


def solution(mesh):
    row, col, one = P("dp", None), P(None, "dp"), P("dp")
    middle, last = P(None, "dp", None), P(None, None, "dp")
    in_specs = (row, row, row, row, col, one, one, row, middle, middle, last, row, row, row)
    out_specs = (row, row, row, row, row, col, one, one, row, middle, middle, last)
    return jax.shard_map(
        make_local(mesh.shape["dp"]), mesh=mesh, in_specs=in_specs, out_specs=out_specs, check_vma=False
    )
```

```python
import functools

import jax
import jax.numpy as jnp
from jax import lax
from jax.experimental import pallas as pl
from jax.experimental.pallas import tpu as pltpu
from jax.sharding import PartitionSpec as P

EXPERTS = 16
PLANE = 8
MINE = EXPERTS // PLANE
HEADS = 16
HEAD_SIZE = 64
BLOCK = 128
MOST_DOC = 256
MIB = 2**20
VMEM_ROOM = 60 * MIB
SMALL = pl.CostEstimate(flops=1, bytes_accessed=1, transcendentals=0)
epsilon = 1e-06
neg_large = -1000000000.0
BF = jnp.bfloat16
F32 = jnp.float32


def dot(a, b, ca, cb):
    return lax.dot_general(a, b, (((ca,), (cb,)), ((), ())), preferred_element_type=F32)

def rms_scale(values):
    return lax.rsqrt(jnp.mean(values * values, axis=-1, keepdims=True) + epsilon)

def swap_halves(u):
    lane = lax.broadcasted_iota(jnp.int32, u.shape, 1)
    return jnp.where(lane % 64 < 32, pltpu.roll(u, u.shape[1] - 32, 1), pltpu.roll(u, 32, 1))

def crossed(u, w):
    lane = lax.broadcasted_iota(jnp.int32, u.shape, 1)
    return (
        jnp.where(lane < 64, u, pltpu.roll(w, 64, 1)),
        jnp.where(lane < 64, pltpu.roll(u, 64, 1), w),
    )


def key_range(rows, qb):
    end = (qb + 1) * BLOCK
    return max(0, end - BLOCK - MOST_DOC), end

def fill_mask(mask_ref, seg_col_ref, seg_row_ref, rows):
    for qb in range(rows // BLOCK):
        low, high = key_range(rows, qb)
        keys = low + lax.broadcasted_iota(jnp.int32, (high - low, BLOCK), 0)
        queries = qb * BLOCK + lax.broadcasted_iota(jnp.int32, (high - low, BLOCK), 1)
        same = seg_col_ref[low:high, :1] == seg_row_ref[:1, qb * BLOCK : (qb + 1) * BLOCK]
        mask_ref[qb, : high - low] = jnp.where(same & (keys <= queries), 1.0, 0.0)

def masked_scores(mask_ref, k_c, q_pair, qb, span):
    s = dot(k_c, q_pair, 1, 1)
    m = mask_ref[qb, :span]
    return jnp.where(jnp.concatenate([m, m], axis=1) > 0, s, neg_large)

def piece_copies(me_ref, spots, pieces, whole_ref, sems, inward):
    copies = []
    for ref, (offsets, first) in zip(pieces, spots):
        if offsets is None:
            sides = [(ref, whole_ref)]
        else:
            share, cols = ref.shape[1:]
            sides = []
            for i, offset in enumerate(offsets):
                row = pl.multiple_of((me_ref[0] ^ offset) * share, share)
                sides.append((ref.at[i], whole_ref.at[pl.ds(row, share), first : first + cols]))
        for part, place in sides:
            source, target = (part, place) if inward else (place, part)
            copies.append(pltpu.make_async_copy(source, target, sems.at[len(copies)]))
    return copies


def spot_columns(spots):
    return [first if offsets else -1 for offsets, first in spots for _ in (offsets or [None])]


def piece_count(spots):
    return sum(1 if offsets is None else len(offsets) for offsets, _ in spots)


def forward_kernel(spots, me_ref, x_ref, routes_ref, seg_col_ref, seg_row_ref, cos_ref, sin_ref, *refs):
    pieces, refs = refs[: len(spots)], refs[len(spots) :]
    lse_ref, h2_ref, *outs = refs[:9]
    mask_ref, w_ref, h1_ref, q_ref, k_ref, v_ref, o_ref, r1_ref, sems, out_sems = refs[9:]

    def leave(i, source):
        copy = pltpu.make_async_copy(source, outs[i], out_sems.at[i])
        copy.start()
        return copy

    copies = piece_copies(me_ref, spots, pieces, w_ref, sems, True)
    for copy in copies:
        copy.start()
    fill_mask(mask_ref, seg_col_ref, seg_row_ref, x_ref.shape[0])
    for copy in copies:
        copy.wait()
    leaving = [leave(0, w_ref)]
    rows, width = x_ref.shape
    x = x_ref[...].astype(F32)
    gains = w_ref[:, 3072:3200].astype(F32).T
    h1_ref[...] = (x * rms_scale(x) * gains[16:17]).astype(BF)
    leaving.append(leave(1, h1_ref))

    @pl.loop(0, 4)
    def _(j):
        qs = pl.ds(pl.multiple_of(j * 256, 256), 256)
        ks = pl.ds(pl.multiple_of(j * 128, 128), 128)
        vs = pl.ds(pl.multiple_of(1536 + j * 128, 128), 128)
        kw = pl.ds(pl.multiple_of(1024 + j * 128, 128), 128)
        h1 = h1_ref[...]
        cos, sin = cos_ref[...], sin_ref[...]
        q2 = dot(h1, w_ref[:, qs], 1, 0)
        qa, qb_ = crossed(q2[:, :128], q2[:, 128:])
        qa = (qa * cos + swap_halves(qa) * sin).astype(BF) * BF(0.125)
        qb_ = (qb_ * cos + swap_halves(qb_) * sin).astype(BF) * BF(0.125)
        k = dot(h1, w_ref[:, kw], 1, 0)
        k = (k * cos + swap_halves(k) * sin).astype(BF)
        v32 = dot(h1, w_ref[:, vs], 1, 0)
        v = v32.astype(BF)
        q_ref[:, qs] = jnp.concatenate([qa, qb_], axis=1)
        k_ref[:, ks] = k
        v_ref[:, ks] = v
        vt = v32.T.astype(BF)
        lane = lax.broadcasted_iota(jnp.int32, (rows, 128), 1)
        sub = lax.broadcasted_iota(jnp.int32, (128, rows), 0)
        outs = []
        for qb in range(rows // BLOCK):
            low, high = key_range(rows, qb)
            blk = slice(qb * BLOCK, (qb + 1) * BLOCK)
            q_pair = jnp.concatenate([qa[blk], qb_[blk]], axis=0)
            total = None
            for c in range(2):
                k_c = jnp.where(lane[low:high] // 64 == c, k[low:high], BF(0))
                vt_c = jnp.where(sub[:, low:high] // 64 == c, vt[:, low:high], BF(0))
                s = masked_scores(mask_ref, k_c, q_pair, qb, high - low)
                top = jnp.max(s, axis=0, keepdims=True)
                e = jnp.exp(s - top)
                norm = jnp.sum(e, axis=0, keepdims=True)
                p = (e * (1.0 / norm)).astype(BF)
                part = dot(vt_c, p, 1, 0)
                total = part if total is None else total + part
                lse = top + jnp.log(norm)
                lse_ref[j, c : c + 1, blk] = lse[:, :128]
                lse_ref[j, 2 + c : 3 + c, blk] = lse[:, 128:]
            outs.append(total)
        a = jnp.concatenate([t[:, :128] for t in outs], axis=1).T
        b = jnp.concatenate([t[:, 128:] for t in outs], axis=1).T
        o_ref[:, qs] = jnp.concatenate(crossed(a, b), axis=1).astype(BF)

    leaving += [leave(i, ref) for i, ref in ((2, q_ref), (3, k_ref), (4, v_ref), (5, o_ref))]
    r1 = x_ref[...].astype(F32) + dot(o_ref[...], w_ref[:, 2048:3072], 1, 1)
    r1_ref[...] = r1
    leaving.append(leave(6, r1_ref))
    h2 = (r1 * rms_scale(r1) * gains[17:18]).astype(BF)
    h2_ref[:rows] = h2
    logits = dot(h2, w_ref[:, 3072:3200], 1, 0).T[:EXPERTS]
    at = lax.broadcasted_iota(jnp.int32, (EXPERTS, rows), 0)
    chosen = at < 0
    for t in range(routes_ref.shape[0]):
        chosen = chosen | (at == routes_ref[t : t + 1])
    logits = jnp.where(chosen, logits, neg_large)
    ex = jnp.where(chosen, jnp.exp(logits - jnp.max(logits, axis=0, keepdims=True)), 0.0)
    gates = ex / jnp.sum(ex, axis=0, keepdims=True)
    high = gates.astype(BF)
    low = (gates - high.astype(F32)).astype(BF)
    h2_ref[rows:] = jnp.concatenate([high, low], axis=1)
    for copy in leaving:
        copy.wait()

def forward_call(me, x, routes, seg_col, seg_row, cos, sin, pieces, spots):
    rows, width = x.shape
    s = jax.ShapeDtypeStruct
    vmem, anywhere = pl.BlockSpec(memory_space=pltpu.VMEM), pl.BlockSpec(memory_space=pl.ANY)
    return pl.pallas_call(
        functools.partial(forward_kernel, spots),
        in_specs=[pl.BlockSpec(memory_space=pltpu.SMEM)] + [vmem] * 6 + [anywhere] * len(pieces),
        out_specs=[vmem] * 2 + [anywhere] * 7,
        out_shape=[
            s((4, 4, rows), F32),
            s((rows + EXPERTS, width), BF),
            s((width, 3200), BF),
            s((rows, width), BF),
            s((rows, 1024), BF),
            s((rows, 512), BF),
            s((rows, 512), BF),
            s((rows, 1024), BF),
            s((rows, width), F32),
        ],
        scratch_shapes=[
            pltpu.VMEM((rows // BLOCK, BLOCK + MOST_DOC, BLOCK), F32),
            pltpu.VMEM((width, 3200), BF),
            pltpu.VMEM((rows, width), BF),
            pltpu.VMEM((rows, 1024), BF),
            pltpu.VMEM((rows, 512), BF),
            pltpu.VMEM((rows, 512), BF),
            pltpu.VMEM((rows, 1024), BF),
            pltpu.VMEM((rows, width), F32),
            pltpu.SemaphoreType.DMA((piece_count(spots),)),
            pltpu.SemaphoreType.DMA((7,)),
        ],
        cost_estimate=SMALL,
        compiler_params=pltpu.CompilerParams(vmem_limit_bytes=VMEM_ROOM),
    )(me, x, routes, seg_col, seg_row, cos, sin, *pieces)


ARRIVING = 14


def backward_kernel(spots, me_ref, *refs):
    given, refs = refs[:ARRIVING], refs[ARRIVING:]
    lse_ref, seg_col_ref, seg_row_ref, cos_ref, sin_ref, ig_ref = refs[:6]
    pieces, refs = refs[6 : 6 + len(spots)], refs[6 + len(spots) :]
    held, refs = refs[:ARRIVING], refs[ARRIVING:]
    mask_ref, do_ref, dqkv_ref, dr1_ref, wg_ref, sems, in_sems = refs
    p0, p1, p2, p3, r1_ref, cot_ref, h2_ref, w_ref, o_ref, q_ref, k_ref, v_ref, h1_ref, x_ref = held
    parts = [(given[i], held[i]) for i in range(7)]
    for cols in (slice(3072, 3200), slice(2048, 3072), slice(0, 2048)):
        parts.append((given[7].at[:, cols], w_ref.at[:, cols]))
        if cols.start == 2048:
            parts += [(given[i], held[i]) for i in range(8, 12)]
    parts += [(given[12], h1_ref), (given[13], x_ref)]
    copies = [pltpu.make_async_copy(source, target, in_sems.at[i]) for i, (source, target) in enumerate(parts)]
    for copy in copies:
        copy.start()
    fill_mask(mask_ref, seg_col_ref, seg_row_ref, r1_ref.shape[0])
    for copy in copies[:8]:
        copy.wait()
    rows, width = x_ref.shape
    misc = w_ref[:, 3072:3200]
    gains = misc.astype(F32).T

    def up(ref, sl):
        return ref[sl].astype(F32)

    top, tail = slice(0, rows), slice(rows, rows + EXPERTS)
    dh2 = up(p0, top) + up(p1, top) + up(p2, top) + up(p3, top)
    dg = up(p0, tail) + up(p1, tail) + up(p2, tail) + up(p3, tail)
    dg = dg[:, :rows] + dg[:, rows:]
    gates = up(h2_ref, tail)
    gates = gates[:, :rows] + gates[:, rows:]
    h2 = h2_ref[:rows]
    dlog = gates * (dg - jnp.sum(gates * dg, axis=0, keepdims=True))
    dlog = jnp.concatenate([dlog, jnp.zeros((128 - EXPERTS, rows), F32)], axis=0).T.astype(BF)
    dh2 = dh2 + dot(dlog, misc, 1, 1)
    r1 = r1_ref[...]
    s2 = rms_scale(r1)
    w2 = dh2 * gains[17:18]
    gain2_grad = jnp.sum(dh2 * r1 * s2, axis=0, keepdims=True)
    dr1 = cot_ref[...].astype(F32) + s2 * w2 - r1 * (s2 * s2 * s2) * jnp.mean(w2 * r1, axis=-1, keepdims=True)
    dr1_ref[...] = dr1
    dz = dr1.astype(BF)
    for copy in copies[8:13]:
        copy.wait()
    wg_ref[:, 2048:3072] = dot(dz, o_ref[...], 0, 0).astype(BF)
    do_ref[...] = dot(dz, w_ref[:, 2048:3072], 1, 0).astype(BF)
    router_t = dot(dlog, h2, 0, 0)

    @pl.loop(0, 4)
    def _(j):
        qs = pl.ds(pl.multiple_of(j * 256, 256), 256)
        ks = pl.ds(pl.multiple_of(j * 128, 128), 128)
        vs = pl.ds(pl.multiple_of(1536 + j * 128, 128), 128)
        kw = pl.ds(pl.multiple_of(1024 + j * 128, 128), 128)
        cos, sin = cos_ref[...], sin_ref[...]
        def back(g):
            return g * cos - swap_halves(g) * sin
        q, k, v = q_ref[:, qs], k_ref[:, ks], v_ref[:, ks]
        do = do_ref[:, qs].astype(F32)
        do = jnp.concatenate(crossed(do[:, :128], do[:, 128:]), axis=1).astype(BF)
        kt = k.astype(F32).T.astype(BF)
        lane = lax.broadcasted_iota(jnp.int32, (rows, 128), 1)
        sub = lax.broadcasted_iota(jnp.int32, (128, rows), 0)
        dks = [jnp.zeros((BLOCK, 128), F32) for _ in range(rows // BLOCK)]
        dvs = [jnp.zeros((BLOCK, 128), F32) for _ in range(rows // BLOCK)]
        dqs = []
        for qb in range(rows // BLOCK):
            low, high = key_range(rows, qb)
            blk = slice(qb * BLOCK, (qb + 1) * BLOCK)
            q_pair = jnp.concatenate([q[blk, :128], q[blk, 128:]], axis=0)
            do_pair = jnp.concatenate([do[blk, :128], do[blk, 128:]], axis=0)
            dq_t = None
            for c in range(2):
                mine = lane[low:high] // 64 == c
                k_c = jnp.where(mine, k[low:high], BF(0))
                v_c = jnp.where(mine, v[low:high], BF(0))
                kt_c = jnp.where(sub[:, low:high] // 64 == c, kt[:, low:high], BF(0))
                s = masked_scores(mask_ref, k_c, q_pair, qb, high - low)
                lse = jnp.concatenate([lse_ref[j, c : c + 1, blk], lse_ref[j, 2 + c : 3 + c, blk]], axis=1)
                p = jnp.exp(s - lse)
                dp = dot(v_c, do_pair, 1, 1)
                inner = jnp.sum(p * dp, axis=0, keepdims=True)
                ds = (p * (dp - inner)).astype(BF)
                dk = dot(ds, q_pair, 1, 0)
                dv = dot(p.astype(BF), do_pair, 1, 0)
                t = dot(kt_c, ds, 1, 0)
                dq_t = t if dq_t is None else dq_t + t
                for i, kb in enumerate(range(low // BLOCK, high // BLOCK)):
                    sl = slice(i * BLOCK, (i + 1) * BLOCK)
                    dks[kb] = dks[kb] + jnp.where(mine[sl], dk[sl], 0.0)
                    dvs[kb] = dvs[kb] + jnp.where(mine[sl], dv[sl], 0.0)
            dqs.append(dq_t)
        dqa = jnp.concatenate([t[:, :128] for t in dqs], axis=1).T * 0.125
        dqb = jnp.concatenate([t[:, 128:] for t in dqs], axis=1).T * 0.125
        dqkv_ref[:, qs] = jnp.concatenate(crossed(back(dqa), back(dqb)), axis=1).astype(BF)
        dqkv_ref[:, kw] = back(jnp.concatenate(dks, axis=0)).astype(BF)
        dqkv_ref[:, vs] = jnp.concatenate(dvs, axis=0).astype(BF)

    for copy in copies[13:]:
        copy.wait()
    leaving = piece_copies(me_ref, spots, pieces, wg_ref, sems, False)
    wg_ref[:, :1536] = dot(h1_ref[...], dqkv_ref[:, :1536], 0, 0).astype(BF)
    early = [i for i, first in enumerate(spot_columns(spots)) if first == 0]
    for i in early:
        leaving[i].start()
    wg_ref[:, 1536:2048] = dot(h1_ref[...], dqkv_ref[:, 1536:], 0, 0).astype(BF)
    dh1 = dot(dqkv_ref[...], w_ref[:, :2048], 1, 1)
    x = x_ref[...].astype(F32)
    s1 = rms_scale(x)
    w1 = dh1 * gains[16:17]
    gain1_grad = jnp.sum(dh1 * x * s1, axis=0, keepdims=True)
    at = lax.broadcasted_iota(jnp.int32, (128, width), 0)
    misc_t = jnp.where(at == 16, gain1_grad, jnp.where(at == 17, gain2_grad, router_t))
    wg_ref[:, 3072:3200] = misc_t.T.astype(BF)
    for i in range(len(leaving)):
        if i not in early:
            leaving[i].start()
    ig_ref[...] = dr1_ref[...] + s1 * w1 - x * (s1 * s1 * s1) * jnp.mean(w1 * x, axis=-1, keepdims=True)
    for copy in leaving:
        copy.wait()


def backward_call(me, parts, x, r1, cot, h1, h2, w, q, k, v, o, lse, seg_col, seg_row, cos, sin, piece_shapes, spots):
    rows, width = x.shape
    s = jax.ShapeDtypeStruct
    vmem, anywhere = pl.BlockSpec(memory_space=pltpu.VMEM), pl.BlockSpec(memory_space=pl.ANY)
    arriving = [*parts, r1, cot, h2, w, o, q, k, v, h1, x]
    return pl.pallas_call(
        functools.partial(backward_kernel, spots),
        in_specs=[pl.BlockSpec(memory_space=pltpu.SMEM)] + [anywhere] * ARRIVING + [vmem] * 5,
        out_specs=[vmem] + [anywhere] * len(spots),
        out_shape=[s((rows, width), F32)] + [s(shape, BF) for shape in piece_shapes],
        scratch_shapes=[pltpu.VMEM(a.shape, a.dtype) for a in arriving]
        + [
            pltpu.VMEM((rows // BLOCK, BLOCK + MOST_DOC, BLOCK), F32),
            pltpu.VMEM((rows, 1024), BF),
            pltpu.VMEM((rows, 2048), BF),
            pltpu.VMEM((rows, width), F32),
            pltpu.VMEM((width, 3200), BF),
            pltpu.SemaphoreType.DMA((piece_count(spots),)),
            pltpu.SemaphoreType.DMA((ARRIVING + 2,)),
        ],
        cost_estimate=SMALL,
        compiler_params=pltpu.CompilerParams(vmem_limit_bytes=VMEM_ROOM),
    )(me, *arriving, lse, seg_col, seg_row, cos, sin)


def expert_kernel(plan, count, place_ref, *refs):
    blocks = len(plan)
    arrays, refs = refs[:count], refs[count:]
    w_refs = refs[:6]
    ug0, ug1, da0, da1, db0, db1, h_all, g_all = refs[6:14]
    backs, forths = refs[14 : 14 + blocks], refs[14 + blocks : 14 + 2 * blocks]
    h_buf, g_buf, back_buf, forth_buf, gates_buf, dg_buf, sems, out_sems = refs[14 + 2 * blocks :]
    rows = g_buf.shape[1]
    step = pl.program_id(0)
    slot = lax.rem(step, 2)

    def copies(i):
        found = []
        for buf, parts in ((h_buf, plan[i][0]), (g_buf, plan[i][1])):
            for array, start, size, at in parts:
                sem = sems.at[i % 2, len(found)]
                found.append(
                    pltpu.make_async_copy(
                        arrays[array].at[pl.ds(start, size)], buf.at[i % 2, pl.ds(at, size)], sem
                    )
                )
        return found

    def results(i):
        return (
            pltpu.make_async_copy(back_buf.at[i % 2], backs[i], out_sems.at[i % 2, 0]),
            pltpu.make_async_copy(forth_buf.at[i % 2], forths[i], out_sems.at[i % 2, 1]),
        )

    for i in range(blocks):

        @pl.when(step == i)
        def _(i=i):
            if i == 0:
                for copy in copies(0):
                    copy.start()
            if i + 1 < blocks:
                for copy in copies(i + 1):
                    copy.start()
            if i >= 2:
                for copy in results(i - 2):
                    copy.wait()
            for copy in copies(i):
                copy.wait()

    tail = h_buf[slot, rows:].astype(F32)
    tail = tail[:, :rows] + tail[:, rows:]
    gates_buf[...] = jnp.concatenate([tail, jnp.zeros((128 - EXPERTS, rows), F32)], axis=0).T
    place = place_ref[0]
    tile = rows // 2
    lane = lax.broadcasted_iota(jnp.int32, (tile, 128), 1)

    @pl.loop(0, 2)
    def _(r):
        part = pl.ds(pl.multiple_of(r * tile, tile), tile)
        h, g, gates = h_buf[slot, part], g_buf[slot, part], gates_buf[part]
        h_all[part], g_all[part] = h, g
        totals = []
        for e, (ug_ref, da_ref, db_ref) in enumerate(((ug0, da0, db0), (ug1, da1, db1))):
            wg_ref, wu_ref, wd_ref = w_refs[3 * e : 3 * e + 3]
            ff = wg_ref.shape[2]
            gate = jnp.sum(jnp.where(lane == place * MINE + e, gates, 0.0), axis=1, keepdims=True)
            total = 0.0
            for half in range(2):
                sl = slice(half * ff // 2, (half + 1) * ff // 2)
                a = dot(h, wg_ref[0, :, sl], 1, 0)
                b = dot(h, wu_ref[0, :, sl], 1, 0)
                gd = dot(g, wd_ref[0, :, sl], 1, 0)
                sigma = 0.5 * jnp.tanh(0.5 * a) + 0.5
                silu = a * sigma
                u = (silu * b).astype(BF).astype(F32)
                total = total + jnp.sum(u * gd, axis=1, keepdims=True)
                ug_ref[part, sl] = (u * gate).astype(BF)
                du = gd * gate
                db_ref[part, sl] = (du * silu).astype(BF)
                da_ref[part, sl] = (du * b * (sigma * (1.0 + a * (1.0 - sigma)))).astype(BF)
            totals.append(total)
        back = dot(da0[part], w_refs[0][0], 1, 1) + dot(db0[part], w_refs[1][0], 1, 1)
        back = back + dot(da1[part], w_refs[3][0], 1, 1) + dot(db1[part], w_refs[4][0], 1, 1)
        back_buf[slot, part] = back.astype(BF)
        forth = dot(ug0[part], w_refs[2][0], 1, 1) + dot(ug1[part], w_refs[5][0], 1, 1)
        forth_buf[slot, part] = forth.astype(BF)
        dg_buf[part] = jnp.where(lane == 0, totals[0], totals[1])

    dg = dg_buf[...].T
    at = lax.broadcasted_iota(jnp.int32, (EXPERTS, rows), 0)
    dg = jnp.where(at == place * MINE, dg[0:1], jnp.where(at == place * MINE + 1, dg[1:2], 0.0))
    high = dg.astype(BF)
    low = (dg - high.astype(F32)).astype(BF)
    back_buf[slot, rows:] = jnp.concatenate([high, low], axis=1)

    for i in range(blocks):

        @pl.when(step == i)
        def _(i=i):
            for copy in results(i):
                copy.start()
            if i == blocks - 1:
                for copy in (*results(i - 1), *results(i)):
                    copy.wait()


def expert_call(place, arrays, plan, weights):
    _, width, ff = weights.shape
    blocks = len(plan)
    rows = sum(piece[2] for piece in plan[0][1])
    most = max(len(h) + len(g) for h, g in plan)
    s = jax.ShapeDtypeStruct
    at = lambda i: (i, 0)
    anywhere = pl.BlockSpec(memory_space=pl.ANY)
    hidden, tile = pl.BlockSpec((rows, ff), at), pl.BlockSpec((rows, width), at)
    out = pl.pallas_call(
        functools.partial(expert_kernel, plan, len(arrays)),
        grid=(blocks,),
        in_specs=[pl.BlockSpec(memory_space=pltpu.SMEM)]
        + [anywhere] * len(arrays)
        + [pl.BlockSpec((1, width, ff), lambda i, k=k: (k, 0, 0), pipeline_mode=pl.Buffered(1)) for k in range(6)],
        out_specs=[hidden] * 6 + [tile] * 2 + [anywhere] * (2 * blocks),
        out_shape=[s((PLANE * rows, ff), BF)] * 6
        + [s((PLANE * rows, width), BF)] * 2
        + [s((rows + EXPERTS, width), BF)] * blocks
        + [s((rows, width), BF)] * blocks,
        scratch_shapes=[
            pltpu.VMEM((2, rows + EXPERTS, width), BF),
            pltpu.VMEM((2, rows, width), BF),
            pltpu.VMEM((2, rows + EXPERTS, width), BF),
            pltpu.VMEM((2, rows, width), BF),
            pltpu.VMEM((rows, 128), F32),
            pltpu.VMEM((rows, 128), F32),
            pltpu.SemaphoreType.DMA((2, most)),
            pltpu.SemaphoreType.DMA((2, 2)),
        ],
        cost_estimate=SMALL,
        compiler_params=pltpu.CompilerParams(vmem_limit_bytes=44 * MIB),
    )(place, *arrays, *[weights] * 6)
    return out[:8], out[8 : 8 + blocks], out[8 + blocks :]


STEPS = 4


def weight_grad_kernel(count, sums, sum_steps, left_ref, *refs):
    rights, refs = refs[:count], refs[count:]
    terms, refs = refs[: 2 * sums], refs[2 * sums :]
    out_ref, totals, acc_ref = refs[0], refs[1:-1], refs[-1]
    k = pl.program_id(0)
    ff = rights[0].shape[1]
    part = dot(left_ref[...], jnp.concatenate([r[...] for r in rights], axis=1), 0, 0)

    @pl.when(k < sum_steps)
    def _():
        for i in range(sums):
            totals[i][...] = (terms[2 * i][...].astype(F32) + terms[2 * i + 1][...].astype(F32)).astype(BF)

    @pl.when(k == 0)
    def _():
        acc_ref[...] = part

    @pl.when(k > 0)
    def _():
        acc_ref[...] += part

    @pl.when(k == STEPS - 1)
    def _():
        for t in range(count):
            out_ref[t] = acc_ref[:, t * ff : (t + 1) * ff].astype(BF)


def weight_grads(left, rights, pairs=()):
    total, width = left.shape
    ff = rights[0].shape[1]
    count = len(rights)
    step = total // STEPS
    row = lambda i: (i, 0)
    rows = pairs[0][0].shape[0] if pairs else 0
    sum_steps = next(n for n in (4, 3, 2, 1) if rows % (16 * n) == 0)
    tile = pl.BlockSpec((rows // sum_steps, width), lambda i: (jnp.minimum(i, sum_steps - 1), 0))
    s = jax.ShapeDtypeStruct
    out = pl.pallas_call(
        functools.partial(weight_grad_kernel, count, len(pairs), sum_steps),
        grid=(STEPS,),
        in_specs=[pl.BlockSpec((step, width), row)]
        + [pl.BlockSpec((step, ff), row)] * count
        + [tile] * (2 * len(pairs)),
        out_specs=[pl.BlockSpec((count, width, ff), lambda i: (0, 0, 0), pipeline_mode=pl.Buffered(1))]
        + [tile] * len(pairs),
        out_shape=[s((count, width, ff), BF)] + [s((rows, width), BF)] * len(pairs),
        scratch_shapes=[pltpu.VMEM((width, count * ff), F32)],
        cost_estimate=SMALL,
        compiler_params=pltpu.CompilerParams(vmem_limit_bytes=VMEM_ROOM),
    )(left, *rights, *[term for pair in pairs for term in pair])
    return out[0], out[1:]


def up(v):
    return v.astype(F32)


def after(value, *others):
    return lax.optimization_barrier((value, *others))[0]


CUT = 1536
COLUMNS = 3200


def make_local(n):
    outer = n // PLANE
    plane_groups = [[PLANE * z + i for i in range(PLANE)] for z in range(outer)]
    outer_groups = [[PLANE * z + i for z in range(outer)] for i in range(PLANE)]
    pieced = outer == 4

    def swap(array, offset):
        return lax.ppermute(array, "dp", [(i, i ^ offset) for i in range(n)])

    along_z = [PLANE * k for k in range(4)]

    def dense_gather(part, *earlier):
        if not pieced:
            return [lax.all_gather(part, "dp", axis=0, tiled=True)], [(None, 0)]
        line = after([part] + [swap(part, k) for k in along_z[1:]], *earlier)
        left, right = jnp.stack([t[:, :CUT] for t in line]), jnp.stack([t[:, CUT:] for t in line])
        left_x, right_y = swap(left, 2), swap(right, 4)
        left_y, right_x = swap(left, 4), swap(right, 2)
        left_xy, right_xy = swap(left_x, 4), swap(right_y, 2)
        found = [(left, 0, 0), (left_x, 2, 0), (left_y, 4, 0), (left_xy, 6, 0)]
        found += [(right, 0, CUT), (right_x, 2, CUT), (right_y, 4, CUT), (right_xy, 6, CUT)]
        found += [(swap(piece, 1), offset + 1, first) for piece, offset, first in found]
        return [f[0] for f in found], [([f[1] + k for k in along_z], f[2]) for f in found]

    def grad_spots(share):
        if not pieced:
            return [(n * share, COLUMNS)], [(None, 0)]
        shapes, spots = [], []
        for core in (1, 0):
            for major, minor, first, cols in ((2, 4, 0, CUT), (4, 2, CUT, COLUMNS - CUT)):
                for far in (0, major):
                    shapes.append((8, share, cols))
                    spots.append(([core + far + d + k for d in (0, minor) for k in along_z], first))
        return shapes, spots

    def dense_sum(pieces, earlier):
        if not pieced:
            return lax.psum_scatter(up(pieces[0]), "dp", scatter_dimension=0, tiled=True)

        def add(a, b):
            return (up(a) + up(b)).astype(BF)

        near_l, far_l, near_r, far_r = (add(keep, swap(sent, 1)) for sent, keep in zip(pieces[:4], pieces[4:]))
        far_l, far_r = after((far_l, far_r), earlier)
        got_l, got_r = swap(far_l, 2), swap(far_r, 4)
        sent_l, sent_r = add(near_l[4:], got_l[4:]), add(near_r[4:], got_r[4:])
        left = add(add(near_l[:4], got_l[:4]), swap(sent_l, 4))
        right = add(add(near_r[:4], got_r[:4]), swap(sent_r, 2))
        both = jnp.concatenate([left, right], axis=2)
        total = up(both[0])
        for k in range(1, 4):
            total = total + up(swap(both[k], PLANE * k))
        return total

    def both_cores(same_core):
        return [b for part in same_core for b in (part, swap(part, 1))]

    def local(
        tokens,
        query_weight,
        key_projection_weight,
        value_projection_weight,
        output_weight,
        first_gain,
        second_gain,
        router_weight,
        gate_weight,
        up_weight,
        down_weight,
        routes,
        segments,
        cotangent,
    ):
        rows, width = tokens.shape
        ff = gate_weight.shape[2]
        share = query_weight.shape[0]
        me = lax.axis_index("dp").astype(jnp.int32).reshape(1)
        place = lax.rem(me, PLANE)

        expert_part = jnp.stack(
            [w.reshape(PLANE, MINE, share, ff) for w in (gate_weight, up_weight, down_weight.transpose(0, 2, 1))],
            axis=2,
        )
        dense_part = jnp.concatenate(
            [
                query_weight,
                key_projection_weight,
                value_projection_weight,
                output_weight.T,
                router_weight,
                first_gain[:, None],
                second_gain[:, None],
                jnp.zeros((share, 128 - EXPERTS - 2), BF),
            ],
            axis=1,
        )
        dense_part = after(dense_part, expert_part)
        expert_part = lax.all_to_all(
            expert_part, "dp", split_axis=0, concat_axis=0, axis_index_groups=plane_groups
        )

        expert_part = expert_part.transpose(1, 2, 0, 3, 4).reshape(3 * MINE, PLANE * share, ff)
        weights = lax.all_gather(expert_part, "dp", axis=1, tiled=True, axis_index_groups=outer_groups)

        positions = jnp.arange(rows, dtype=F32)
        frequency = 10000.0 ** (-2.0 * jnp.arange(HEAD_SIZE // 2, dtype=F32) / HEAD_SIZE)
        angles = positions[:, None] * frequency[None, :]
        cosine, sine = jnp.cos(angles), jnp.sin(angles)
        cosine = jnp.concatenate([cosine] * 4, axis=1)
        sine = jnp.concatenate([-sine, sine, -sine, sine], axis=1)
        seg_col = segments.reshape(rows, 1)
        seg_row = segments.reshape(1, rows)

        half = rows // 2
        pieces, spots = dense_gather(dense_part, cosine, sine, seg_col, expert_part)
        late = after(cotangent, *pieces)
        cot_x, cot_y = swap(late, 2), swap(late, 4)

        lse, h2, dense, h1, q, k, v, o, r1 = forward_call(
            me, tokens, routes.T, seg_col, seg_row, cosine, sine, pieces, spots
        )
        h2 = after(h2, cot_x, cot_y)
        h2_x, h2_y, h2_core = swap(h2, 2), swap(h2, 4), swap(h2, 1)
        cot_core = swap(cotangent, 1)
        h2_x, h2_y, cot_x, cot_y = after((h2_x, h2_y, cot_x, cot_y), h2_core, cot_core)
        corner_x = swap(jnp.concatenate([h2_y[:half], cot_y[:half]], axis=0), 2)
        corner_y = swap(jnp.concatenate([h2_x[half:], cot_x[half:]], axis=0), 4)
        cores = [swap(t, 1) for t in (h2_x, cot_x, h2_y, cot_y)]
        corner_x, corner_y = after((corner_x, corner_y), *cores)
        long = rows + EXPERTS

        def pieces_of(h, g):
            return ([(h, 0, long, 0)], [(g, 0, rows, 0)])

        first_arrays = [corner_x, swap(corner_x, 1), corner_y, swap(corner_y, 1), h2_x, cores[0], cot_x, cores[1]]
        first_plan = [
            (
                [(i, 0, half, 0), (i + 2, 0, long - half, half)],
                [(i, half, half, 0), (i + 2, long - half, half, half)],
            )
            for i in range(2)
        ]
        first_plan += [pieces_of(i, 2 + i) for i in (4, 5)]
        second_arrays = [h2, h2_core, h2_y, cores[2], cotangent, cot_core, cot_y, cores[3]]
        second_plan = [pieces_of(8 + i, 12 + i) for i in range(4)]

        def outer_sum(grads):
            if not pieced:
                grads = up(grads)
            return lax.psum_scatter(grads, "dp", scatter_dimension=1, tiled=True, axis_index_groups=outer_groups)

        def with_core(block, other):
            return (up(block) + up(other)).astype(BF)

        def together(*values):
            return lax.optimization_barrier(values)

        top, low = slice(0, half), slice(half, None)

        kept, back, out = expert_call(place, first_arrays + second_arrays, first_plan + second_plan, weights)
        core_xy, core_x, core_y = swap(back[1], 1), swap(back[3], 1), swap(back[7], 1)
        sum_xy = [with_core(back[0][part], core_xy[part]) for part in (top, low)]
        sum_xy, core_x, core_y, kept, back, out = together(sum_xy, core_x, core_y, kept, back, out)

        ug0, ug1, da0, da1, db0, db1, tokens_all, grads_all = kept
        grads_d, (sum_x, sum_y) = weight_grads(grads_all, [ug0, ug1], [(back[2], core_x), (back[6], core_y)])
        via_x, via_y, out_core = swap(sum_xy[0], 2), swap(sum_xy[1], 4), [swap(out[i], 1) for i in (1, 3, 7)]
        grads_d, sum_x, sum_y, via_x, via_y, out_core, kept, out, back = together(
            grads_d, sum_x, sum_y, via_x, via_y, out_core, kept, out, back
        )
        sums_d = outer_sum(grads_d)
        sum_y = with_core(sum_y, jnp.pad(via_x, ((0, sum_y.shape[0] - half), (0, 0))))
        sum_x = with_core(sum_x, jnp.pad(via_y, ((half, 0), (0, 0))))
        sum_x, sum_y, kept, back, out, out_core = together(sum_x, sum_y, kept, back, out, out_core)

        _, _, da0, da1, db0, db1, tokens_all, _ = kept
        grads_gu, (out_xy, out_x, out_y) = weight_grads(
            tokens_all,
            [da0, da1, db0, db1],
            [(out[0], out_core[0]), (out[2], out_core[1]), (out[6], out_core[2])],
        )
        got_x, got_y, core_own, out_core_own = swap(sum_x, 2), swap(sum_y, 4), swap(back[5], 1), swap(out[5], 1)
        grads_gu, got_x, got_y, core_own, out_core_own, out_xy, out_x, out_y, _ = together(
            grads_gu, got_x, got_y, core_own, out_core_own, out_xy, out_x, out_y, (first_arrays, second_arrays)
        )
        sums_gu = outer_sum(grads_gu)
        got = [back[4], core_own, got_x, got_y]
        got, out_x, out_y, out_xy = together(got, out_x, out_y, [out_xy[top], out_xy[low]])

        shapes, grad_places = grad_spots(share)
        input_grad, *grad_pieces = backward_call(
            me, got, tokens, r1, cotangent, h1, h2, dense, q, k, v, o, lse, seg_col, seg_row, cosine, sine,
            shapes, grad_places,
        )
        got_out = [swap(out_x, 2), swap(out_y, 4), swap(out_xy[0], 6)]
        input_grad, grad_pieces, got_out, out_xy = together(input_grad, grad_pieces, got_out, out_xy)
        got_out_low = swap(out_xy[1], 6)
        output = r1 + up(out[4]) + up(out_core_own) + up(got_out[0]) + up(got_out[1])
        output_top, output_low = (output[top] + up(got_out[2])).astype(BF), output[low]
        owned = jnp.concatenate([sums_d, sums_gu], axis=0).reshape(3 * MINE, PLANE, share, ff).transpose(1, 0, 2, 3)
        dense_grads = dense_sum(grad_pieces, (got_out_low, output_top, output_low))
        output = jnp.concatenate([output_top, (output_low + up(got_out_low)).astype(BF)], axis=0)
        owned = lax.all_to_all(owned, "dp", split_axis=0, concat_axis=0, axis_index_groups=plane_groups)

        def experts_of(kind):
            return up(owned[:, MINE * kind : MINE * (kind + 1)]).reshape(EXPERTS, share, ff)

        down_out, gate_out, up_out = experts_of(0).transpose(0, 2, 1), experts_of(1), experts_of(2)
        return (
            output,
            input_grad,
            dense_grads[:, :1024],
            dense_grads[:, 1024:1536],
            dense_grads[:, 1536:2048],
            dense_grads[:, 2048:3072].T,
            dense_grads[:, 3072 + EXPERTS],
            dense_grads[:, 3073 + EXPERTS],
            dense_grads[:, 3072 : 3072 + EXPERTS],
            gate_out,
            up_out,
            down_out,
        )

    return local


def solution(mesh):
    row, col, one = P("dp", None), P(None, "dp"), P("dp")
    middle, last = P(None, "dp", None), P(None, None, "dp")
    in_specs = (row, row, row, row, col, one, one, row, middle, middle, last, row, row, row)
    out_specs = (row, row, row, row, row, col, one, one, row, middle, middle, last)
    return jax.shard_map(
        make_local(mesh.shape["dp"]), mesh=mesh, in_specs=in_specs, out_specs=out_specs, check_vma=False
    )
```

```python
import functools

import jax
import jax.numpy as jnp
from jax import lax
from jax.experimental import pallas as pl
from jax.experimental.pallas import tpu as pltpu
from jax.sharding import PartitionSpec as P

EXPERTS = 16
PLANE = 8
MINE = EXPERTS // PLANE
HEADS = 16
HEAD_SIZE = 64
BLOCK = 128
MOST_DOC = 256
MIB = 2**20
VMEM_ROOM = 60 * MIB
SMALL = pl.CostEstimate(flops=1, bytes_accessed=1, transcendentals=0)
epsilon = 1e-06
neg_large = -1000000000.0
BF = jnp.bfloat16
F32 = jnp.float32


def dot(a, b, ca, cb):
    return lax.dot_general(a, b, (((ca,), (cb,)), ((), ())), preferred_element_type=F32)

def rms_scale(values):
    return lax.rsqrt(jnp.mean(values * values, axis=-1, keepdims=True) + epsilon)

def swap_halves(u):
    lane = lax.broadcasted_iota(jnp.int32, u.shape, 1)
    return jnp.where(lane % 64 < 32, pltpu.roll(u, u.shape[1] - 32, 1), pltpu.roll(u, 32, 1))

def crossed(u, w):
    lane = lax.broadcasted_iota(jnp.int32, u.shape, 1)
    return (
        jnp.where(lane < 64, u, pltpu.roll(w, 64, 1)),
        jnp.where(lane < 64, pltpu.roll(u, 64, 1), w),
    )


def key_range(rows, qb):
    end = (qb + 1) * BLOCK
    return max(0, end - BLOCK - MOST_DOC), end

def fill_mask(mask_ref, seg_col_ref, seg_row_ref, rows):
    for qb in range(rows // BLOCK):
        low, high = key_range(rows, qb)
        keys = low + lax.broadcasted_iota(jnp.int32, (high - low, BLOCK), 0)
        queries = qb * BLOCK + lax.broadcasted_iota(jnp.int32, (high - low, BLOCK), 1)
        same = seg_col_ref[low:high, :1] == seg_row_ref[:1, qb * BLOCK : (qb + 1) * BLOCK]
        mask_ref[qb, : high - low] = jnp.where(same & (keys <= queries), 1.0, 0.0)

def masked_scores(mask_ref, k_c, q_pair, qb, span):
    s = dot(k_c, q_pair, 1, 1)
    m = mask_ref[qb, :span]
    return jnp.where(jnp.concatenate([m, m], axis=1) > 0, s, neg_large)

def piece_copies(me_ref, spots, pieces, whole_ref, sems, inward):
    copies = []
    for ref, (offsets, first) in zip(pieces, spots):
        if offsets is None:
            sides = [(ref, whole_ref)]
        else:
            share, cols = ref.shape[1:]
            sides = []
            for i, offset in enumerate(offsets):
                row = pl.multiple_of((me_ref[0] ^ offset) * share, share)
                sides.append((ref.at[i], whole_ref.at[pl.ds(row, share), first : first + cols]))
        for part, place in sides:
            source, target = (part, place) if inward else (place, part)
            copies.append(pltpu.make_async_copy(source, target, sems.at[len(copies)]))
    return copies


def spot_columns(spots):
    return [first if offsets else -1 for offsets, first in spots for _ in (offsets or [None])]


def piece_count(spots):
    return sum(1 if offsets is None else len(offsets) for offsets, _ in spots)


def forward_kernel(spots, me_ref, x_ref, routes_ref, seg_col_ref, seg_row_ref, cos_ref, sin_ref, *refs):
    pieces, refs = refs[: len(spots)], refs[len(spots) :]
    lse_ref, h2_ref, *outs = refs[:9]
    mask_ref, w_ref, h1_ref, q_ref, k_ref, v_ref, o_ref, r1_ref, sems, out_sems = refs[9:]

    def leave(i, source):
        copy = pltpu.make_async_copy(source, outs[i], out_sems.at[i])
        copy.start()
        return copy

    copies = piece_copies(me_ref, spots, pieces, w_ref, sems, True)
    for copy in copies:
        copy.start()
    fill_mask(mask_ref, seg_col_ref, seg_row_ref, x_ref.shape[0])
    for copy in copies:
        copy.wait()
    leaving = [leave(0, w_ref)]
    rows, width = x_ref.shape
    x = x_ref[...].astype(F32)
    gains = w_ref[:, 3072:3200].astype(F32).T
    h1_ref[...] = (x * rms_scale(x) * gains[16:17]).astype(BF)
    leaving.append(leave(1, h1_ref))

    @pl.loop(0, 4)
    def _(j):
        qs = pl.ds(pl.multiple_of(j * 256, 256), 256)
        ks = pl.ds(pl.multiple_of(j * 128, 128), 128)
        vs = pl.ds(pl.multiple_of(1536 + j * 128, 128), 128)
        kw = pl.ds(pl.multiple_of(1024 + j * 128, 128), 128)
        h1 = h1_ref[...]
        cos, sin = cos_ref[...], sin_ref[...]
        q2 = dot(h1, w_ref[:, qs], 1, 0)
        qa, qb_ = crossed(q2[:, :128], q2[:, 128:])
        qa = (qa * cos + swap_halves(qa) * sin).astype(BF) * BF(0.125)
        qb_ = (qb_ * cos + swap_halves(qb_) * sin).astype(BF) * BF(0.125)
        k = dot(h1, w_ref[:, kw], 1, 0)
        k = (k * cos + swap_halves(k) * sin).astype(BF)
        v32 = dot(h1, w_ref[:, vs], 1, 0)
        v = v32.astype(BF)
        q_ref[:, qs] = jnp.concatenate([qa, qb_], axis=1)
        k_ref[:, ks] = k
        v_ref[:, ks] = v
        vt = v32.T.astype(BF)
        lane = lax.broadcasted_iota(jnp.int32, (rows, 128), 1)
        sub = lax.broadcasted_iota(jnp.int32, (128, rows), 0)
        outs = []
        for qb in range(rows // BLOCK):
            low, high = key_range(rows, qb)
            blk = slice(qb * BLOCK, (qb + 1) * BLOCK)
            q_pair = jnp.concatenate([qa[blk], qb_[blk]], axis=0)
            total = None
            for c in range(2):
                k_c = jnp.where(lane[low:high] // 64 == c, k[low:high], BF(0))
                vt_c = jnp.where(sub[:, low:high] // 64 == c, vt[:, low:high], BF(0))
                s = masked_scores(mask_ref, k_c, q_pair, qb, high - low)
                top = jnp.max(s, axis=0, keepdims=True)
                e = jnp.exp(s - top)
                norm = jnp.sum(e, axis=0, keepdims=True)
                p = (e * (1.0 / norm)).astype(BF)
                part = dot(vt_c, p, 1, 0)
                total = part if total is None else total + part
                lse = top + jnp.log(norm)
                lse_ref[j, c : c + 1, blk] = lse[:, :128]
                lse_ref[j, 2 + c : 3 + c, blk] = lse[:, 128:]
            outs.append(total)
        a = jnp.concatenate([t[:, :128] for t in outs], axis=1).T
        b = jnp.concatenate([t[:, 128:] for t in outs], axis=1).T
        o_ref[:, qs] = jnp.concatenate(crossed(a, b), axis=1).astype(BF)

    leaving += [leave(i, ref) for i, ref in ((2, q_ref), (3, k_ref), (4, v_ref), (5, o_ref))]
    r1 = x_ref[...].astype(F32) + dot(o_ref[...], w_ref[:, 2048:3072], 1, 1)
    r1_ref[...] = r1
    leaving.append(leave(6, r1_ref))
    h2 = (r1 * rms_scale(r1) * gains[17:18]).astype(BF)
    h2_ref[:rows] = h2
    logits = dot(h2, w_ref[:, 3072:3200], 1, 0).T[:EXPERTS]
    at = lax.broadcasted_iota(jnp.int32, (EXPERTS, rows), 0)
    chosen = at < 0
    for t in range(routes_ref.shape[0]):
        chosen = chosen | (at == routes_ref[t : t + 1])
    logits = jnp.where(chosen, logits, neg_large)
    ex = jnp.where(chosen, jnp.exp(logits - jnp.max(logits, axis=0, keepdims=True)), 0.0)
    gates = ex / jnp.sum(ex, axis=0, keepdims=True)
    high = gates.astype(BF)
    low = (gates - high.astype(F32)).astype(BF)
    h2_ref[rows:] = jnp.concatenate([high, low], axis=1)
    for copy in leaving:
        copy.wait()

def forward_call(me, x, routes, seg_col, seg_row, cos, sin, pieces, spots):
    rows, width = x.shape
    s = jax.ShapeDtypeStruct
    vmem, anywhere = pl.BlockSpec(memory_space=pltpu.VMEM), pl.BlockSpec(memory_space=pl.ANY)
    return pl.pallas_call(
        functools.partial(forward_kernel, spots),
        in_specs=[pl.BlockSpec(memory_space=pltpu.SMEM)] + [vmem] * 6 + [anywhere] * len(pieces),
        out_specs=[vmem] * 2 + [anywhere] * 7,
        out_shape=[
            s((4, 4, rows), F32),
            s((rows + EXPERTS, width), BF),
            s((width, 3200), BF),
            s((rows, width), BF),
            s((rows, 1024), BF),
            s((rows, 512), BF),
            s((rows, 512), BF),
            s((rows, 1024), BF),
            s((rows, width), F32),
        ],
        scratch_shapes=[
            pltpu.VMEM((rows // BLOCK, BLOCK + MOST_DOC, BLOCK), F32),
            pltpu.VMEM((width, 3200), BF),
            pltpu.VMEM((rows, width), BF),
            pltpu.VMEM((rows, 1024), BF),
            pltpu.VMEM((rows, 512), BF),
            pltpu.VMEM((rows, 512), BF),
            pltpu.VMEM((rows, 1024), BF),
            pltpu.VMEM((rows, width), F32),
            pltpu.SemaphoreType.DMA((piece_count(spots),)),
            pltpu.SemaphoreType.DMA((7,)),
        ],
        cost_estimate=SMALL,
        compiler_params=pltpu.CompilerParams(vmem_limit_bytes=VMEM_ROOM),
    )(me, x, routes, seg_col, seg_row, cos, sin, *pieces)


ARRIVING = 14


def backward_kernel(spots, me_ref, *refs):
    given, refs = refs[:ARRIVING], refs[ARRIVING:]
    lse_ref, seg_col_ref, seg_row_ref, cos_ref, sin_ref, ig_ref = refs[:6]
    pieces, refs = refs[6 : 6 + len(spots)], refs[6 + len(spots) :]
    held, refs = refs[:ARRIVING], refs[ARRIVING:]
    mask_ref, do_ref, dqkv_ref, dr1_ref, wg_ref, sems, in_sems = refs
    p0, p1, p2, p3, r1_ref, cot_ref, h2_ref, w_ref, o_ref, q_ref, k_ref, v_ref, h1_ref, x_ref = held
    parts = [(given[i], held[i]) for i in range(7)]
    for cols in (slice(3072, 3200), slice(2048, 3072), slice(0, 2048)):
        parts.append((given[7].at[:, cols], w_ref.at[:, cols]))
        if cols.start == 2048:
            parts += [(given[i], held[i]) for i in range(8, 12)]
    parts += [(given[12], h1_ref), (given[13], x_ref)]
    copies = [pltpu.make_async_copy(source, target, in_sems.at[i]) for i, (source, target) in enumerate(parts)]
    for copy in copies:
        copy.start()
    fill_mask(mask_ref, seg_col_ref, seg_row_ref, r1_ref.shape[0])
    for copy in copies[:8]:
        copy.wait()
    rows, width = x_ref.shape
    misc = w_ref[:, 3072:3200]
    gains = misc.astype(F32).T

    def up(ref, sl):
        return ref[sl].astype(F32)

    top, tail = slice(0, rows), slice(rows, rows + EXPERTS)
    dh2 = up(p0, top) + up(p1, top) + up(p2, top) + up(p3, top)
    dg = up(p0, tail) + up(p1, tail) + up(p2, tail) + up(p3, tail)
    dg = dg[:, :rows] + dg[:, rows:]
    gates = up(h2_ref, tail)
    gates = gates[:, :rows] + gates[:, rows:]
    h2 = h2_ref[:rows]
    dlog = gates * (dg - jnp.sum(gates * dg, axis=0, keepdims=True))
    dlog = jnp.concatenate([dlog, jnp.zeros((128 - EXPERTS, rows), F32)], axis=0).T.astype(BF)
    dh2 = dh2 + dot(dlog, misc, 1, 1)
    r1 = r1_ref[...]
    s2 = rms_scale(r1)
    w2 = dh2 * gains[17:18]
    gain2_grad = jnp.sum(dh2 * r1 * s2, axis=0, keepdims=True)
    dr1 = cot_ref[...].astype(F32) + s2 * w2 - r1 * (s2 * s2 * s2) * jnp.mean(w2 * r1, axis=-1, keepdims=True)
    dr1_ref[...] = dr1
    dz = dr1.astype(BF)
    for copy in copies[8:13]:
        copy.wait()
    wg_ref[:, 2048:3072] = dot(dz, o_ref[...], 0, 0).astype(BF)
    do_ref[...] = dot(dz, w_ref[:, 2048:3072], 1, 0).astype(BF)
    router_t = dot(dlog, h2, 0, 0)

    @pl.loop(0, 4)
    def _(j):
        qs = pl.ds(pl.multiple_of(j * 256, 256), 256)
        ks = pl.ds(pl.multiple_of(j * 128, 128), 128)
        vs = pl.ds(pl.multiple_of(1536 + j * 128, 128), 128)
        kw = pl.ds(pl.multiple_of(1024 + j * 128, 128), 128)
        cos, sin = cos_ref[...], sin_ref[...]
        def back(g):
            return g * cos - swap_halves(g) * sin
        q, k, v = q_ref[:, qs], k_ref[:, ks], v_ref[:, ks]
        do = do_ref[:, qs].astype(F32)
        do = jnp.concatenate(crossed(do[:, :128], do[:, 128:]), axis=1).astype(BF)
        kt = k.astype(F32).T.astype(BF)
        lane = lax.broadcasted_iota(jnp.int32, (rows, 128), 1)
        sub = lax.broadcasted_iota(jnp.int32, (128, rows), 0)
        dks = [jnp.zeros((BLOCK, 128), F32) for _ in range(rows // BLOCK)]
        dvs = [jnp.zeros((BLOCK, 128), F32) for _ in range(rows // BLOCK)]
        dqs = []
        for qb in range(rows // BLOCK):
            low, high = key_range(rows, qb)
            blk = slice(qb * BLOCK, (qb + 1) * BLOCK)
            q_pair = jnp.concatenate([q[blk, :128], q[blk, 128:]], axis=0)
            do_pair = jnp.concatenate([do[blk, :128], do[blk, 128:]], axis=0)
            dq_t = None
            for c in range(2):
                mine = lane[low:high] // 64 == c
                k_c = jnp.where(mine, k[low:high], BF(0))
                v_c = jnp.where(mine, v[low:high], BF(0))
                kt_c = jnp.where(sub[:, low:high] // 64 == c, kt[:, low:high], BF(0))
                s = masked_scores(mask_ref, k_c, q_pair, qb, high - low)
                lse = jnp.concatenate([lse_ref[j, c : c + 1, blk], lse_ref[j, 2 + c : 3 + c, blk]], axis=1)
                p = jnp.exp(s - lse)
                dp = dot(v_c, do_pair, 1, 1)
                inner = jnp.sum(p * dp, axis=0, keepdims=True)
                ds = (p * (dp - inner)).astype(BF)
                dk = dot(ds, q_pair, 1, 0)
                dv = dot(p.astype(BF), do_pair, 1, 0)
                t = dot(kt_c, ds, 1, 0)
                dq_t = t if dq_t is None else dq_t + t
                for i, kb in enumerate(range(low // BLOCK, high // BLOCK)):
                    sl = slice(i * BLOCK, (i + 1) * BLOCK)
                    dks[kb] = dks[kb] + jnp.where(mine[sl], dk[sl], 0.0)
                    dvs[kb] = dvs[kb] + jnp.where(mine[sl], dv[sl], 0.0)
            dqs.append(dq_t)
        dqa = jnp.concatenate([t[:, :128] for t in dqs], axis=1).T * 0.125
        dqb = jnp.concatenate([t[:, 128:] for t in dqs], axis=1).T * 0.125
        dqkv_ref[:, qs] = jnp.concatenate(crossed(back(dqa), back(dqb)), axis=1).astype(BF)
        dqkv_ref[:, kw] = back(jnp.concatenate(dks, axis=0)).astype(BF)
        dqkv_ref[:, vs] = jnp.concatenate(dvs, axis=0).astype(BF)

    for copy in copies[13:]:
        copy.wait()
    leaving = piece_copies(me_ref, spots, pieces, wg_ref, sems, False)
    wg_ref[:, :1536] = dot(h1_ref[...], dqkv_ref[:, :1536], 0, 0).astype(BF)
    early = [i for i, first in enumerate(spot_columns(spots)) if first == 0]
    for i in early:
        leaving[i].start()
    wg_ref[:, 1536:2048] = dot(h1_ref[...], dqkv_ref[:, 1536:], 0, 0).astype(BF)
    dh1 = dot(dqkv_ref[...], w_ref[:, :2048], 1, 1)
    x = x_ref[...].astype(F32)
    s1 = rms_scale(x)
    w1 = dh1 * gains[16:17]
    gain1_grad = jnp.sum(dh1 * x * s1, axis=0, keepdims=True)
    at = lax.broadcasted_iota(jnp.int32, (128, width), 0)
    misc_t = jnp.where(at == 16, gain1_grad, jnp.where(at == 17, gain2_grad, router_t))
    wg_ref[:, 3072:3200] = misc_t.T.astype(BF)
    for i in range(len(leaving)):
        if i not in early:
            leaving[i].start()
    ig_ref[...] = dr1_ref[...] + s1 * w1 - x * (s1 * s1 * s1) * jnp.mean(w1 * x, axis=-1, keepdims=True)
    for copy in leaving:
        copy.wait()


def backward_call(me, parts, x, r1, cot, h1, h2, w, q, k, v, o, lse, seg_col, seg_row, cos, sin, piece_shapes, spots):
    rows, width = x.shape
    s = jax.ShapeDtypeStruct
    vmem, anywhere = pl.BlockSpec(memory_space=pltpu.VMEM), pl.BlockSpec(memory_space=pl.ANY)
    arriving = [*parts, r1, cot, h2, w, o, q, k, v, h1, x]
    return pl.pallas_call(
        functools.partial(backward_kernel, spots),
        in_specs=[pl.BlockSpec(memory_space=pltpu.SMEM)] + [anywhere] * ARRIVING + [vmem] * 5,
        out_specs=[vmem] + [anywhere] * len(spots),
        out_shape=[s((rows, width), F32)] + [s(shape, BF) for shape in piece_shapes],
        scratch_shapes=[pltpu.VMEM(a.shape, a.dtype) for a in arriving]
        + [
            pltpu.VMEM((rows // BLOCK, BLOCK + MOST_DOC, BLOCK), F32),
            pltpu.VMEM((rows, 1024), BF),
            pltpu.VMEM((rows, 2048), BF),
            pltpu.VMEM((rows, width), F32),
            pltpu.VMEM((width, 3200), BF),
            pltpu.SemaphoreType.DMA((piece_count(spots),)),
            pltpu.SemaphoreType.DMA((ARRIVING + 2,)),
        ],
        cost_estimate=SMALL,
        compiler_params=pltpu.CompilerParams(vmem_limit_bytes=VMEM_ROOM),
    )(me, *arriving, lse, seg_col, seg_row, cos, sin)


def expert_kernel(plan, count, place_ref, *refs):
    blocks = len(plan)
    arrays, refs = refs[:count], refs[count:]
    w_refs = refs[:6]
    ug0, ug1, da0, da1, db0, db1, h_all, g_all = refs[6:14]
    backs, forths = refs[14 : 14 + blocks], refs[14 + blocks : 14 + 2 * blocks]
    h_buf, g_buf, back_buf, forth_buf, gates_buf, dg_buf, sems, out_sems = refs[14 + 2 * blocks :]
    rows = g_buf.shape[1]
    step = pl.program_id(0)
    slot = lax.rem(step, 2)

    def copies(i):
        found = []
        for buf, parts in ((h_buf, plan[i][0]), (g_buf, plan[i][1])):
            for array, start, size, at in parts:
                sem = sems.at[i % 2, len(found)]
                found.append(
                    pltpu.make_async_copy(
                        arrays[array].at[pl.ds(start, size)], buf.at[i % 2, pl.ds(at, size)], sem
                    )
                )
        return found

    def results(i):
        return (
            pltpu.make_async_copy(back_buf.at[i % 2], backs[i], out_sems.at[i % 2, 0]),
            pltpu.make_async_copy(forth_buf.at[i % 2], forths[i], out_sems.at[i % 2, 1]),
        )

    for i in range(blocks):

        @pl.when(step == i)
        def _(i=i):
            if i == 0:
                for copy in copies(0):
                    copy.start()
            if i + 1 < blocks:
                for copy in copies(i + 1):
                    copy.start()
            if i >= 2:
                for copy in results(i - 2):
                    copy.wait()
            for copy in copies(i):
                copy.wait()

    tail = h_buf[slot, rows:].astype(F32)
    tail = tail[:, :rows] + tail[:, rows:]
    gates_buf[...] = jnp.concatenate([tail, jnp.zeros((128 - EXPERTS, rows), F32)], axis=0).T
    place = place_ref[0]
    tile = rows // 2
    lane = lax.broadcasted_iota(jnp.int32, (tile, 128), 1)

    @pl.loop(0, 2)
    def _(r):
        part = pl.ds(pl.multiple_of(r * tile, tile), tile)
        h, g, gates = h_buf[slot, part], g_buf[slot, part], gates_buf[part]
        h_all[part], g_all[part] = h, g
        totals = []
        for e, (ug_ref, da_ref, db_ref) in enumerate(((ug0, da0, db0), (ug1, da1, db1))):
            wg_ref, wu_ref, wd_ref = w_refs[3 * e : 3 * e + 3]
            ff = wg_ref.shape[2]
            gate = jnp.sum(jnp.where(lane == place * MINE + e, gates, 0.0), axis=1, keepdims=True)
            total = 0.0
            for half in range(2):
                sl = slice(half * ff // 2, (half + 1) * ff // 2)
                a = dot(h, wg_ref[0, :, sl], 1, 0)
                b = dot(h, wu_ref[0, :, sl], 1, 0)
                gd = dot(g, wd_ref[0, :, sl], 1, 0)
                sigma = 0.5 * jnp.tanh(0.5 * a) + 0.5
                silu = a * sigma
                u = (silu * b).astype(BF).astype(F32)
                total = total + jnp.sum(u * gd, axis=1, keepdims=True)
                ug_ref[part, sl] = (u * gate).astype(BF)
                du = gd * gate
                db_ref[part, sl] = (du * silu).astype(BF)
                da_ref[part, sl] = (du * b * (sigma * (1.0 + a * (1.0 - sigma)))).astype(BF)
            totals.append(total)
        back = dot(da0[part], w_refs[0][0], 1, 1) + dot(db0[part], w_refs[1][0], 1, 1)
        back = back + dot(da1[part], w_refs[3][0], 1, 1) + dot(db1[part], w_refs[4][0], 1, 1)
        back_buf[slot, part] = back.astype(BF)
        forth = dot(ug0[part], w_refs[2][0], 1, 1) + dot(ug1[part], w_refs[5][0], 1, 1)
        forth_buf[slot, part] = forth.astype(BF)
        dg_buf[part] = jnp.where(lane == 0, totals[0], totals[1])

    dg = dg_buf[...].T
    at = lax.broadcasted_iota(jnp.int32, (EXPERTS, rows), 0)
    dg = jnp.where(at == place * MINE, dg[0:1], jnp.where(at == place * MINE + 1, dg[1:2], 0.0))
    high = dg.astype(BF)
    low = (dg - high.astype(F32)).astype(BF)
    back_buf[slot, rows:] = jnp.concatenate([high, low], axis=1)

    for i in range(blocks):

        @pl.when(step == i)
        def _(i=i):
            for copy in results(i):
                copy.start()
            if i == blocks - 1:
                for copy in (*results(i - 1), *results(i)):
                    copy.wait()


def expert_call(place, arrays, plan, weights):
    _, width, ff = weights.shape
    blocks = len(plan)
    rows = sum(piece[2] for piece in plan[0][1])
    most = max(len(h) + len(g) for h, g in plan)
    s = jax.ShapeDtypeStruct
    at = lambda i: (i, 0)
    anywhere = pl.BlockSpec(memory_space=pl.ANY)
    hidden, tile = pl.BlockSpec((rows, ff), at), pl.BlockSpec((rows, width), at)
    out = pl.pallas_call(
        functools.partial(expert_kernel, plan, len(arrays)),
        grid=(blocks,),
        in_specs=[pl.BlockSpec(memory_space=pltpu.SMEM)]
        + [anywhere] * len(arrays)
        + [pl.BlockSpec((1, width, ff), lambda i, k=k: (k, 0, 0), pipeline_mode=pl.Buffered(1)) for k in range(6)],
        out_specs=[hidden] * 6 + [tile] * 2 + [anywhere] * (2 * blocks),
        out_shape=[s((PLANE * rows, ff), BF)] * 6
        + [s((PLANE * rows, width), BF)] * 2
        + [s((rows + EXPERTS, width), BF)] * blocks
        + [s((rows, width), BF)] * blocks,
        scratch_shapes=[
            pltpu.VMEM((2, rows + EXPERTS, width), BF),
            pltpu.VMEM((2, rows, width), BF),
            pltpu.VMEM((2, rows + EXPERTS, width), BF),
            pltpu.VMEM((2, rows, width), BF),
            pltpu.VMEM((rows, 128), F32),
            pltpu.VMEM((rows, 128), F32),
            pltpu.SemaphoreType.DMA((2, most)),
            pltpu.SemaphoreType.DMA((2, 2)),
        ],
        cost_estimate=SMALL,
        compiler_params=pltpu.CompilerParams(vmem_limit_bytes=44 * MIB),
    )(place, *arrays, *[weights] * 6)
    return out[:8], out[8 : 8 + blocks], out[8 + blocks :]


STEPS = 4


def weight_grad_kernel(count, sums, sum_steps, left_ref, *refs):
    rights, refs = refs[:count], refs[count:]
    terms, refs = refs[: 2 * sums], refs[2 * sums :]
    out_ref, totals, acc_ref = refs[0], refs[1:-1], refs[-1]
    k = pl.program_id(0)
    ff = rights[0].shape[1]
    part = dot(left_ref[...], jnp.concatenate([r[...] for r in rights], axis=1), 0, 0)

    @pl.when(k < sum_steps)
    def _():
        for i in range(sums):
            totals[i][...] = (terms[2 * i][...].astype(F32) + terms[2 * i + 1][...].astype(F32)).astype(BF)

    @pl.when(k == 0)
    def _():
        acc_ref[...] = part

    @pl.when(k > 0)
    def _():
        acc_ref[...] += part

    @pl.when(k == STEPS - 1)
    def _():
        for t in range(count):
            out_ref[t] = acc_ref[:, t * ff : (t + 1) * ff].astype(BF)


def weight_grads(left, rights, pairs=()):
    total, width = left.shape
    ff = rights[0].shape[1]
    count = len(rights)
    step = total // STEPS
    row = lambda i: (i, 0)
    rows = pairs[0][0].shape[0] if pairs else 0
    sum_steps = next(n for n in (4, 3, 2, 1) if rows % (16 * n) == 0)
    tile = pl.BlockSpec((rows // sum_steps, width), lambda i: (jnp.minimum(i, sum_steps - 1), 0))
    s = jax.ShapeDtypeStruct
    out = pl.pallas_call(
        functools.partial(weight_grad_kernel, count, len(pairs), sum_steps),
        grid=(STEPS,),
        in_specs=[pl.BlockSpec((step, width), row)]
        + [pl.BlockSpec((step, ff), row)] * count
        + [tile] * (2 * len(pairs)),
        out_specs=[pl.BlockSpec((count, width, ff), lambda i: (0, 0, 0), pipeline_mode=pl.Buffered(1))]
        + [tile] * len(pairs),
        out_shape=[s((count, width, ff), BF)] + [s((rows, width), BF)] * len(pairs),
        scratch_shapes=[pltpu.VMEM((width, count * ff), F32)],
        cost_estimate=SMALL,
        compiler_params=pltpu.CompilerParams(vmem_limit_bytes=VMEM_ROOM),
    )(left, *rights, *[term for pair in pairs for term in pair])
    return out[0], out[1:]


def up(v):
    return v.astype(F32)


def after(value, *others):
    return lax.optimization_barrier((value, *others))[0]


CUT = 1536
COLUMNS = 3200


def make_local(n):
    outer = n // PLANE
    plane_groups = [[PLANE * z + i for i in range(PLANE)] for z in range(outer)]
    outer_groups = [[PLANE * z + i for z in range(outer)] for i in range(PLANE)]
    pieced = outer == 4

    def swap(array, offset):
        return lax.ppermute(array, "dp", [(i, i ^ offset) for i in range(n)])

    along_z = [PLANE * k for k in range(4)]

    def dense_gather(part, *earlier):
        if not pieced:
            return [lax.all_gather(part, "dp", axis=0, tiled=True)], [(None, 0)]
        line = after([part] + [swap(part, k) for k in along_z[1:]], *earlier)
        left, right = jnp.stack([t[:, :CUT] for t in line]), jnp.stack([t[:, CUT:] for t in line])
        left_x, right_y = swap(left, 2), swap(right, 4)
        left_y, right_x = swap(left, 4), swap(right, 2)
        left_xy, right_xy = swap(left_x, 4), swap(right_y, 2)
        found = [(left, 0, 0), (left_x, 2, 0), (left_y, 4, 0), (left_xy, 6, 0)]
        found += [(right, 0, CUT), (right_x, 2, CUT), (right_y, 4, CUT), (right_xy, 6, CUT)]
        found += [(swap(piece, 1), offset + 1, first) for piece, offset, first in found]
        return [f[0] for f in found], [([f[1] + k for k in along_z], f[2]) for f in found]

    def grad_spots(share):
        if not pieced:
            return [(n * share, COLUMNS)], [(None, 0)]
        shapes, spots = [], []
        for core in (1, 0):
            for major, minor, first, cols in ((2, 4, 0, CUT), (4, 2, CUT, COLUMNS - CUT)):
                for far in (0, major):
                    shapes.append((8, share, cols))
                    spots.append(([core + far + d + k for d in (0, minor) for k in along_z], first))
        return shapes, spots

    def dense_sum(pieces, earlier, packed):
        if not pieced:
            return lax.psum_scatter(up(pieces[0]), "dp", scatter_dimension=0, tiled=True), packed

        def add(a, b):
            return (up(a) + up(b)).astype(BF)

        near_l, far_l, near_r, far_r = (add(keep, swap(sent, 1)) for sent, keep in zip(pieces[:4], pieces[4:]))
        far_l, far_r = after((far_l, far_r), earlier)
        got_l, got_r = swap(far_l, 2), swap(far_r, 4)
        sent_l, sent_r = add(near_l[4:], got_l[4:]), add(near_r[4:], got_r[4:])
        left = add(add(near_l[:4], got_l[:4]), swap(sent_l, 4))
        right = add(add(near_r[:4], got_r[:4]), swap(sent_r, 2))
        both = jnp.concatenate([left, right], axis=2)
        both, packed = lax.optimization_barrier((both, packed))
        total = up(both[0])
        for k in range(1, 4):
            total = total + up(swap(both[k], PLANE * k))
        return total, packed

    def both_cores(same_core):
        return [b for part in same_core for b in (part, swap(part, 1))]

    def local(
        tokens,
        query_weight,
        key_projection_weight,
        value_projection_weight,
        output_weight,
        first_gain,
        second_gain,
        router_weight,
        gate_weight,
        up_weight,
        down_weight,
        routes,
        segments,
        cotangent,
    ):
        rows, width = tokens.shape
        ff = gate_weight.shape[2]
        share = query_weight.shape[0]
        me = lax.axis_index("dp").astype(jnp.int32).reshape(1)
        place = lax.rem(me, PLANE)

        expert_part = jnp.stack(
            [w.reshape(PLANE, MINE, share, ff) for w in (gate_weight, up_weight, down_weight.transpose(0, 2, 1))],
            axis=2,
        )
        dense_part = jnp.concatenate(
            [
                query_weight,
                key_projection_weight,
                value_projection_weight,
                output_weight.T,
                router_weight,
                first_gain[:, None],
                second_gain[:, None],
                jnp.zeros((share, 128 - EXPERTS - 2), BF),
            ],
            axis=1,
        )
        dense_part = after(dense_part, expert_part)
        expert_part = lax.all_to_all(
            expert_part, "dp", split_axis=0, concat_axis=0, axis_index_groups=plane_groups
        )

        expert_part = expert_part.transpose(1, 2, 0, 3, 4).reshape(3 * MINE, PLANE * share, ff)
        weights = lax.all_gather(expert_part, "dp", axis=1, tiled=True, axis_index_groups=outer_groups)

        positions = jnp.arange(rows, dtype=F32)
        frequency = 10000.0 ** (-2.0 * jnp.arange(HEAD_SIZE // 2, dtype=F32) / HEAD_SIZE)
        angles = positions[:, None] * frequency[None, :]
        cosine, sine = jnp.cos(angles), jnp.sin(angles)
        cosine = jnp.concatenate([cosine] * 4, axis=1)
        sine = jnp.concatenate([-sine, sine, -sine, sine], axis=1)
        seg_col = segments.reshape(rows, 1)
        seg_row = segments.reshape(1, rows)

        half = rows // 2
        pieces, spots = dense_gather(dense_part, cosine, sine, seg_col, expert_part)
        late = after(cotangent, *pieces)
        cot_x, cot_y = swap(late, 2), swap(late, 4)

        lse, h2, dense, h1, q, k, v, o, r1 = forward_call(
            me, tokens, routes.T, seg_col, seg_row, cosine, sine, pieces, spots
        )
        h2 = after(h2, cot_x, cot_y)
        h2_x, h2_y, h2_core = swap(h2, 2), swap(h2, 4), swap(h2, 1)
        cot_core = swap(cotangent, 1)
        h2_x, h2_y, cot_x, cot_y = after((h2_x, h2_y, cot_x, cot_y), h2_core, cot_core)
        corner_x = swap(jnp.concatenate([h2_y[:half], cot_y[:half]], axis=0), 2)
        corner_y = swap(jnp.concatenate([h2_x[half:], cot_x[half:]], axis=0), 4)
        cores = [swap(t, 1) for t in (h2_x, cot_x, h2_y, cot_y)]
        corner_x, corner_y = after((corner_x, corner_y), *cores)
        long = rows + EXPERTS

        def pieces_of(h, g):
            return ([(h, 0, long, 0)], [(g, 0, rows, 0)])

        first_arrays = [corner_x, swap(corner_x, 1), corner_y, swap(corner_y, 1), h2_x, cores[0], cot_x, cores[1]]
        first_plan = [
            (
                [(i, 0, half, 0), (i + 2, 0, long - half, half)],
                [(i, half, half, 0), (i + 2, long - half, half, half)],
            )
            for i in range(2)
        ]
        first_plan += [pieces_of(i, 2 + i) for i in (4, 5)]
        second_arrays = [h2, h2_core, h2_y, cores[2], cotangent, cot_core, cot_y, cores[3]]
        second_plan = [pieces_of(8 + i, 12 + i) for i in range(4)]

        def outer_sum(grads):
            if not pieced:
                grads = up(grads)
            return lax.psum_scatter(grads, "dp", scatter_dimension=1, tiled=True, axis_index_groups=outer_groups)

        def with_core(block, other):
            return (up(block) + up(other)).astype(BF)

        def together(*values):
            return lax.optimization_barrier(values)

        top, low = slice(0, half), slice(half, None)

        kept, back, out = expert_call(place, first_arrays + second_arrays, first_plan + second_plan, weights)
        core_xy, core_x, core_y = swap(back[1], 1), swap(back[3], 1), swap(back[7], 1)
        sum_xy = [with_core(back[0][part], core_xy[part]) for part in (top, low)]
        sum_xy, core_x, core_y, kept, back, out = together(sum_xy, core_x, core_y, kept, back, out)

        ug0, ug1, da0, da1, db0, db1, tokens_all, grads_all = kept
        grads_d, (sum_x, sum_y) = weight_grads(grads_all, [ug0, ug1], [(back[2], core_x), (back[6], core_y)])
        via_x, via_y, out_core = swap(sum_xy[0], 2), swap(sum_xy[1], 4), [swap(out[i], 1) for i in (1, 3, 7)]
        grads_d, sum_x, sum_y, via_x, via_y, out_core, kept, out, back = together(
            grads_d, sum_x, sum_y, via_x, via_y, out_core, kept, out, back
        )
        sums_d = outer_sum(grads_d)
        sum_y = with_core(sum_y, jnp.pad(via_x, ((0, sum_y.shape[0] - half), (0, 0))))
        sum_x = with_core(sum_x, jnp.pad(via_y, ((half, 0), (0, 0))))
        sum_x, sum_y, kept, back, out, out_core = together(sum_x, sum_y, kept, back, out, out_core)

        _, _, da0, da1, db0, db1, tokens_all, _ = kept
        grads_gu, (out_xy, out_x, out_y) = weight_grads(
            tokens_all,
            [da0, da1, db0, db1],
            [(out[0], out_core[0]), (out[2], out_core[1]), (out[6], out_core[2])],
        )
        got_x, got_y, core_own, out_core_own = swap(sum_x, 2), swap(sum_y, 4), swap(back[5], 1), swap(out[5], 1)
        grads_gu, got_x, got_y, core_own, out_core_own, out_xy, out_x, out_y, _ = together(
            grads_gu, got_x, got_y, core_own, out_core_own, out_xy, out_x, out_y, (first_arrays, second_arrays)
        )
        sums_gu = outer_sum(grads_gu)
        got = [back[4], core_own, got_x, got_y]
        got, out_x, out_y, out_xy = together(got, out_x, out_y, [out_xy[top], out_xy[low]])

        shapes, grad_places = grad_spots(share)
        input_grad, *grad_pieces = backward_call(
            me, got, tokens, r1, cotangent, h1, h2, dense, q, k, v, o, lse, seg_col, seg_row, cosine, sine,
            shapes, grad_places,
        )
        got_out = [swap(out_x, 2), swap(out_y, 4), swap(out_xy[0], 6)]
        input_grad, grad_pieces, got_out, out_xy = together(input_grad, grad_pieces, got_out, out_xy)
        got_out_low = swap(out_xy[1], 6)
        output = r1 + up(out[4]) + up(out_core_own) + up(got_out[0]) + up(got_out[1])
        output_top, output_low = (output[top] + up(got_out[2])).astype(BF), output[low]
        owned = jnp.concatenate(
            [s.reshape(-1, PLANE, share, ff).transpose(1, 0, 2, 3) for s in (sums_d, sums_gu)], axis=1
        )
        dense_grads, owned = dense_sum(grad_pieces, (got_out_low, output_top, output_low), owned)
        output = jnp.concatenate([output_top, (output_low + up(got_out_low)).astype(BF)], axis=0)
        owned = lax.all_to_all(owned, "dp", split_axis=0, concat_axis=0, axis_index_groups=plane_groups)

        def experts_of(kind):
            return up(owned[:, MINE * kind : MINE * (kind + 1)]).reshape(EXPERTS, share, ff)

        down_out, gate_out, up_out = experts_of(0).transpose(0, 2, 1), experts_of(1), experts_of(2)
        return (
            output,
            input_grad,
            dense_grads[:, :1024],
            dense_grads[:, 1024:1536],
            dense_grads[:, 1536:2048],
            dense_grads[:, 2048:3072].T,
            dense_grads[:, 3072 + EXPERTS],
            dense_grads[:, 3073 + EXPERTS],
            dense_grads[:, 3072 : 3072 + EXPERTS],
            gate_out,
            up_out,
            down_out,
        )

    return local


def solution(mesh):
    row, col, one = P("dp", None), P(None, "dp"), P("dp")
    middle, last = P(None, "dp", None), P(None, None, "dp")
    in_specs = (row, row, row, row, col, one, one, row, middle, middle, last, row, row, row)
    out_specs = (row, row, row, row, row, col, one, one, row, middle, middle, last)
    return jax.shard_map(
        make_local(mesh.shape["dp"]), mesh=mesh, in_specs=in_specs, out_specs=out_specs, check_vma=False
    )
```
